32 devices in a mesh: wide: 16 (over z, x, core), narrow: 2 (over y).
Axes of the slice: x: 2, y: 2, z: 4, core: 2. Of those that a mesh axis runs over, the one named last changes fastest.
Arguments:
- tokens: bfloat16 [32, 1024, 768], P(('wide', 'narrow')), may hold values from -6 to 6
- lengths: int32 [32, 4], P(('wide', 'narrow')), may hold values from 1 to 512, 1024 in all within a row
- cotangent: bfloat16 [32, 1024, 768], P(('wide', 'narrow')), may hold values from -6 to 6
- vectors: bfloat16 [11, 768], P(None, ('wide', 'narrow')), may hold values from -6 to 3, as said below
- time_recept: bfloat16 [589824], P(('wide', 'narrow')), may hold values from -0.21875 to 0.21875
- time_key: bfloat16 [589824], P(('wide', 'narrow')), may hold values from -0.21875 to 0.21875
- time_value: bfloat16 [589824], P(('wide', 'narrow')), may hold values from -0.21875 to 0.21875
- time_output: bfloat16 [589824], P(('wide', 'narrow')), may hold values from -1.25 to 1.25
- channel_key: bfloat16 [2359296], P(('wide', 'narrow')), may hold values from -0.21875 to 0.21875
- channel_value: bfloat16 [2359296], P(('wide', 'narrow')), may hold values from -0.109375 to 0.109375
- channel_recept: bfloat16 [589824], P(('wide', 'narrow')), may hold values from -0.21875 to 0.21875
Outputs:
- result: bfloat16 [32, 1024, 768], P(('wide', 'narrow'))
- input_grad: bfloat16 [32, 1024, 768], P(('wide', 'narrow'))
- vectors_grad: float32 [11, 768], P(None, ('wide', 'narrow'))
- time_recept_grad: float32 [589824], P(('wide', 'narrow'))
- time_key_grad: float32 [589824], P(('wide', 'narrow'))
- time_value_grad: float32 [589824], P(('wide', 'narrow'))
- time_output_grad: float32 [589824], P(('wide', 'narrow'))
- channel_key_grad: float32 [2359296], P(('wide', 'narrow'))
- channel_value_grad: float32 [2359296], P(('wide', 'narrow'))
- channel_recept_grad: float32 [589824], P(('wide', 'narrow'))
The draws below stay inside these ranges and needn't reach their ends.
Inputs may be any that keep to these rules, and one draw needn't show every extreme that they name: Each row's 4 document lengths sum to 1024; each row's longest document has 512 tokens. `vectors`: the gains lie in [0.5, 1.5], the biases in [-0.5, 0.5], the five mix rows in [0, 1], decay in [-6, 3] and bonus in [-1.5, 1.5].
All inputs are finite; a program needn't handle non-finite values.
Results may differ from the reference program's by a relative error of at most 0.0085.
Values may be sent and summed in bfloat16 or wider, within the bound.
A program may use at most 256 MiB of HBM per device.

```python
import math
from functools import partial
import jax
import jax.numpy as jnp
import numpy as np
from jax import lax

D = 768
FF = 3072
LENGTH = 1024
BLOCK = 32
DOCS = 4
PARAM_ROWS = 11
MOSTLEN = 512
ROWS = 32


def draw_vectors(key, part):
    key = jax.random.fold_in(key, 11)
    samples = jax.random.uniform(key, (PARAM_ROWS, D), jnp.float32)
    lower_ends = [0.7, -0.3, 0.0, 0.0, 0.0, -6.0, -1.0, 0.7, -0.3, 0.0, 0.0]
    extents = [0.6, 0.6, 1.0, 1.0, 1.0, 8.5, 2.0, 0.6, 0.6, 1.0, 1.0]
    offsets = jnp.array(lower_ends, jnp.float32)[:, None]
    extent_col = jnp.array(extents, jnp.float32)[:, None]
    return (offsets + extent_col * samples).astype(jnp.bfloat16)


def block_scale(stream_key, extent, cuts, least, largest):
    loudness, own = 1.0, jax.random.fold_in(stream_key, 6)
    for position, parts in cuts:
        draws = jnp.exp(jax.random.uniform(jax.random.fold_in(own, position), (parts,), jnp.float32, least / len(cuts), largest / len(cuts)))
        loudness = loudness * jnp.repeat(draws, extent[position] // parts).reshape([-1 if axis == position else 1 for axis in range(len(extent))])
    return loudness


def split_up(count, total, bound, lean):
    loads = [(1 << 20) // math.isqrt(rank ** lean) + 1 for rank in range(2, count + 1)]
    spare, holding = total - bound - (count - 1), [1] * (count - 1)
    while spare > 0:
        movable = [i for i in range(count - 1) if holding[i] < bound]
        mass, budget = sum([loads[i] for i in movable]), spare
        for i in movable:
            extra = min(bound - holding[i], max(1, budget * loads[i] // mass), spare)
            holding[i] = holding[i] + extra
            spare = spare - extra
    return np.array([bound] + holding)


def uneven(own_key, number_of, total, bound, slope):
    if number_of == 2:
        one = jax.random.randint(own_key, (), max(1, total - bound), min(bound, total - 1) + 1)
        return jnp.stack([one, total - one])
    tallies = jnp.asarray(split_up(number_of, total, bound, slope), jnp.int32)
    couples = (number_of - 1) // 2
    source_of, taker = tallies[1:1 + 2 * couples:2], tallies[2:2 + 2 * couples:2]
    margin = jnp.minimum(source_of - 1, bound - taker)
    moved = jax.random.randint(jax.random.fold_in(own_key, 1), (couples,), 0, 1 << 20) % (margin + 1)
    tallies = tallies.at[1:1 + 2 * couples:2].set(source_of - moved).at[2:2 + 2 * couples:2].set(taker + moved)
    return tallies[jax.random.permutation(jax.random.fold_in(own_key, 2), number_of)]


def gaussian(own_key, extent, scale, limit, shards=(), kind=jnp.bfloat16):
    factor_of = block_scale(own_key, extent, shards, -0.22, 0.18) if shards else 1.0
    result = jax.random.normal(own_key, extent, jnp.float32) * scale * factor_of
    return jnp.minimum(jnp.maximum(result, -limit), limit).astype(kind)


def setup_inputs(seed: int = 0) -> dict:
    arg_keys = jax.random.split(jax.random.key(seed), 12)
    return {
        "tokens": gaussian(arg_keys[0], (ROWS, LENGTH, D), 1.0, 6.0, ((0, 32),)),
        "lengths": jax.vmap(lambda own: uneven(own, DOCS, LENGTH, MOSTLEN, 2))(jax.random.split(arg_keys[1], ROWS)).reshape((ROWS, DOCS)).astype(jnp.int32),
        "cotangent": gaussian(arg_keys[2], (ROWS, LENGTH, D), 1.0, 6.0, ((0, 32),)),
        "vectors": draw_vectors(jax.random.fold_in(arg_keys[11], 71), 0),
        "time_recept": gaussian(arg_keys[4], (D * D,), D ** -0.5, 0.21875, ((0, 32),)),
        "time_key": gaussian(arg_keys[5], (D * D,), D ** -0.5, 0.21875, ((0, 32),)),
        "time_value": gaussian(arg_keys[6], (D * D,), D ** -0.5, 0.21875, ((0, 32),)),
        "time_output": gaussian(arg_keys[7], (D * D,), (D // 32) ** -0.5, 1.25, ((0, 32),)),
        "channel_key": gaussian(arg_keys[8], (D * FF,), D ** -0.5, 0.21875, ((0, 32),)),
        "channel_value": gaussian(arg_keys[9], (FF * D,), FF ** -0.5, 0.109375, ((0, 32),)),
        "channel_recept": gaussian(arg_keys[10], (D * D,), D ** -0.5, 0.21875, ((0, 32),)),
    }


@jax.custom_vjp
def low(v):
    return lax.optimization_barrier(v.astype(jnp.bfloat16)).astype(jnp.float32)

@jax.custom_vjp
def low_back(v):
    return v

def low_keep(v):
    return (low(v), None)

def low_pass(kept, grad):
    return (grad,)

def back_keep(v):
    return (v, None)

def back_low(kept, grad):
    return (low(grad),)
low.defvjp(low_keep, low_pass)
low_back.defvjp(back_keep, back_low)
epsilon = 1e-05

def layer_norm(signal, gain_vec, offset):
    centred = signal - lax.optimization_barrier(jnp.mean(signal, axis=-1, keepdims=True))
    spread = lax.optimization_barrier(jnp.mean(centred * centred, axis=-1, keepdims=True))
    return centred * lax.rsqrt(spread + epsilon) * gain_vec + offset

def continue_mask(lengths):
    offsets = jnp.cumsum(lengths, axis=-1) - lengths
    positions = jnp.arange(LENGTH, dtype=jnp.int32)
    matches = (positions[None, :, None] == offsets[:, None, :]).astype(jnp.float32)
    return 1.0 - lax.optimization_barrier(jnp.sum(matches, axis=-1))

def shifted(signal, text_persists):
    earlier = jnp.concatenate([jnp.zeros_like(signal[:, :1]), signal[:, :-1]], axis=1)
    return earlier * text_persists[..., None]

def mixing(normed, before, mix_ratio):
    return mix_ratio * normed + (1.0 - mix_ratio) * before

def product(signal, matrix):
    return jnp.dot(signal, matrix, precision=lax.Precision.HIGHEST)

def scaled_address_content(address_matrix, content_matrix, text_persists, fading_speed, initial_extra_share):
    group_size = address_matrix.shape[0]
    model_width = address_matrix.shape[2]
    block_size = min(BLOCK, LENGTH)
    block_count = LENGTH // block_size

    def arrange(tensor_in):
        turned = jnp.swapaxes(tensor_in, 0, 1)
        return turned.reshape((block_count, block_size) + turned.shape[1:])
    factor = jnp.exp(fading_speed)

    def per_token(carry_state, pieces):
        top_prior_carry, bottom_prior_carry = carry_state
        present_address, present_content, continue_now = pieces
        top_prior_carry = top_prior_carry * continue_now[:, None]
        bottom_prior_carry = bottom_prior_carry * continue_now[:, None]
        present_extra_factor = jnp.exp(initial_extra_share + present_address)
        residual_result = (top_prior_carry + present_extra_factor * present_content) / (bottom_prior_carry + present_extra_factor)
        weight = jnp.exp(present_address)
        return ((factor * top_prior_carry + weight * present_content, factor * bottom_prior_carry + weight), residual_result)

    def run_block(carry_state, pieces):
        return lax.scan(per_token, carry_state, pieces)
    zero_state = jnp.zeros((group_size, model_width), jnp.float32)
    _, outputs = lax.scan(jax.checkpoint(run_block), (zero_state, zero_state), (arrange(address_matrix), arrange(content_matrix), arrange(text_persists)))
    return jnp.swapaxes(outputs.reshape(LENGTH, group_size, model_width), 0, 1)

def forward(token_float, weights, text_persists):
    params, recept_mat, key_mat, value_mat, output_mat, expand_mat, shrink_mat, gate_mat = weights
    normed = layer_norm(token_float, params[0], params[1])
    before = shifted(normed, text_persists)
    mixed_recept = low(mixing(normed, before, params[2]))
    mixed_key = low(mixing(normed, before, params[3]))
    mixed_value = low(mixing(normed, before, params[4]))
    receptance_before_mixing = low_back(product(mixed_recept, recept_mat))
    address_unmixed = low_back(product(mixed_key, key_mat))
    content_unmixed = low_back(product(mixed_value, value_mat))
    blended_state = scaled_address_content(address_unmixed, content_unmixed, text_persists, -jnp.exp(params[5]), params[6])
    attended = low(jax.nn.sigmoid(receptance_before_mixing) * blended_state)
    middle = token_float + low_back(product(attended, output_mat))
    normed_two = layer_norm(middle, params[7], params[8])
    before_two = shifted(normed_two, text_persists)
    channel_in = low(mixing(normed_two, before_two, params[9]))
    gate_in = low(mixing(normed_two, before_two, params[10]))
    expanded = low_back(product(channel_in, expand_mat))
    squared = low(jnp.square(jnp.maximum(expanded, 0.0)))
    shrunk = low_back(product(squared, shrink_mat))
    gate_pre = low_back(product(gate_in, gate_mat))
    return middle + jax.nn.sigmoid(gate_pre) * shrunk

def reference(tokens, lengths, cotangent, vectors, time_recept, time_key, time_value, time_output, channel_key, channel_value, channel_recept):
    row_total = tokens.shape[0]
    group_size = math.gcd(row_total, 4)
    weights = (vectors.astype(jnp.float32), time_recept.astype(jnp.float32).reshape(D, D), time_key.astype(jnp.float32).reshape(D, D), time_value.astype(jnp.float32).reshape(D, D), time_output.astype(jnp.float32).reshape(D, D), channel_key.astype(jnp.float32).reshape(D, FF), channel_value.astype(jnp.float32).reshape(FF, D), channel_recept.astype(jnp.float32).reshape(D, D))
    text_persists = continue_mask(lengths)

    def grouped(tensor_in):
        return tensor_in.reshape((row_total // group_size, group_size) + tensor_in.shape[1:])

    def per_group(totals, pieces):
        token_part, cotangent_part, continue_part = pieces
        outputs, pullback = jax.vjp(partial(forward, text_persists=continue_part), token_part.astype(jnp.float32), weights)
        gradients = pullback(cotangent_part.astype(jnp.float32))
        totals = jax.tree.map(jnp.add, totals, gradients[1])
        return (totals, (outputs.astype(jnp.bfloat16), gradients[0].astype(jnp.bfloat16)))
    initial = jax.tree.map(jnp.zeros_like, weights)
    totals, (results, input_grads) = lax.scan(per_group, initial, (grouped(tokens), grouped(cotangent), grouped(text_persists)))
    return (results.reshape(tokens.shape), input_grads.reshape(tokens.shape), totals[0], totals[1].reshape(-1), totals[2].reshape(-1), totals[3].reshape(-1), totals[4].reshape(-1), totals[5].reshape(-1), totals[6].reshape(-1), totals[7].reshape(-1))
```

```python
from functools import partial

import jax
import jax.numpy as jnp
from jax import lax
from jax.experimental import pallas as pl
from jax.experimental.pallas import tpu as pltpu
from jax.sharding import PartitionSpec as P


SEG = 16
LANES = 128
EPS = 1e-05
F32 = jnp.float32
BF16 = jnp.bfloat16
VMEM_LIMIT = 62 * 1024 * 1024


def wide_of(column, width):
    return jnp.concatenate([column] * (width // LANES), axis=1)


def dot_nn(left, right):
    return jnp.dot(left, right, preferred_element_type=F32)


def dot_nt(left, right):
    return lax.dot_general(left, right, (((1,), (1,)), ((), ())), preferred_element_type=F32)


def dot_tn(left, right):
    return lax.dot_general(left, right, (((0,), (0,)), ((), ())), preferred_element_type=F32)


def local(source, target, sem):
    return pltpu.make_async_copy(source, target, sem)


def rows_at(index, size):
    return pl.ds(pl.multiple_of(index * size, size), size)


def fill_mask(lengths, mask, length):
    steps = length // SEG

    @pl.loop(0, length // 128)
    def _(block):
        row = block * 128 + lax.broadcasted_iota(jnp.int32, (128, LANES), 0)
        place = (row % SEG) * steps + row // SEG
        start = jnp.int32(0)
        fresh = place == 0
        for doc in range(lengths.shape[1] - 1):
            start = start + lengths[0, doc]
            fresh = jnp.logical_or(fresh, place == start)
        mask[rows_at(block, 128), :] = jnp.where(fresh, 0.0, 1.0)


def widen(source, target):
    @pl.loop(0, source.shape[0] // 32)
    def _(block):
        rows = rows_at(block, 32)
        for c in range(target.shape[0]):
            target[c, rows, :] = source[rows, c * LANES : (c + 1) * LANES].astype(F32)


def narrow(source, target):
    @pl.loop(0, target.shape[0] // 32)
    def _(block):
        rows = rows_at(block, 32)
        for c in range(source.shape[0]):
            target[rows, c * LANES : (c + 1) * LANES] = source[c, rows, :].astype(BF16)


def take_step(source, step, steps):
    strip = pl.ds(step, SEG, stride=steps)
    return jnp.concatenate([source[c, strip, :] for c in range(source.shape[0])], axis=1)


def put_step(target, step, steps, rows):
    strip = pl.ds(step, SEG, stride=steps)
    for c in range(target.shape[0]):
        target[c, strip, :] = rows[:, c * LANES : (c + 1) * LANES]


def norm_rows(rows):
    centred = rows - jnp.mean(rows, axis=-1, keepdims=True)
    scale = lax.rsqrt(jnp.mean(centred * centred, axis=-1, keepdims=True) + EPS)
    return centred * scale, scale


def join_runs(local_end, through, backward):
    index = lax.broadcasted_iota(jnp.int32, local_end[0].shape, 0)
    if backward:
        index = SEG - 1 - index
    states = list(local_end)
    hop = 1
    while hop < SEG:
        turn = SEG - hop if backward else hop
        inside = index >= hop
        moved = pltpu.roll(through, turn, 0)
        states = [jnp.where(inside, s + through * pltpu.roll(s, turn, 0), s) for s in states]
        through = jnp.where(inside, through * moved, through)
        hop *= 2
    turn = SEG - 1 if backward else 1
    return [jnp.where(index >= 1, pltpu.roll(s, turn, 0), 0.0) for s in states]


def forward_kernel(
    lengths, tokens, cotangent, vec, w4_in, wk_in, wv_in, wg_in,
    result, n1_out, n2_out, r_out, mix_out, state_out, att_out, cig_out, sq_out, gsg_out, up_out,
    w4, wk, wv, wg, nat, norm, mid, state, half, sq, mask, rsd, sems,
):
    length, width = tokens.shape
    steps = length // SEG

    load_tok = local(tokens, half.at[0], sems.at[0])
    load_cot = local(cotangent, half.at[1], sems.at[1])
    load_w4 = local(w4_in, w4, sems.at[2])
    load_wk = local(wk_in, wk, sems.at[3])
    load_wv = local(wv_in, wv, sems.at[4])
    load_wg = local(wg_in, wg, sems.at[5])
    for copy in (load_tok, load_cot, load_w4, load_wk, load_wv, load_wg):
        copy.start()
    fill_mask(lengths, mask, length)
    load_tok.wait()
    widen(half.at[0], nat)

    @pl.loop(0, steps, unroll=2)
    def _(step):
        rows = take_step(nat, step, steps)
        mid[rows_at(step, SEG), :] = rows
        normed, scale = norm_rows(rows)
        norm[rows_at(step + 1, SEG), :] = normed
        rsd[0, rows_at(step, SEG), :] = jnp.broadcast_to(scale, (SEG, LANES))

    norm[0:SEG, :] = pltpu.roll(norm[length : length + SEG, :], 1, 0)
    save_n1 = local(norm, n1_out, sems.at[6])
    save_n1.start()

    @pl.loop(0, steps, unroll=2)
    def _(step):
        gain, bias = vec[0:1, :], vec[1:2, :]
        rows = rows_at(step, SEG)
        now = norm[rows_at(step + 1, SEG), :] * gain + bias
        before = (norm[rows, :] * gain + bias) * wide_of(mask[rows, :], width)
        change = now - before
        for q in range(3):
            half[2 + q, rows, :] = (before + vec[2 + q : 3 + q, :] * change).astype(BF16)

    save_mix = local(half.at[2:5], mix_out, sems.at[7])
    save_mix.start()

    load_w4.wait()
    for q in range(3):

        @pl.loop(0, 2)
        def _(part):
            rows = rows_at(part, length // 2)
            pre = dot_nn(half[2 + q, rows, :], w4[:, q].reshape(width, width))
            if q == 0:
                pre = jax.nn.sigmoid(pre)
            if q == 1:
                pre = jnp.exp(pre)
            state[q, rows, :] = pre

    rate = -jnp.exp(vec[5:6, :])
    fade = jnp.exp(rate)

    def first(step, carry):
        top, bottom, through = carry
        rows = rows_at(step, SEG)
        keep = mask[rows, :]
        factor = fade * wide_of(keep, width)
        key = state[1, rows, :]
        return factor * top + key * state[2, rows, :], factor * bottom + key, through * keep

    zero = jnp.zeros((SEG, width), F32)
    top, bottom, through = lax.fori_loop(0, steps, first, (zero, zero, jnp.ones((SEG, LANES), F32)), unroll=2)
    through = wide_of(through, width) * jnp.exp(rate * steps)
    top, bottom = join_runs((top, bottom), through, False)

    def second(step, carry):
        top, bottom = carry
        rows = rows_at(step, SEG)
        keep = wide_of(mask[rows, :], width)
        top, bottom = top * keep, bottom * keep
        key = state[1, rows, :]
        key_value = key * state[2, rows, :]
        bonus = jnp.exp(vec[6:7, :])
        blended = (top + bonus * key_value) / (bottom + bonus * key)
        half[5, rows, :] = (state[0, rows, :] * blended).astype(BF16)
        state[3, rows, :] = top
        state[4, rows, :] = bottom
        return fade * top + key_value, fade * bottom + key

    lax.fori_loop(0, steps, second, (top, bottom), unroll=2)
    save_state = local(state, state_out, sems.at[8])
    save_state.start()
    save_att = local(half.at[5], att_out, sems.at[9])
    save_att.start()

    @pl.loop(0, 2)
    def _(part):
        rows = rows_at(part, length // 2)
        mid[rows, :] += dot_nn(half[5, rows, :], w4[:, 3].reshape(width, width))

    save_n1.wait()

    @pl.loop(0, steps, unroll=2)
    def _(step):
        rows = rows_at(step, SEG)
        normed, scale = norm_rows(mid[rows, :])
        norm[rows_at(step + 1, SEG), :] = normed
        rsd[1, rows, :] = jnp.broadcast_to(scale, (SEG, LANES))

    norm[0:SEG, :] = pltpu.roll(norm[length : length + SEG, :], 1, 0)
    save_n2 = local(norm, n2_out, sems.at[10])
    save_n2.start()
    save_r = local(rsd, r_out, sems.at[11])
    save_r.start()
    save_mix.wait()

    @pl.loop(0, steps, unroll=2)
    def _(step):
        gain, bias = vec[7:8, :], vec[8:9, :]
        rows = rows_at(step, SEG)
        now = norm[rows_at(step + 1, SEG), :] * gain + bias
        before = (norm[rows, :] * gain + bias) * wide_of(mask[rows, :], width)
        change = now - before
        for q in range(2):
            half[2 + q, rows, :] = (before + vec[9 + q : 10 + q, :] * change).astype(BF16)

    save_cig = local(half.at[2:4], cig_out, sems.at[12])
    save_cig.start()

    load_cot.wait()
    widen(half.at[1], nat)

    @pl.loop(0, steps, unroll=2)
    def _(step):
        half[0, rows_at(step, SEG), :] = take_step(nat, step, steps).astype(BF16)

    save_up = local(half.at[0], up_out, sems.at[13])
    save_up.start()

    load_wk.wait()
    for q in range(4):

        @pl.loop(0, 2)
        def _(part):
            rows = rows_at(part, length // 2)
            pre = jnp.maximum(dot_nn(half[2, rows, :], wk[:, q].reshape(width, width)), 0.0)
            sq[rows, q * width : (q + 1) * width] = (pre * pre).astype(BF16)

    save_sq = local(sq, sq_out, sems.at[14])
    save_sq.start()

    save_state.wait()
    load_wg.wait()
    load_wv.wait()

    @pl.loop(0, 2)
    def _(part):
        rows = rows_at(part, length // 2)
        state[0, rows, :] = jax.nn.sigmoid(dot_nn(half[3, rows, :], wg[...].reshape(width, width)))
        state[1, rows, :] = dot_nn(sq[rows, :], wv[...].reshape(4 * width, width))

    save_att.wait()

    @pl.loop(0, steps, unroll=2)
    def _(step):
        rows = rows_at(step, SEG)
        gate, shrunk = state[0, rows, :], state[1, rows, :]
        upstream = half[0, rows, :].astype(F32)
        gated = gate * shrunk
        put_step(nat, step, steps, mid[rows, :] + gated)
        half[4, rows, :] = (upstream * gate).astype(BF16)
        half[5, rows, :] = (upstream * gated * (1.0 - gate)).astype(BF16)

    save_gsg = local(half.at[4:6], gsg_out, sems.at[15])
    save_gsg.start()
    narrow(nat, half.at[1])
    save_res = local(half.at[1], result, sems.at[16])
    save_res.start()
    for copy in (save_n2, save_r, save_cig, save_up, save_sq, save_gsg, save_res):
        copy.wait()


def backward_kernel(
    lengths, vec, w4_in, wk_in, wv_in, wg_in, n1_in, n2_in, r_in, mix_in, state_in, att_in, cig_in, sq_in, gsg_in, up_in,
    input_grad, vec_grad, g4_out, gk_out, gv_out, gg_out,
    wk, wv, wg, big, sq, half, mask, rsd, nat, grad, grad_gate, sums, sems,
):
    length, width = input_grad.shape
    steps = length // SEG
    n_buf, gm_buf, nb_buf, s_buf = 0, 1, 2, 3

    load_gsg = local(gsg_in, half.at[0:2], sems.at[0])
    load_sq = local(sq_in, sq, sems.at[1])
    load_wv = local(wv_in, wv, sems.at[2])
    load_cig = local(cig_in, half.at[2:4], sems.at[3])
    load_wk = local(wk_in, wk, sems.at[4])
    load_wg = local(wg_in, wg, sems.at[5])
    load_n2 = local(n2_in, big.at[n_buf], sems.at[6])
    load_r = local(r_in, rsd, sems.at[7])
    for copy in (load_gsg, load_sq, load_wv, load_cig, load_wk, load_wg, load_n2, load_r):
        copy.start()
    fill_mask(lengths, mask, length)

    load_gsg.wait()
    load_sq.wait()

    @pl.loop(0, 4)
    def _(part):
        out = dot_tn(sq[:, rows_at(part, width)], half[0]).astype(BF16)
        grad[pl.ds(part * 4, 4)] = out.reshape(4, 4, 48, width)

    save_gv = local(grad, gv_out, sems.at[8])
    save_gv.start()

    load_wv.wait()

    @pl.loop(0, 4)
    def _(part):
        cols = rows_at(part, width)
        back = dot_nt(half[0], wv[pl.ds(part * 4, 4)].reshape(width, width))
        expanded = jnp.sqrt(sq[:, cols].astype(F32))
        sq[:, cols] = (2.0 * expanded * back).astype(BF16)

    load_mix = local(mix_in, wv.reshape(3, length, width), sems.at[9])
    load_mix.start()

    load_cig.wait()
    grad_gate[...] = dot_tn(half[3], half[1]).astype(BF16).reshape(16, 48, width)
    save_gg = local(grad_gate, gg_out, sems.at[10])
    save_gg.start()

    load_wg.wait()
    load_wk.wait()
    big[s_buf, 0:length, :] = dot_nt(half[1], wg[...].reshape(width, width))
    load_up = local(up_in, half.at[1], sems.at[11])
    load_up.start()

    @pl.loop(0, 2)
    def _(part):
        rows = rows_at(part, length // 2)
        out = dot_nt(sq[rows, 0:width], wk[:, 0].reshape(width, width))
        for q in range(1, 4):
            out += dot_nt(sq[rows, q * width : (q + 1) * width], wk[:, q].reshape(width, width))
        big[gm_buf, rows, :] = out

    load_w4 = local(w4_in, wk, sems.at[12])
    load_w4.start()

    save_gv.wait()
    for q in range(4):
        grad[:, q] = dot_tn(half[2], sq[:, q * width : (q + 1) * width]).astype(BF16).reshape(16, 48, width)
    save_gk = local(grad, gk_out, sems.at[13])
    save_gk.start()
    load_att = local(att_in, sq.at[:, 0:width], sems.at[14])
    load_att.start()

    load_n2.wait()
    load_r.wait()

    zero8 = jnp.zeros((8, width), F32)
    zero = jnp.zeros((SEG, width), F32)

    def fold(rows):
        return rows[0:8] + rows[8:16]

    def mix_two(step, carry):
        sum_channel, sum_gate = carry
        rows = rows_at(step, SEG)
        gain, bias = vec[7:8, :], vec[8:9, :]
        keep = wide_of(mask[rows, :], width)
        now = big[n_buf, rows_at(step + 1, SEG), :] * gain + bias
        before = (big[n_buf, rows, :] * gain + bias) * keep
        change = now - before
        in_channel, in_gate = big[gm_buf, rows, :], big[s_buf, rows, :]
        mix_channel, mix_gate = vec[9:10, :], vec[10:11, :]
        scaled = mix_channel * in_channel + mix_gate * in_gate
        big[gm_buf, rows, :] = scaled
        big[nb_buf, rows, :] = (in_channel + in_gate - scaled) * keep
        return sum_channel + fold(in_channel * change), sum_gate + fold(in_gate * change)

    sum_channel, sum_gate = lax.fori_loop(0, steps, mix_two, (zero8, zero8), unroll=2)
    sums[9:10, :] = jnp.sum(sum_channel, axis=0, keepdims=True)
    sums[10:11, :] = jnp.sum(sum_gate, axis=0, keepdims=True)
    big[nb_buf, length : length + SEG, :] = pltpu.roll(big[nb_buf, 0:SEG, :], SEG - 1, 0)
    load_up.wait()

    def norm_two(step, carry):
        sum_gain, sum_bias = carry
        rows = rows_at(step, SEG)
        normed = big[n_buf, rows_at(step + 1, SEG), :]
        incoming = big[gm_buf, rows, :] + big[nb_buf, rows_at(step + 1, SEG), :]
        scaled = incoming * vec[7:8, :]
        mean = jnp.mean(scaled, axis=-1, keepdims=True)
        along = jnp.mean(scaled * normed, axis=-1, keepdims=True)
        scale = wide_of(rsd[1, rows, :], width)
        out = half[1, rows, :].astype(F32) + scale * (scaled - mean - normed * along)
        big[gm_buf, rows, :] = out
        half[0, rows, :] = out.astype(BF16)
        return sum_gain + fold(incoming * normed), sum_bias + fold(incoming)

    sum_gain, sum_bias = lax.fori_loop(0, steps, norm_two, (zero8, zero8), unroll=2)
    sums[7:8, :] = jnp.sum(sum_gain, axis=0, keepdims=True)
    sums[8:9, :] = jnp.sum(sum_bias, axis=0, keepdims=True)
    load_n1 = local(n1_in, big.at[n_buf], sems.at[15])
    load_n1.start()
    load_state = local(state_in, big.at[3:8, 0:length], sems.at[16])
    load_state.start()

    load_att.wait()
    load_w4.wait()
    save_gk.wait()
    grad[:, 3] = dot_tn(sq[:, 0:width], half[0]).astype(BF16).reshape(16, 48, width)

    @pl.loop(0, 2)
    def _(part):
        rows = rows_at(part, length // 2)
        big[nb_buf, rows, :] = dot_nt(half[0, rows, :], wk[:, 3].reshape(width, width))

    rate = -jnp.exp(vec[5:6, :])
    fade = jnp.exp(rate)
    load_state.wait()

    def first(index, carry):
        right, below, through = carry
        step = steps - 1 - index
        rows = rows_at(step, SEG)
        keep_column = mask[rows, :]
        keep = wide_of(keep_column, width)
        bonus = jnp.exp(vec[6:7, :])
        gate, key, value = big[s_buf, rows, :], big[s_buf + 1, rows, :], big[s_buf + 2, rows, :]
        own = bonus * key
        inverse = 1.0 / (big[s_buf + 4, rows, :] + own)
        blended = (big[s_buf + 3, rows, :] + own * value) * inverse
        incoming = big[nb_buf, rows, :] * gate
        sq[rows, width : 2 * width] = (incoming * blended * (1.0 - gate)).astype(BF16)
        weight = incoming * inverse
        big[nb_buf, rows, :] = weight
        big[s_buf, rows, :] = blended
        right = keep * (weight + fade * right)
        below = keep * (weight * blended + fade * below)
        return right, below, through * keep_column

    right, below, through = lax.fori_loop(0, steps, first, (zero, zero, jnp.ones((SEG, LANES), F32)), unroll=2)
    through = wide_of(through, width) * jnp.exp(rate * steps)
    right, below = join_runs((right, below), through, True)

    def second(index, carry):
        right, below, sum_decay, sum_bonus = carry
        step = steps - 1 - index
        rows = rows_at(step, SEG)
        keep = wide_of(mask[rows, :], width)
        bonus = jnp.exp(vec[6:7, :])
        weight, blended = big[nb_buf, rows, :], big[s_buf, rows, :]
        key, value = big[s_buf + 1, rows, :], big[s_buf + 2, rows, :]
        own = bonus * key * weight
        own_key = own * (value - blended)
        sq[rows, 2 * width : 3 * width] = (own_key + key * (right * value - below)).astype(BF16)
        sq[rows, 3 * width : 4 * width] = (own + key * right).astype(BF16)
        sum_bonus = sum_bonus + fold(own_key)
        sum_decay = sum_decay + fold(right * big[s_buf + 3, rows, :] - below * big[s_buf + 4, rows, :])
        right = keep * (weight + fade * right)
        below = keep * (weight * blended + fade * below)
        return right, below, sum_decay, sum_bonus

    _, _, sum_decay, sum_bonus = lax.fori_loop(0, steps, second, (right, below, zero8, zero8), unroll=2)
    sums[5:6, :] = jnp.sum(sum_decay, axis=0, keepdims=True) * (rate * fade)
    sums[6:7, :] = jnp.sum(sum_bonus, axis=0, keepdims=True)

    load_mix.wait()
    mixed = wv.reshape(3, length, width)
    for q in range(3):
        grad[:, q] = dot_tn(mixed[q], sq[:, (q + 1) * width : (q + 2) * width]).astype(BF16).reshape(16, 48, width)
    save_g4 = local(grad, g4_out, sems.at[17])
    save_g4.start()
    for q, place in enumerate((s_buf, s_buf + 3, s_buf + 4)):

        @pl.loop(0, 2)
        def _(part):
            rows = rows_at(part, length // 2)
            big[place, rows, :] = dot_nt(
                sq[rows, (q + 1) * width : (q + 2) * width], wk[:, q].reshape(width, width)
            )

    load_n1.wait()

    def mix_one(step, carry):
        rows = rows_at(step, SEG)
        gain, bias = vec[0:1, :], vec[1:2, :]
        keep = wide_of(mask[rows, :], width)
        now = big[n_buf, rows_at(step + 1, SEG), :] * gain + bias
        before = (big[n_buf, rows, :] * gain + bias) * keep
        change = now - before
        out = []
        scaled, total = None, None
        for q, place in enumerate((s_buf, s_buf + 3, s_buf + 4)):
            incoming = big[place, rows, :]
            part = vec[2 + q : 3 + q, :] * incoming
            scaled = part if scaled is None else scaled + part
            total = incoming if total is None else total + incoming
            out.append(carry[q] + fold(incoming * change))
        big[s_buf, rows, :] = scaled
        big[nb_buf, rows, :] = (total - scaled) * keep
        return tuple(out)

    sum_mix = lax.fori_loop(0, steps, mix_one, (zero8, zero8, zero8), unroll=2)
    for q in range(3):
        sums[2 + q : 3 + q, :] = jnp.sum(sum_mix[q], axis=0, keepdims=True)
    big[nb_buf, length : length + SEG, :] = pltpu.roll(big[nb_buf, 0:SEG, :], SEG - 1, 0)

    def norm_one(step, carry):
        sum_gain, sum_bias = carry
        rows = rows_at(step, SEG)
        normed = big[n_buf, rows_at(step + 1, SEG), :]
        incoming = big[s_buf, rows, :] + big[nb_buf, rows_at(step + 1, SEG), :]
        scaled = incoming * vec[0:1, :]
        mean = jnp.mean(scaled, axis=-1, keepdims=True)
        along = jnp.mean(scaled * normed, axis=-1, keepdims=True)
        scale = wide_of(rsd[0, rows, :], width)
        out = big[gm_buf, rows, :] + scale * (scaled - mean - normed * along)
        put_step(nat, step, steps, out)
        return sum_gain + fold(incoming * normed), sum_bias + fold(incoming)

    sum_gain, sum_bias = lax.fori_loop(0, steps, norm_one, (zero8, zero8), unroll=2)
    sums[0:1, :] = jnp.sum(sum_gain, axis=0, keepdims=True)
    sums[1:2, :] = jnp.sum(sum_bias, axis=0, keepdims=True)
    sums[11:16, :] = jnp.zeros((5, width), F32)
    narrow(nat, half.at[0])
    save_in = local(half.at[0], input_grad, sems.at[18])
    save_in.start()
    save_vec = local(sums, vec_grad, sems.at[19])
    save_vec.start()
    for copy in (save_gg, save_g4, save_in, save_vec):
        copy.wait()


ANY = pl.BlockSpec(memory_space=pl.ANY)
SMEM = pl.BlockSpec(memory_space=pltpu.SMEM)
VMEM = pl.BlockSpec(memory_space=pltpu.VMEM)


def run_forward(lengths, tokens, cotangent, vec, w4, wk, wv, wg):
    length, width = tokens.shape
    shape = jax.ShapeDtypeStruct
    outs = (
        shape((length, width), BF16),
        shape((length + SEG, width), F32),
        shape((length + SEG, width), F32),
        shape((2, length, LANES), F32),
        shape((3, length, width), BF16),
        shape((5, length, width), F32),
        shape((length, width), BF16),
        shape((2, length, width), BF16),
        shape((length, 4 * width), BF16),
        shape((2, length, width), BF16),
        shape((length, width), BF16),
    )
    return pl.pallas_call(
        forward_kernel,
        out_shape=outs,
        in_specs=[SMEM, ANY, ANY, VMEM, ANY, ANY, ANY, ANY],
        out_specs=[ANY] * len(outs),
        scratch_shapes=[
            pltpu.VMEM((16, 4, 48, width), BF16),
            pltpu.VMEM((16, 4, 48, width), BF16),
            pltpu.VMEM((16, 192, width), BF16),
            pltpu.VMEM((16, 48, width), BF16),
            pltpu.VMEM((width // LANES, length, LANES), F32),
            pltpu.VMEM((length + SEG, width), F32),
            pltpu.VMEM((length, width), F32),
            pltpu.VMEM((5, length, width), F32),
            pltpu.VMEM((6, length, width), BF16),
            pltpu.VMEM((length, 4 * width), BF16),
            pltpu.VMEM((length, LANES), F32),
            pltpu.VMEM((2, length, LANES), F32),
            pltpu.SemaphoreType.DMA((17,)),
        ],
        compiler_params=pltpu.CompilerParams(vmem_limit_bytes=VMEM_LIMIT),
        name="forward",
    )(lengths, tokens, cotangent, vec, w4, wk, wv, wg)


def run_backward(lengths, vec, w4, wk, wv, wg, saved):
    n1, n2, r, mix, state, att, cig, sq, gsg, up = saved
    length, width = up.shape
    shape = jax.ShapeDtypeStruct
    slabs = shape((16, 4, 48, width), BF16)
    outs = (shape((length, width), BF16), shape((16, width), F32), slabs, slabs, slabs, shape((16, 48, width), BF16))
    return pl.pallas_call(
        backward_kernel,
        out_shape=outs,
        in_specs=[SMEM, VMEM] + [ANY] * 14,
        out_specs=[ANY] * len(outs),
        scratch_shapes=[
            pltpu.VMEM((16, 4, 48, width), BF16),
            pltpu.VMEM((16, 192, width), BF16),
            pltpu.VMEM((16, 48, width), BF16),
            pltpu.VMEM((8, length + SEG, width), F32),
            pltpu.VMEM((length, 4 * width), BF16),
            pltpu.VMEM((4, length, width), BF16),
            pltpu.VMEM((length, LANES), F32),
            pltpu.VMEM((2, length, LANES), F32),
            pltpu.VMEM((width // LANES, length, LANES), F32),
            pltpu.VMEM((16, 4, 48, width), BF16),
            pltpu.VMEM((16, 48, width), BF16),
            pltpu.VMEM((16, width), F32),
            pltpu.SemaphoreType.DMA((20,)),
        ],
        compiler_params=pltpu.CompilerParams(vmem_limit_bytes=VMEM_LIMIT),
        name="backward",
    )(lengths, vec, w4, wk, wv, wg, n1, n2, r, mix, state, att, cig, sq, gsg, up)


AXES = ("wide", "narrow")


def per_device(
    tokens, lengths, cotangent, vectors,
    time_recept, time_key, time_value, time_output, channel_key, channel_value, channel_recept,
):
    _, length, width = tokens.shape

    def whole(part, axis=0):
        return lax.all_gather(part, AXES, axis=axis, tiled=True)

    vec = jnp.pad(whole(vectors, 1).astype(F32), ((0, 5), (0, 0)))
    square = [whole(m).reshape(16, 48, width) for m in (time_recept, time_key, time_value, time_output)]
    w4 = jnp.stack(square, axis=1)
    wk = jnp.swapaxes(whole(channel_key).reshape(16, 48, 4, width), 1, 2)
    wv = whole(channel_value).reshape(16, 192, width)
    wg = whole(channel_recept).reshape(16, 48, width)
    out = run_forward(lengths, tokens[0], cotangent[0], vec, w4, wk, wv, wg)
    input_grad, vec_grad, g4, gk, gv, gg = run_backward(lengths, vec, w4, wk, wv, wg, out[1:])

    def owned(full, axis=0):
        return lax.psum_scatter(full.astype(F32), AXES, scatter_dimension=axis, tiled=True)

    return (
        out[0][None],
        input_grad[None],
        owned(vec_grad[:11], 1),
        *[owned(g4[:, q].reshape(-1)) for q in range(4)],
        owned(jnp.swapaxes(gk, 1, 2).reshape(-1)),
        owned(gv.reshape(-1)),
        owned(gg.reshape(-1)),
    )


def solution(mesh):
    both = P(AXES)
    rows = P(AXES, None, None)
    return jax.shard_map(
        per_device,
        mesh=mesh,
        in_specs=(rows, P(AXES, None), rows, P(None, AXES)) + (both,) * 7,
        out_specs=(rows, rows, P(None, AXES)) + (both,) * 7,
        check_vma=False,
    )
```

```python
from functools import partial

import jax
import jax.numpy as jnp
from jax import lax
from jax.experimental import pallas as pl
from jax.experimental.pallas import tpu as pltpu
from jax.sharding import PartitionSpec as P


SEG = 16
LANES = 128
EPS = 1e-05
F32 = jnp.float32
BF16 = jnp.bfloat16
VMEM_LIMIT = 62 * 1024 * 1024


def wide_of(column, width):
    return jnp.concatenate([column] * (width // LANES), axis=1)


def dot_nn(left, right):
    return jnp.dot(left, right, preferred_element_type=F32)


def dot_nt(left, right):
    return lax.dot_general(left, right, (((1,), (1,)), ((), ())), preferred_element_type=F32)


def dot_tn(left, right):
    return lax.dot_general(left, right, (((0,), (0,)), ((), ())), preferred_element_type=F32)


def local(source, target, sem):
    return pltpu.make_async_copy(source, target, sem)


def rows_at(index, size):
    return pl.ds(pl.multiple_of(index * size, size), size)


def fill_mask(lengths, mask, length):
    steps = length // SEG

    @pl.loop(0, length // 128)
    def _(block):
        row = block * 128 + lax.broadcasted_iota(jnp.int32, (128, LANES), 0)
        place = (row % SEG) * steps + row // SEG
        start = jnp.int32(0)
        fresh = place == 0
        for doc in range(lengths.shape[1] - 1):
            start = start + lengths[0, doc]
            fresh = jnp.logical_or(fresh, place == start)
        mask[rows_at(block, 128), :] = jnp.where(fresh, 0.0, 1.0)


def widen(source, target):
    @pl.loop(0, source.shape[0] // 32)
    def _(block):
        rows = rows_at(block, 32)
        for c in range(target.shape[0]):
            target[c, rows, :] = source[rows, c * LANES : (c + 1) * LANES].astype(F32)


def narrow(source, target):
    @pl.loop(0, target.shape[0] // 32)
    def _(block):
        rows = rows_at(block, 32)
        for c in range(source.shape[0]):
            target[rows, c * LANES : (c + 1) * LANES] = source[c, rows, :].astype(BF16)


def take_step(source, step, steps):
    strip = pl.ds(step, SEG, stride=steps)
    return jnp.concatenate([source[c, strip, :] for c in range(source.shape[0])], axis=1)


def put_step(target, step, steps, rows):
    strip = pl.ds(step, SEG, stride=steps)
    for c in range(target.shape[0]):
        target[c, strip, :] = rows[:, c * LANES : (c + 1) * LANES]


def norm_rows(rows):
    centred = rows - jnp.mean(rows, axis=-1, keepdims=True)
    scale = lax.rsqrt(jnp.mean(centred * centred, axis=-1, keepdims=True) + EPS)
    return centred * scale, scale


def join_runs(local_end, through, backward):
    index = lax.broadcasted_iota(jnp.int32, local_end[0].shape, 0)
    if backward:
        index = SEG - 1 - index
    states = list(local_end)
    hop = 1
    while hop < SEG:
        turn = SEG - hop if backward else hop
        inside = index >= hop
        moved = pltpu.roll(through, turn, 0)
        states = [jnp.where(inside, s + through * pltpu.roll(s, turn, 0), s) for s in states]
        through = jnp.where(inside, through * moved, through)
        hop *= 2
    turn = SEG - 1 if backward else 1
    return [jnp.where(index >= 1, pltpu.roll(s, turn, 0), 0.0) for s in states]


class Place:
    def __init__(self):
        index = lax.axis_index("wide")
        self.z, self.x, self.c = index // 4, index // 2 % 2, index % 2
        self.y = lax.axis_index("narrow")

    def at(self, z=None, x=None, c=None, y=None):
        z, x = self.z if z is None else z, self.x if x is None else x
        c, y = self.c if c is None else c, self.y if y is None else y
        return (z * 4 + x * 2 + c, y)

    def along_z(self, hop):
        return (self.z + hop) % 4

    def partners(self):
        return [self.at(z=self.along_z(hop)) for hop in (1, 2, 3)] + [
            self.at(x=1 - self.x), self.at(y=1 - self.y), self.at(c=1 - self.c)
        ]


def greet(place):
    barrier = pltpu.get_barrier_semaphore()
    partners = place.partners()
    for partner in partners:
        pl.semaphore_signal(barrier, inc=1, device_id=partner, device_id_type=pl.DeviceIdType.MESH)
    pl.semaphore_wait(barrier, len(partners))


def remote(source, target, send, recv, device):
    return pltpu.make_async_remote_copy(
        src_ref=source, dst_ref=target, send_sem=send, recv_sem=recv,
        device_id=device, device_id_type=pl.DeviceIdType.MESH,
    )


class Gather:
    def __init__(self, place, piece, half_cols, order, send, recv):
        every = slice(None)
        p, (z, x, c) = place, (place.z, place.x, place.c)
        spans = []
        mine = piece(z, x, c, half_cols)
        spans.append([(mine, p.at(z=p.along_z(hop))) for hop in (1, 2, 3)])
        if order == "xy":
            spans.append([(piece(every, x, c, half_cols), p.at(x=1 - x))])
            spans.append([(piece(every, every, c, half_cols), p.at(y=1 - p.y))])
        else:
            spans.append([(piece(every, x, c, half_cols), p.at(y=1 - p.y))])
            spans.append([(piece(every, x, c, every), p.at(x=1 - x))])
        spans.append([(piece(every, every, c, every), p.at(c=1 - c))])
        self.phases, number = [], 0
        for span in spans:
            copies = []
            for ref, device in span:
                copies.append(remote(ref, ref, send.at[number], recv.at[number], device))
                number += 1
            self.phases.append(copies)

    def start(self, phase):
        for copy in self.phases[phase]:
            copy.start()

    def arrive(self, phase):
        for copy in self.phases[phase]:
            copy.wait_recv()

    def step(self, phase):
        if phase:
            self.arrive(phase - 1)
        if phase < len(self.phases):
            self.start(phase)

    def finish(self):
        for copies in self.phases:
            for copy in copies:
                copy.wait_send()


def join_vectors(tiles, vec, share):
    width = vec.shape[1]
    lane = lax.broadcasted_iota(jnp.int32, (16, LANES), 1)
    blocks = [jnp.zeros((16, LANES), F32) for _ in range(width // LANES)]
    for index in range(width // share):
        z, x, c, y = index // 8, index // 4 % 2, index // 2 % 2, index % 2
        block, shift = index * share // LANES, index * share % LANES
        tile = tiles[z, x, c, y]
        tile = pltpu.roll(tile, shift, 1) if shift else tile
        if shift + share > LANES:
            blocks[block] += jnp.where(lane >= shift, tile, 0.0)
            blocks[block + 1] += jnp.where(lane < shift, tile, 0.0)
        else:
            blocks[block] += tile
    for block, tile in enumerate(blocks):
        vec[:, block * LANES : (block + 1) * LANES] = tile


class Gathers:
    GROUPS = (
        (("4", 1, 1, "xy"), ("4", 2, 1, "yx")),
        (("4", 0, 1, "xy"), ("4", 3, 1, "yx")),
        (("k", 0, 1, "xy"), ("k", 1, 1, "yx")),
        (("k", 2, 1, "xy"), ("k", 3, 1, "yx")),
        (("g", 0, 1, "xy"),),
        (("v", 0, 1, "yx"), ("v", 1, 1, "xy")),
        (("v", 2, 1, "yx"), ("v", 3, 1, "xy")),
    )
    AHEAD = 0

    def __init__(self, shards, stages, weights, tile_in, tiles, vec, share, send, recv):
        self.place = place = Place()
        self.shards, self.stages, self.weights = shards, stages, weights
        self.tile_in, self.tiles, self.vec, self.share = tile_in, tiles, vec, share
        half = weights["4"].shape[-1] // 2
        self.cols = pl.ds(pl.multiple_of(place.y * half, half), half)
        self.halves = {
            name: remote(shards[name].at[1 - place.y], stages[name], send.at[0, i], recv.at[0, i], place.at(y=1 - place.y))
            for i, name in enumerate("4kvg")
        }
        self.vectors = Gather(
            place, lambda z, x, c, y: tiles.at[z, x, c, y], place.y, "xy", send.at[1], recv.at[1]
        )
        self.groups, number = [], 2
        for members in self.GROUPS:
            group = []
            for name, first, count, order in members:

                def piece(z, x, c, cols, ref=weights[name], first=first, count=count):
                    return ref.at[z, x, c, pl.ds(first, count), :, cols]

                group.append(Gather(place, piece, self.cols, order, send.at[number], recv.at[number]))
                number += 1
            self.groups.append(group)

    def begin(self):
        place = self.place
        self.tiles[place.z, place.x, place.c, place.y] = self.tile_in[...]
        greet(place)
        self.vectors.start(0)
        for name in "4kvg":
            self.halves[name].start()

    def merge(self):
        place, y = self.place, self.place.y
        for name in "4kgv":
            self.halves[name].wait_recv()
            slab = self.weights[name].at[place.z, place.x, place.c]
            mine, theirs = self.shards[name].at[y], self.stages[name]
            for q in range(mine.shape[0]):
                if name == "v":
                    slab[2 * y + q, :, self.cols] = mine[q]
                    slab[2 * (1 - y) + q, :, self.cols] = theirs[q]
                else:
                    one, two = mine[q].astype(F32), theirs[q].astype(F32)
                    upper, lower = jnp.where(y == 0, one, two), jnp.where(y == 0, two, one)
                    slab[q, :, self.cols] = jnp.concatenate([upper, lower], axis=0).astype(BF16)
            if name == "4":
                self.stage(0)

    def stage(self, number):
        for index, group in enumerate(self.groups):
            if 1 <= number - index <= 4:
                for piece in group:
                    piece.arrive(number - index - 1)
                for piece in group:
                    if number - index < 4:
                        piece.start(number - index)
            early = max(index - self.AHEAD, 0)
            if number == early:
                for piece in group:
                    piece.start(0)

    def finish(self):
        self.vectors.finish()
        for name in "4kvg":
            self.halves[name].wait_send()
        for group in self.groups:
            for piece in group:
                piece.finish()


def forward_kernel(share, *refs):
    lengths, tokens, cotangent, vec_in, w4_in, wk_in, wv_in, wg_in = refs[:8]
    result, n1_out, n2_out, r_out, mix_out, state_out, att_out, cig_out, sq_out, gsg_out, up_out = refs[8:19]
    length, width = tokens.shape
    steps = length // SEG
    if share:
        w4_out, wk_out, wv_out, wg_out, vec_out = refs[19:24]
        w4, wk, wv, wg, nat, norm, mid, state, half, sq, mask, rsd, sems = refs[24:37]
        stage4, stagek, stagev, stageg, tiles, vec, send, recv = refs[37:]
        gathers = Gathers(
            {"4": w4_in, "k": wk_in, "v": wv_in, "g": wg_in},
            {"4": stage4, "k": stagek, "v": stagev, "g": stageg},
            {"4": w4, "k": wk, "v": wv, "g": wg},
            vec_in, tiles, vec, share, send, recv,
        )
    else:
        w4, wk, wv, wg, nat, norm, mid, state, half, sq, mask, rsd, sems = refs[19:]
        vec, gathers = vec_in, None

    def stage(number):
        if gathers:
            gathers.stage(number)

    load_tok = local(tokens, half.at[0], sems.at[0])
    load_cot = local(cotangent, half.at[1], sems.at[1])
    load_tok.start()
    load_cot.start()
    pairs = ((w4_in, w4), (wk_in, wk), (wv_in, wv), (wg_in, wg))
    if gathers:
        gathers.begin()
    else:
        loads = [local(source, target, sems.at[2 + i]) for i, (source, target) in enumerate(pairs)]
        for copy in loads:
            copy.start()
    fill_mask(lengths, mask, length)
    load_tok.wait()
    widen(half.at[0], nat)
    if gathers:
        gathers.merge()
        gathers.vectors.step(1)

    @pl.loop(0, steps, unroll=2)
    def _(step):
        rows = take_step(nat, step, steps)
        mid[rows_at(step, SEG), :] = rows
        normed, scale = norm_rows(rows)
        norm[rows_at(step + 1, SEG), :] = normed
        rsd[0, rows_at(step, SEG), :] = jnp.broadcast_to(scale, (SEG, LANES))

    norm[0:SEG, :] = pltpu.roll(norm[length : length + SEG, :], 1, 0)
    save_n1 = local(norm, n1_out, sems.at[6])
    save_n1.start()
    if gathers:
        gathers.vectors.step(2)
        stage(1)
        gathers.vectors.step(3)
    load_cot.wait()
    widen(half.at[1], nat)
    if gathers:
        gathers.vectors.step(4)
        join_vectors(tiles, vec, share)

    @pl.loop(0, steps, unroll=2)
    def _(step):
        gain, bias = vec[0:1, :], vec[1:2, :]
        rows = rows_at(step, SEG)
        now = norm[rows_at(step + 1, SEG), :] * gain + bias
        before = (norm[rows, :] * gain + bias) * wide_of(mask[rows, :], width)
        change = now - before
        for q in range(3):
            half[2 + q, rows, :] = (before + vec[2 + q : 3 + q, :] * change).astype(BF16)

    save_mix = local(half.at[2:5], mix_out, sems.at[7])
    save_mix.start()
    stage(2)

    @pl.loop(0, steps, unroll=2)
    def _(step):
        half[0, rows_at(step, SEG), :] = take_step(nat, step, steps).astype(BF16)

    save_up = local(half.at[0], up_out, sems.at[13])
    save_up.start()
    stage(3)
    stage(4)

    if not gathers:
        for copy in loads:
            copy.wait()
    for q in (1, 2, 0):
        if q == 0:
            stage(5)

        @pl.loop(0, 2)
        def _(part):
            rows = rows_at(part, length // 2)
            pre = dot_nn(half[2 + q, rows, :], w4[:, :, :, q].reshape(width, width))
            if q == 0:
                pre = jax.nn.sigmoid(pre)
            if q == 1:
                pre = jnp.exp(pre)
            state[q, rows, :] = pre

    rate = -jnp.exp(vec[5:6, :])
    fade = jnp.exp(rate)

    def first(step, carry):
        top, bottom, through = carry
        rows = rows_at(step, SEG)
        keep = mask[rows, :]
        factor = fade * wide_of(keep, width)
        key = state[1, rows, :]
        return factor * top + key * state[2, rows, :], factor * bottom + key, through * keep

    zero = jnp.zeros((SEG, width), F32)
    top, bottom, through = lax.fori_loop(0, steps, first, (zero, zero, jnp.ones((SEG, LANES), F32)), unroll=2)
    through = wide_of(through, width) * jnp.exp(rate * steps)
    top, bottom = join_runs((top, bottom), through, False)

    stage(6)

    def second(step, carry):
        top, bottom = carry
        rows = rows_at(step, SEG)
        keep = wide_of(mask[rows, :], width)
        top, bottom = top * keep, bottom * keep
        key = state[1, rows, :]
        key_value = key * state[2, rows, :]
        bonus = jnp.exp(vec[6:7, :])
        blended = (top + bonus * key_value) / (bottom + bonus * key)
        half[5, rows, :] = (state[0, rows, :] * blended).astype(BF16)
        state[3, rows, :] = top
        state[4, rows, :] = bottom
        return fade * top + key_value, fade * bottom + key

    lax.fori_loop(0, steps, second, (top, bottom), unroll=2)
    save_state = local(state, state_out, sems.at[8])
    save_state.start()
    save_att = local(half.at[5], att_out, sems.at[9])
    save_att.start()

    stage(7)

    @pl.loop(0, 2)
    def _(part):
        rows = rows_at(part, length // 2)
        mid[rows, :] += dot_nn(half[5, rows, :], w4[:, :, :, 3].reshape(width, width))

    stage(8)

    save_n1.wait()

    @pl.loop(0, steps, unroll=2)
    def _(step):
        rows = rows_at(step, SEG)
        normed, scale = norm_rows(mid[rows, :])
        norm[rows_at(step + 1, SEG), :] = normed
        rsd[1, rows, :] = jnp.broadcast_to(scale, (SEG, LANES))

    norm[0:SEG, :] = pltpu.roll(norm[length : length + SEG, :], 1, 0)
    save_n2 = local(norm, n2_out, sems.at[10])
    save_n2.start()
    save_r = local(rsd, r_out, sems.at[11])
    save_r.start()
    save_mix.wait()

    @pl.loop(0, steps, unroll=2)
    def _(step):
        gain, bias = vec[7:8, :], vec[8:9, :]
        rows = rows_at(step, SEG)
        now = norm[rows_at(step + 1, SEG), :] * gain + bias
        before = (norm[rows, :] * gain + bias) * wide_of(mask[rows, :], width)
        change = now - before
        for q in range(2):
            half[2 + q, rows, :] = (before + vec[9 + q : 10 + q, :] * change).astype(BF16)

    save_cig = local(half.at[2:4], cig_out, sems.at[12])
    save_cig.start()

    stage(9)

    for q in range(4):

        @pl.loop(0, 2)
        def _(part):
            rows = rows_at(part, length // 2)
            pre = jnp.maximum(dot_nn(half[2, rows, :], wk[:, :, :, q].reshape(width, width)), 0.0)
            sq[rows, q * width : (q + 1) * width] = (pre * pre).astype(BF16)

    save_sq = local(sq, sq_out, sems.at[14])
    save_sq.start()

    save_state.wait()

    @pl.loop(0, 2)
    def _(part):
        rows = rows_at(part, length // 2)
        state[0, rows, :] = jax.nn.sigmoid(dot_nn(half[3, rows, :], wg[...].reshape(width, width)))

    stage(10)
    stage(11)
    if gathers:
        saves = [
            local(source, target, sems.at[i])
            for source, target, i in (
                (w4, w4_out, 2), (wk, wk_out, 3), (wv, wv_out, 4), (wg, wg_out, 5), (vec, vec_out, 17)
            )
        ]
        for copy in saves:
            copy.start()

    @pl.loop(0, 2)
    def _(part):
        rows = rows_at(part, length // 2)
        state[1, rows, :] = dot_nn(sq[rows, :], wv[...].reshape(4 * width, width))

    save_att.wait()

    @pl.loop(0, steps, unroll=2)
    def _(step):
        rows = rows_at(step, SEG)
        gate, shrunk = state[0, rows, :], state[1, rows, :]
        upstream = half[0, rows, :].astype(F32)
        gated = gate * shrunk
        put_step(nat, step, steps, mid[rows, :] + gated)
        half[4, rows, :] = (upstream * gate).astype(BF16)
        half[5, rows, :] = (upstream * gated * (1.0 - gate)).astype(BF16)

    save_gsg = local(half.at[4:6], gsg_out, sems.at[15])
    save_gsg.start()
    narrow(nat, half.at[1])
    save_res = local(half.at[1], result, sems.at[16])
    save_res.start()
    for copy in (save_n2, save_r, save_cig, save_up, save_sq, save_gsg, save_res):
        copy.wait()
    if gathers:
        for copy in saves:
            copy.wait()
        gathers.finish()


def backward_kernel(
    lengths, vec, w4_in, wk_in, wv_in, wg_in, n1_in, n2_in, r_in, mix_in, state_in, att_in, cig_in, sq_in, gsg_in, up_in,
    input_grad, vec_grad, g4_out, gk_out, gv_out, gg_out,
    wk, wv, wg, big, sq, half, mask, rsd, nat, grad, grad_gate, sums, sems,
):
    length, width = input_grad.shape
    steps = length // SEG
    n_buf, gm_buf, nb_buf, s_buf = 0, 1, 2, 3

    load_gsg = local(gsg_in, half.at[0:2], sems.at[0])
    load_sq = local(sq_in, sq, sems.at[1])
    load_wv = local(wv_in, wv, sems.at[2])
    load_cig = local(cig_in, half.at[2:4], sems.at[3])
    load_wk = local(wk_in, wk, sems.at[4])
    load_wg = local(wg_in, wg, sems.at[5])
    load_n2 = local(n2_in, big.at[n_buf], sems.at[6])
    load_r = local(r_in, rsd, sems.at[7])
    for copy in (load_gsg, load_sq, load_wv, load_cig, load_wk, load_wg, load_n2, load_r):
        copy.start()
    fill_mask(lengths, mask, length)

    load_gsg.wait()
    load_sq.wait()

    @pl.loop(0, 4)
    def _(part):
        out = dot_tn(sq[:, rows_at(part, width)], half[0]).astype(BF16)
        grad[part] = out.reshape(2, 2, 4, 48, width)

    save_gv = local(grad, gv_out, sems.at[8])
    save_gv.start()

    load_wv.wait()

    @pl.loop(0, 4)
    def _(part):
        cols = rows_at(part, width)
        back = dot_nt(half[0], wv[part].reshape(width, width))
        expanded = jnp.sqrt(sq[:, cols].astype(F32))
        sq[:, cols] = (2.0 * expanded * back).astype(BF16)

    load_mix = local(mix_in, wv.reshape(3, length, width), sems.at[9])
    load_mix.start()

    load_cig.wait()
    grad_gate[...] = dot_tn(half[3], half[1]).astype(BF16).reshape(4, 2, 2, 1, 48, width)
    save_gg = local(grad_gate, gg_out, sems.at[10])
    save_gg.start()

    load_wg.wait()
    load_wk.wait()
    big[s_buf, 0:length, :] = dot_nt(half[1], wg[...].reshape(width, width))
    load_up = local(up_in, half.at[1], sems.at[11])
    load_up.start()

    @pl.loop(0, 2)
    def _(part):
        rows = rows_at(part, length // 2)
        out = dot_nt(sq[rows, 0:width], wk[:, :, :, 0].reshape(width, width))
        for q in range(1, 4):
            out += dot_nt(sq[rows, q * width : (q + 1) * width], wk[:, :, :, q].reshape(width, width))
        big[gm_buf, rows, :] = out

    load_w4 = local(w4_in, wk, sems.at[12])
    load_w4.start()

    save_gv.wait()
    for q in range(4):
        grad[:, :, :, q] = dot_tn(half[2], sq[:, q * width : (q + 1) * width]).astype(BF16).reshape(4, 2, 2, 48, width)
    save_gk = local(grad, gk_out, sems.at[13])
    save_gk.start()
    load_att = local(att_in, sq.at[:, 0:width], sems.at[14])
    load_att.start()

    load_n2.wait()
    load_r.wait()

    zero8 = jnp.zeros((8, width), F32)
    zero = jnp.zeros((SEG, width), F32)

    def fold(rows):
        return rows[0:8] + rows[8:16]

    def mix_two(step, carry):
        sum_channel, sum_gate = carry
        rows = rows_at(step, SEG)
        gain, bias = vec[7:8, :], vec[8:9, :]
        keep = wide_of(mask[rows, :], width)
        now = big[n_buf, rows_at(step + 1, SEG), :] * gain + bias
        before = (big[n_buf, rows, :] * gain + bias) * keep
        change = now - before
        in_channel, in_gate = big[gm_buf, rows, :], big[s_buf, rows, :]
        mix_channel, mix_gate = vec[9:10, :], vec[10:11, :]
        scaled = mix_channel * in_channel + mix_gate * in_gate
        big[gm_buf, rows, :] = scaled
        big[nb_buf, rows, :] = (in_channel + in_gate - scaled) * keep
        return sum_channel + fold(in_channel * change), sum_gate + fold(in_gate * change)

    sum_channel, sum_gate = lax.fori_loop(0, steps, mix_two, (zero8, zero8), unroll=2)
    sums[9:10, :] = jnp.sum(sum_channel, axis=0, keepdims=True)
    sums[10:11, :] = jnp.sum(sum_gate, axis=0, keepdims=True)
    big[nb_buf, length : length + SEG, :] = pltpu.roll(big[nb_buf, 0:SEG, :], SEG - 1, 0)
    load_up.wait()

    def norm_two(step, carry):
        sum_gain, sum_bias = carry
        rows = rows_at(step, SEG)
        normed = big[n_buf, rows_at(step + 1, SEG), :]
        incoming = big[gm_buf, rows, :] + big[nb_buf, rows_at(step + 1, SEG), :]
        scaled = incoming * vec[7:8, :]
        mean = jnp.mean(scaled, axis=-1, keepdims=True)
        along = jnp.mean(scaled * normed, axis=-1, keepdims=True)
        scale = wide_of(rsd[1, rows, :], width)
        out = half[1, rows, :].astype(F32) + scale * (scaled - mean - normed * along)
        big[gm_buf, rows, :] = out
        half[0, rows, :] = out.astype(BF16)
        return sum_gain + fold(incoming * normed), sum_bias + fold(incoming)

    sum_gain, sum_bias = lax.fori_loop(0, steps, norm_two, (zero8, zero8), unroll=2)
    sums[7:8, :] = jnp.sum(sum_gain, axis=0, keepdims=True)
    sums[8:9, :] = jnp.sum(sum_bias, axis=0, keepdims=True)
    load_n1 = local(n1_in, big.at[n_buf], sems.at[15])
    load_n1.start()
    load_state = local(state_in, big.at[3:8, 0:length], sems.at[16])
    load_state.start()

    load_att.wait()
    load_w4.wait()
    save_gk.wait()
    grad[:, :, :, 3] = dot_tn(sq[:, 0:width], half[0]).astype(BF16).reshape(4, 2, 2, 48, width)

    @pl.loop(0, 2)
    def _(part):
        rows = rows_at(part, length // 2)
        big[nb_buf, rows, :] = dot_nt(half[0, rows, :], wk[:, :, :, 3].reshape(width, width))

    rate = -jnp.exp(vec[5:6, :])
    fade = jnp.exp(rate)
    load_state.wait()

    def first(index, carry):
        right, below, through = carry
        step = steps - 1 - index
        rows = rows_at(step, SEG)
        keep_column = mask[rows, :]
        keep = wide_of(keep_column, width)
        bonus = jnp.exp(vec[6:7, :])
        gate, key, value = big[s_buf, rows, :], big[s_buf + 1, rows, :], big[s_buf + 2, rows, :]
        own = bonus * key
        inverse = 1.0 / (big[s_buf + 4, rows, :] + own)
        blended = (big[s_buf + 3, rows, :] + own * value) * inverse
        incoming = big[nb_buf, rows, :] * gate
        sq[rows, width : 2 * width] = (incoming * blended * (1.0 - gate)).astype(BF16)
        weight = incoming * inverse
        big[nb_buf, rows, :] = weight
        big[s_buf, rows, :] = blended
        right = keep * (weight + fade * right)
        below = keep * (weight * blended + fade * below)
        return right, below, through * keep_column

    right, below, through = lax.fori_loop(0, steps, first, (zero, zero, jnp.ones((SEG, LANES), F32)), unroll=2)
    through = wide_of(through, width) * jnp.exp(rate * steps)
    right, below = join_runs((right, below), through, True)

    def second(index, carry):
        right, below, sum_decay, sum_bonus = carry
        step = steps - 1 - index
        rows = rows_at(step, SEG)
        keep = wide_of(mask[rows, :], width)
        bonus = jnp.exp(vec[6:7, :])
        weight, blended = big[nb_buf, rows, :], big[s_buf, rows, :]
        key, value = big[s_buf + 1, rows, :], big[s_buf + 2, rows, :]
        own = bonus * key * weight
        own_key = own * (value - blended)
        sq[rows, 2 * width : 3 * width] = (own_key + key * (right * value - below)).astype(BF16)
        sq[rows, 3 * width : 4 * width] = (own + key * right).astype(BF16)
        sum_bonus = sum_bonus + fold(own_key)
        sum_decay = sum_decay + fold(right * big[s_buf + 3, rows, :] - below * big[s_buf + 4, rows, :])
        right = keep * (weight + fade * right)
        below = keep * (weight * blended + fade * below)
        return right, below, sum_decay, sum_bonus

    _, _, sum_decay, sum_bonus = lax.fori_loop(0, steps, second, (right, below, zero8, zero8), unroll=2)
    sums[5:6, :] = jnp.sum(sum_decay, axis=0, keepdims=True) * (rate * fade)
    sums[6:7, :] = jnp.sum(sum_bonus, axis=0, keepdims=True)

    load_mix.wait()
    mixed = wv.reshape(3, length, width)
    for q in range(3):
        grad[:, :, :, q] = dot_tn(mixed[q], sq[:, (q + 1) * width : (q + 2) * width]).astype(BF16).reshape(4, 2, 2, 48, width)
    save_g4 = local(grad, g4_out, sems.at[17])
    save_g4.start()
    for q, place in enumerate((s_buf, s_buf + 3, s_buf + 4)):

        @pl.loop(0, 2)
        def _(part):
            rows = rows_at(part, length // 2)
            big[place, rows, :] = dot_nt(
                sq[rows, (q + 1) * width : (q + 2) * width], wk[:, :, :, q].reshape(width, width)
            )

    load_n1.wait()

    def mix_one(step, carry):
        rows = rows_at(step, SEG)
        gain, bias = vec[0:1, :], vec[1:2, :]
        keep = wide_of(mask[rows, :], width)
        now = big[n_buf, rows_at(step + 1, SEG), :] * gain + bias
        before = (big[n_buf, rows, :] * gain + bias) * keep
        change = now - before
        out = []
        scaled, total = None, None
        for q, place in enumerate((s_buf, s_buf + 3, s_buf + 4)):
            incoming = big[place, rows, :]
            part = vec[2 + q : 3 + q, :] * incoming
            scaled = part if scaled is None else scaled + part
            total = incoming if total is None else total + incoming
            out.append(carry[q] + fold(incoming * change))
        big[s_buf, rows, :] = scaled
        big[nb_buf, rows, :] = (total - scaled) * keep
        return tuple(out)

    sum_mix = lax.fori_loop(0, steps, mix_one, (zero8, zero8, zero8), unroll=2)
    for q in range(3):
        sums[2 + q : 3 + q, :] = jnp.sum(sum_mix[q], axis=0, keepdims=True)
    big[nb_buf, length : length + SEG, :] = pltpu.roll(big[nb_buf, 0:SEG, :], SEG - 1, 0)

    def norm_one(step, carry):
        sum_gain, sum_bias = carry
        rows = rows_at(step, SEG)
        normed = big[n_buf, rows_at(step + 1, SEG), :]
        incoming = big[s_buf, rows, :] + big[nb_buf, rows_at(step + 1, SEG), :]
        scaled = incoming * vec[0:1, :]
        mean = jnp.mean(scaled, axis=-1, keepdims=True)
        along = jnp.mean(scaled * normed, axis=-1, keepdims=True)
        scale = wide_of(rsd[0, rows, :], width)
        out = big[gm_buf, rows, :] + scale * (scaled - mean - normed * along)
        put_step(nat, step, steps, out)
        return sum_gain + fold(incoming * normed), sum_bias + fold(incoming)

    sum_gain, sum_bias = lax.fori_loop(0, steps, norm_one, (zero8, zero8), unroll=2)
    sums[0:1, :] = jnp.sum(sum_gain, axis=0, keepdims=True)
    sums[1:2, :] = jnp.sum(sum_bias, axis=0, keepdims=True)
    sums[11:16, :] = jnp.zeros((5, width), F32)
    narrow(nat, half.at[0])
    save_in = local(half.at[0], input_grad, sems.at[18])
    save_in.start()
    save_vec = local(sums, vec_grad, sems.at[19])
    save_vec.start()
    for copy in (save_gg, save_g4, save_in, save_vec):
        copy.wait()


ANY = pl.BlockSpec(memory_space=pl.ANY)
SMEM = pl.BlockSpec(memory_space=pltpu.SMEM)
VMEM = pl.BlockSpec(memory_space=pltpu.VMEM)


def run_forward(lengths, tokens, cotangent, vec, w4, wk, wv, wg, share=None):
    length, width = tokens.shape
    shape = jax.ShapeDtypeStruct
    outs = (
        shape((length, width), BF16),
        shape((length + SEG, width), F32),
        shape((length + SEG, width), F32),
        shape((2, length, LANES), F32),
        shape((3, length, width), BF16),
        shape((5, length, width), F32),
        shape((length, width), BF16),
        shape((2, length, width), BF16),
        shape((length, 4 * width), BF16),
        shape((2, length, width), BF16),
        shape((length, width), BF16),
    )
    slabs, gate = (4, 2, 2, 4, 48, width), (4, 2, 2, 1, 48, width)
    scratch = [
        pltpu.VMEM(slabs, BF16),
        pltpu.VMEM(slabs, BF16),
        pltpu.VMEM(slabs, BF16),
        pltpu.VMEM(gate, BF16),
        pltpu.VMEM((width // LANES, length, LANES), F32),
        pltpu.VMEM((length + SEG, width), F32),
        pltpu.VMEM((length, width), F32),
        pltpu.VMEM((5, length, width), F32),
        pltpu.VMEM((6, length, width), BF16),
        pltpu.VMEM((length, 4 * width), BF16),
        pltpu.VMEM((length, LANES), F32),
        pltpu.VMEM((2, length, LANES), F32),
        pltpu.SemaphoreType.DMA((18,)),
    ]
    in_specs = [SMEM, ANY, ANY, VMEM, ANY, ANY, ANY, ANY]
    params = {}
    if share:
        outs += (shape(slabs, BF16),) * 3 + (shape(gate, BF16), shape((16, width), F32))
        scratch += [pltpu.VMEM(part.shape[1:], BF16) for part in (w4, wk, wv, wg)]
        scratch += [
            pltpu.VMEM((4, 2, 2, 2, 16, LANES), F32),
            pltpu.VMEM((16, width), F32),
            pltpu.SemaphoreType.DMA((15, 6)),
            pltpu.SemaphoreType.DMA((15, 6)),
        ]
        in_specs = [SMEM, ANY, ANY, VMEM, VMEM, VMEM, VMEM, VMEM]
        params = dict(collective_id=0, has_side_effects=True)
    return pl.pallas_call(
        partial(forward_kernel, share),
        out_shape=outs,
        in_specs=in_specs,
        out_specs=[ANY] * len(outs),
        scratch_shapes=scratch,
        compiler_params=pltpu.CompilerParams(vmem_limit_bytes=VMEM_LIMIT, **params),
        name="forward",
    )(lengths, tokens, cotangent, vec, w4, wk, wv, wg)


def run_backward(lengths, vec, w4, wk, wv, wg, saved):
    n1, n2, r, mix, state, att, cig, sq, gsg, up = saved
    length, width = up.shape
    shape = jax.ShapeDtypeStruct
    slabs, gate = (4, 2, 2, 4, 48, width), (4, 2, 2, 1, 48, width)
    full, one = shape(slabs, BF16), shape(gate, BF16)
    outs = (shape((length, width), BF16), shape((16, width), F32), full, full, full, one)
    return pl.pallas_call(
        backward_kernel,
        out_shape=outs,
        in_specs=[SMEM, VMEM] + [ANY] * 14,
        out_specs=[ANY] * len(outs),
        scratch_shapes=[
            pltpu.VMEM(slabs, BF16),
            pltpu.VMEM(slabs, BF16),
            pltpu.VMEM(gate, BF16),
            pltpu.VMEM((8, length + SEG, width), F32),
            pltpu.VMEM((length, 4 * width), BF16),
            pltpu.VMEM((4, length, width), BF16),
            pltpu.VMEM((length, LANES), F32),
            pltpu.VMEM((2, length, LANES), F32),
            pltpu.VMEM((width // LANES, length, LANES), F32),
            pltpu.VMEM(slabs, BF16),
            pltpu.VMEM(gate, BF16),
            pltpu.VMEM((16, width), F32),
            pltpu.SemaphoreType.DMA((20,)),
        ],
        compiler_params=pltpu.CompilerParams(vmem_limit_bytes=VMEM_LIMIT),
        name="backward",
    )(lengths, vec, w4, wk, wv, wg, n1, n2, r, mix, state, att, cig, sq, gsg, up)


AXES = ("wide", "narrow")


def per_device(
    direct, tokens, lengths, cotangent, vectors,
    time_recept, time_key, time_value, time_output, channel_key, channel_value, channel_recept,
):
    _, length, width = tokens.shape
    slabs, gate = (4, 2, 2, 4, 48, width), (4, 2, 2, 1, 48, width)

    if direct:
        share = vectors.shape[1]

        def halves(parts, blocks, rows):
            return jnp.moveaxis(parts.reshape(blocks, rows, 2, width // 2), 2, 0)

        tile = jnp.pad(vectors.astype(F32), ((0, 5), (0, LANES - share)))
        times = jnp.stack([time_recept, time_key, time_value, time_output])
        key = jnp.swapaxes(channel_key.reshape(24, 4, width), 0, 1)
        out = run_forward(
            lengths, tokens[0], cotangent[0], tile,
            halves(times, 4, 24), halves(key, 4, 24), halves(channel_value, 2, 48), halves(channel_recept, 1, 24),
            share=share,
        )
        w4, wk, wv, wg, vec = out[11:]
    else:

        def whole(part, axis=0):
            return lax.all_gather(part, AXES, axis=axis, tiled=True)

        vec = jnp.pad(whole(vectors, 1).astype(F32), ((0, 5), (0, 0)))
        square = [whole(m).reshape(16, 48, width) for m in (time_recept, time_key, time_value, time_output)]
        w4 = jnp.stack(square, axis=1).reshape(slabs)
        wk = jnp.swapaxes(whole(channel_key).reshape(16, 48, 4, width), 1, 2).reshape(slabs)
        wv = whole(channel_value).reshape(slabs)
        wg = whole(channel_recept).reshape(gate)
        out = run_forward(lengths, tokens[0], cotangent[0], vec, w4, wk, wv, wg)
    input_grad, vec_grad, g4, gk, gv, gg = run_backward(lengths, vec, w4, wk, wv, wg, out[1:11])

    def owned(full, axis=0):
        return lax.psum_scatter(full.astype(F32), AXES, scatter_dimension=axis, tiled=True)

    return (
        out[0][None],
        input_grad[None],
        owned(vec_grad[:11], 1),
        *[owned(g4[:, :, :, q].reshape(-1)) for q in range(4)],
        owned(jnp.swapaxes(gk.reshape(16, 4, 48, width), 1, 2).reshape(-1)),
        owned(gv.reshape(-1)),
        owned(gg.reshape(-1)),
    )


def solution(mesh):
    both = P(AXES)
    rows = P(AXES, None, None)
    direct = dict(mesh.shape) == {"wide": 16, "narrow": 2}
    return jax.shard_map(
        partial(per_device, direct),
        mesh=mesh,
        in_specs=(rows, P(AXES, None), rows, P(None, AXES)) + (both,) * 7,
        out_specs=(rows, rows, P(None, AXES)) + (both,) * 7,
        check_vma=False,
    )
```

```python
from functools import partial

import jax
import jax.numpy as jnp
from jax import lax
from jax.experimental import pallas as pl
from jax.experimental.pallas import tpu as pltpu
from jax.sharding import PartitionSpec as P


SEG = 16
LANES = 128
EPS = 1e-05
F32 = jnp.float32
BF16 = jnp.bfloat16
VMEM_LIMIT = 63 * 1024 * 1024


def wide_of(column, width):
    return jnp.concatenate([column] * (width // LANES), axis=1)


def dot_nn(left, right):
    return jnp.dot(left, right, preferred_element_type=F32)


def dot_nt(left, right):
    return lax.dot_general(left, right, (((1,), (1,)), ((), ())), preferred_element_type=F32)


def dot_tn(left, right):
    return lax.dot_general(left, right, (((0,), (0,)), ((), ())), preferred_element_type=F32)


def local(source, target, sem):
    return pltpu.make_async_copy(source, target, sem)


def rows_at(index, size):
    return pl.ds(pl.multiple_of(index * size, size), size)


def fill_mask(lengths, mask, length):
    steps = length // SEG

    @pl.loop(0, length // 128)
    def _(block):
        row = block * 128 + lax.broadcasted_iota(jnp.int32, (128, LANES), 0)
        place = (row % SEG) * steps + row // SEG
        start = jnp.int32(0)
        fresh = place == 0
        for doc in range(lengths.shape[1] - 1):
            start = start + lengths[0, doc]
            fresh = jnp.logical_or(fresh, place == start)
        mask[rows_at(block, 128), :] = jnp.where(fresh, 0.0, 1.0)


def widen(source, target):
    @pl.loop(0, source.shape[0] // 32)
    def _(block):
        rows = rows_at(block, 32)
        for c in range(target.shape[0]):
            target[c, rows, :] = source[rows, c * LANES : (c + 1) * LANES].astype(F32)


def narrow(source, target):
    @pl.loop(0, target.shape[0] // 32)
    def _(block):
        rows = rows_at(block, 32)
        for c in range(source.shape[0]):
            target[rows, c * LANES : (c + 1) * LANES] = source[c, rows, :].astype(BF16)


def take_step(source, step, steps):
    strip = pl.ds(step, SEG, stride=steps)
    return jnp.concatenate([source[c, strip, :] for c in range(source.shape[0])], axis=1)


def put_step(target, step, steps, rows):
    strip = pl.ds(step, SEG, stride=steps)
    for c in range(target.shape[0]):
        target[c, strip, :] = rows[:, c * LANES : (c + 1) * LANES]


def take_rows(source, rows):
    return jnp.concatenate([source[c, rows, :] for c in range(source.shape[0])], axis=1)


def put_rows(target, rows, value):
    for c in range(target.shape[0]):
        target[c, rows, :] = value[:, c * LANES : (c + 1) * LANES]


def norm_rows(rows):
    centred = rows - jnp.mean(rows, axis=-1, keepdims=True)
    scale = lax.rsqrt(jnp.mean(centred * centred, axis=-1, keepdims=True) + EPS)
    return centred * scale, scale


def join_runs(local_end, through, backward):
    index = lax.broadcasted_iota(jnp.int32, local_end[0].shape, 0)
    if backward:
        index = SEG - 1 - index
    states = list(local_end)
    hop = 1
    while hop < SEG:
        turn = SEG - hop if backward else hop
        inside = index >= hop
        moved = pltpu.roll(through, turn, 0)
        states = [jnp.where(inside, s + through * pltpu.roll(s, turn, 0), s) for s in states]
        through = jnp.where(inside, through * moved, through)
        hop *= 2
    turn = SEG - 1 if backward else 1
    return [jnp.where(index >= 1, pltpu.roll(s, turn, 0), 0.0) for s in states]


class Place:
    def __init__(self):
        index = lax.axis_index("wide")
        self.z, self.x, self.c = index // 4, index // 2 % 2, index % 2
        self.y = lax.axis_index("narrow")

    def at(self, z=None, x=None, c=None, y=None):
        z, x = self.z if z is None else z, self.x if x is None else x
        c, y = self.c if c is None else c, self.y if y is None else y
        return (z * 4 + x * 2 + c, y)

    def along_z(self, hop):
        return (self.z + hop) % 4

    def partners(self):
        return [self.at(z=self.along_z(hop)) for hop in (1, 2, 3)] + [
            self.at(x=1 - self.x), self.at(y=1 - self.y), self.at(c=1 - self.c)
        ]


def greet(place):
    barrier = pltpu.get_barrier_semaphore()
    partners = place.partners()
    for partner in partners:
        pl.semaphore_signal(barrier, inc=1, device_id=partner, device_id_type=pl.DeviceIdType.MESH)
    pl.semaphore_wait(barrier, len(partners))


def remote(source, target, send, recv, device):
    return pltpu.make_async_remote_copy(
        src_ref=source, dst_ref=target, send_sem=send, recv_sem=recv,
        device_id=device, device_id_type=pl.DeviceIdType.MESH,
    )


class Gather:
    def __init__(self, place, piece, half_cols, order, send, recv):
        every = slice(None)
        p, (z, x, c) = place, (place.z, place.x, place.c)
        spans = []
        mine = piece(z, x, c, half_cols)
        spans.append([(mine, p.at(z=p.along_z(hop))) for hop in (1, 2, 3)])
        if order == "xy":
            spans.append([(piece(every, x, c, half_cols), p.at(x=1 - x))])
            spans.append([(piece(every, every, c, half_cols), p.at(y=1 - p.y))])
        else:
            spans.append([(piece(every, x, c, half_cols), p.at(y=1 - p.y))])
            spans.append([(piece(every, x, c, every), p.at(x=1 - x))])
        spans.append([(piece(every, every, c, every), p.at(c=1 - c))])
        self.phases, number = [], 0
        for span in spans:
            copies = []
            for ref, device in span:
                copies.append(remote(ref, ref, send.at[number], recv.at[number], device))
                number += 1
            self.phases.append(copies)

    def start(self, phase):
        for copy in self.phases[phase]:
            copy.start()

    def arrive(self, phase):
        for copy in self.phases[phase]:
            copy.wait_recv()

    def step(self, phase):
        if phase:
            self.arrive(phase - 1)
        if phase < len(self.phases):
            self.start(phase)

    def finish(self):
        for copies in self.phases:
            for copy in copies:
                copy.wait_send()


def join_vectors(tiles, vec, share):
    width = vec.shape[1]
    lane = lax.broadcasted_iota(jnp.int32, (16, LANES), 1)
    blocks = [jnp.zeros((16, LANES), F32) for _ in range(width // LANES)]
    for index in range(width // share):
        z, x, c, y = index // 8, index // 4 % 2, index // 2 % 2, index % 2
        block, shift = index * share // LANES, index * share % LANES
        tile = tiles[z, x, c, y]
        tile = pltpu.roll(tile, shift, 1) if shift else tile
        if shift + share > LANES:
            blocks[block] += jnp.where(lane >= shift, tile, 0.0)
            blocks[block + 1] += jnp.where(lane < shift, tile, 0.0)
        else:
            blocks[block] += tile
    for block, tile in enumerate(blocks):
        vec[:, block * LANES : (block + 1) * LANES] = tile


class Gathers:
    GROUPS = (
        (("4", 1, 1, "xy"), ("4", 2, 1, "yx")),
        (("4", 0, 1, "xy"), ("4", 3, 1, "yx")),
        (("k", 0, 1, "xy"), ("k", 1, 1, "yx")),
        (("k", 2, 1, "xy"), ("k", 3, 1, "yx")),
        (("g", 0, 1, "xy"),),
        (("v", 0, 1, "yx"), ("v", 1, 1, "xy")),
        (("v", 2, 1, "yx"), ("v", 3, 1, "xy")),
    )
    AHEAD = 0

    def __init__(self, shards, stages, weights, tile_in, tiles, vec, share, send, recv):
        self.place = place = Place()
        self.shards, self.stages, self.weights = shards, stages, weights
        self.tile_in, self.tiles, self.vec, self.share = tile_in, tiles, vec, share
        half = weights["4"].shape[-1] // 2
        self.cols = pl.ds(pl.multiple_of(place.y * half, half), half)
        self.halves = {
            name: remote(shards[name].at[1 - place.y], stages[name], send.at[0, i], recv.at[0, i], place.at(y=1 - place.y))
            for i, name in enumerate("4kvg")
        }
        self.vectors = Gather(
            place, lambda z, x, c, y: tiles.at[z, x, c, y], place.y, "xy", send.at[1], recv.at[1]
        )
        self.groups, number = [], 2
        for members in self.GROUPS:
            group = []
            for name, first, count, order in members:

                def piece(z, x, c, cols, ref=weights[name], first=first, count=count):
                    return ref.at[z, x, c, pl.ds(first, count), :, cols]

                group.append(Gather(place, piece, self.cols, order, send.at[number], recv.at[number]))
                number += 1
            self.groups.append(group)

    def begin(self):
        place = self.place
        self.tiles[place.z, place.x, place.c, place.y] = self.tile_in[...]
        greet(place)
        self.vectors.start(0)
        for name in "4kvg":
            self.halves[name].start()

    def merge(self):
        place, y = self.place, self.place.y
        for name in "4kgv":
            self.halves[name].wait_recv()
            slab = self.weights[name].at[place.z, place.x, place.c]
            mine, theirs = self.shards[name].at[y], self.stages[name]
            for q in range(mine.shape[0]):
                if name == "v":
                    slab[2 * y + q, :, self.cols] = mine[q]
                    slab[2 * (1 - y) + q, :, self.cols] = theirs[q]
                else:
                    one, two = mine[q].astype(F32), theirs[q].astype(F32)
                    upper, lower = jnp.where(y == 0, one, two), jnp.where(y == 0, two, one)
                    slab[q, :, self.cols] = jnp.concatenate([upper, lower], axis=0).astype(BF16)
            if name == "4":
                self.stage(0)

    def stage(self, number):
        for index, group in enumerate(self.groups):
            if 1 <= number - index <= 4:
                for piece in group:
                    piece.arrive(number - index - 1)
                for piece in group:
                    if number - index < 4:
                        piece.start(number - index)
            early = max(index - self.AHEAD, 0)
            if number == early:
                for piece in group:
                    piece.start(0)

    def finish(self):
        self.vectors.finish()
        for name in "4kvg":
            self.halves[name].wait_send()
        for group in self.groups:
            for piece in group:
                piece.finish()


class Scatter:
    def __init__(self, place, cols, grad, ways, send, recv):
        p, (mine, other), every = place, cols, slice(None)
        self.place, self.mine, self.grad = place, mine, grad
        self.sum, self.first, self.second, self.third, self.y_first = ways
        total, x = self.sum, p.x
        copies = [[remote(grad.at[:, :, 1 - p.c], total, send.at[0], recv.at[0], p.at(c=1 - p.c))]]
        if self.y_first:
            one, to_one = total.at[:, :, :, other], p.at(y=1 - p.y)
            two, to_two = total.at[:, 1 - x, :, mine], p.at(x=1 - x)
        else:
            one, to_one = total.at[:, 1 - x], p.at(x=1 - x)
            two, to_two = total.at[:, x, :, other], p.at(y=1 - p.y)
        copies.append([remote(one, self.first, send.at[1], recv.at[1], to_one)])
        copies.append([remote(two, self.second, send.at[2], recv.at[2], to_two)])
        copies.append([
            remote(total.at[p.along_z(hop), x, :, mine], self.third.at[hop - 1], send.at[2 + hop], recv.at[2 + hop],
                   p.at(z=p.along_z(hop)))
            for hop in (1, 2, 3)
        ])
        self.copies = copies

    def start(self, phase):
        for copy in self.copies[phase]:
            copy.start()

    def sent(self, *phases):
        for phase in phases:
            for copy in self.copies[phase]:
                copy.wait_send()

    def step(self, number):
        if number:
            for copy in self.copies[number - 1]:
                copy.wait_recv()
        p, total, mine = self.place, self.sum, self.mine
        if number == 1:

            @pl.loop(0, 4)
            def _(z):
                for x in range(2):
                    total[z, x] += self.grad[z, x, p.c]

        if number == 2:

            @pl.loop(0, 4)
            def _(z):
                if self.y_first:
                    for x in range(2):
                        total[z, x, :, mine] += self.first[z, x]
                else:
                    total[z, p.x] += self.first[z]

        if number == 3:

            @pl.loop(0, 4)
            def _(z):
                total[z, p.x, :, mine] += self.second[z]

        if number < 4:
            self.start(number)

    def result(self):
        p = self.place
        total = self.sum[p.z, p.x, :, self.mine].astype(F32)
        for hop in range(3):
            total += self.third[hop].astype(F32)
        return total


class Scatters:
    SLOTS = {"v": (0, 1, 2, 3), "4": (0, 1, 2, 3), "k": (4, 5, 6, 7), "g": (8,)}

    def __init__(self, grad, grad_gate, outs, ways, finals, arrived, sums, send, recv, free):
        self.place = place = Place()
        self.outs, self.finals, self.arrived, self.sums, self.free = outs, finals, arrived, sums, free
        half = grad.shape[-1] // 2
        mine = pl.ds(pl.multiple_of(place.y * half, half), half)
        other = pl.ds(pl.multiple_of((1 - place.y) * half, half), half)
        self.mine, self.other = mine, other
        total, first_y, first_x, second, third = ways
        self.pieces, number = {}, 0
        for name, slots in self.SLOTS.items():
            source = grad_gate if name == "g" else grad
            for q, slot in enumerate(slots):
                y_first = slot % 2 == 0
                first = (first_y if y_first else first_x).at[slot // 2]
                way = (total.at[slot], first, second.at[slot], third.at[slot], y_first)
                self.pieces[name, q] = Scatter(
                    place, (mine, other), source.at[:, :, :, q], way, send.at[number], recv.at[number]
                )
                number += 1
        self.last = {
            name: remote(finals[name], arrived[name], send.at[number, i], recv.at[number, i], place.at(y=1 - place.y))
            for i, name in enumerate("4kvg")
        }
        number += 1
        to = [place.at(c=1 - place.c), place.at(y=1 - place.y), place.at(x=1 - place.x)]
        self.hops = [
            [remote(sums.at[i], sums.at[4 + i], send.at[number, i], recv.at[number, i], device)]
            for i, device in enumerate(to)
        ]
        self.hops.append([
            remote(sums.at[3], sums.at[6 + hop], send.at[number, 2 + hop], recv.at[number, 2 + hop],
                   place.at(z=place.along_z(hop)))
            for hop in (1, 2, 3)
        ])

    def step(self, name, qs, number):
        for q in qs:
            self.pieces[name, q].step(number)

    def close(self, name, qs):
        y = self.place.y
        for q in qs:
            piece = self.pieces[name, q]
            piece.step(4)
            total = piece.result()
            if name == "v":

                @pl.when(y == q // 2)
                def _():
                    self.outs[name][q % 2, :, self.mine] = total

                @pl.when(y != q // 2)
                def _():
                    self.finals[name][q % 2] = total.astype(BF16)
            else:
                half = total.shape[0] // 2
                upper, lower = total[:half], total[half:]
                self.outs[name][q, :, self.mine] = jnp.where(y == 0, upper, lower)
                self.finals[name][q] = jnp.where(y == 0, lower, upper).astype(BF16)

    def send_rows(self, name):
        self.last[name].start()

    def take_rows(self, name):
        self.last[name].wait_recv()
        self.outs[name][:, :, self.other] = self.arrived[name][...].astype(F32)

    def release(self):
        for q in range(4):
            self.pieces["v", q].sent(1, 2, 3)
        for partner in self.place.partners():
            pl.semaphore_signal(self.free, inc=1, device_id=partner, device_id_type=pl.DeviceIdType.MESH)

    def claim(self):
        pl.semaphore_wait(self.free, 6)

    def hop(self, number):
        if number:
            for copy in self.hops[number - 1]:
                copy.wait_recv()
        if 1 <= number <= 3:
            self.sums[number] = self.sums[number - 1] + self.sums[3 + number]
        if number < 4:
            for copy in self.hops[number]:
                copy.start()

    def finish(self):
        for (name, _), piece in self.pieces.items():
            if name == "v":
                continue
            piece.sent(1, 2, 3)
            if name != "k":
                piece.sent(0)
        for copy in self.last.values():
            copy.wait_send()
        for copies in self.hops:
            for copy in copies:
                copy.wait_send()


def forward_kernel(share, *refs):
    lengths, tokens, cotangent, vec_in, w4_in, wk_in, wv_in, wg_in = refs[:8]
    result, n1_out, n2_out, r_out, mix_out, state_out, key_out, att_out, cig_out, sq_out, gsg_out, up_out = refs[8:20]
    length, width = tokens.shape
    steps = length // SEG
    if share:
        w4_out, wk_out, wv_out, wg_out, vec_out = refs[20:25]
        w4, wk, wv, wg, nat, norm, mid, state, keys, half, sq, mask, rsd, sems = refs[25:39]
        stage4, stagek, stagev, stageg, tiles, vec, send, recv = refs[39:]
        gathers = Gathers(
            {"4": w4_in, "k": wk_in, "v": wv_in, "g": wg_in},
            {"4": stage4, "k": stagek, "v": stagev, "g": stageg},
            {"4": w4, "k": wk, "v": wv, "g": wg},
            vec_in, tiles, vec, share, send, recv,
        )
    else:
        w4, wk, wv, wg, nat, norm, mid, state, keys, half, sq, mask, rsd, sems = refs[20:]
        vec, gathers = vec_in, None

    def stage(number):
        if gathers:
            gathers.stage(number)

    load_tok = local(tokens, half.at[0], sems.at[0])
    load_cot = local(cotangent, half.at[1], sems.at[1])
    load_tok.start()
    load_cot.start()
    pairs = ((w4_in, w4), (wk_in, wk), (wv_in, wv), (wg_in, wg))
    if gathers:
        gathers.begin()
    else:
        loads = [local(source, target, sems.at[2 + i]) for i, (source, target) in enumerate(pairs)]
        for copy in loads:
            copy.start()
    fill_mask(lengths, mask, length)
    load_tok.wait()
    widen(half.at[0], nat)
    if gathers:
        gathers.merge()
        gathers.vectors.step(1)

    @pl.loop(0, steps, unroll=2)
    def _(step):
        rows = take_step(nat, step, steps)
        mid[rows_at(step, SEG), :] = rows
        normed, scale = norm_rows(rows)
        norm[rows_at(step + 1, SEG), :] = normed
        rsd[0, rows_at(step, SEG), :] = jnp.broadcast_to(scale, (SEG, LANES))

    norm[0:SEG, :] = pltpu.roll(norm[length : length + SEG, :], 1, 0)
    save_n1 = local(norm, n1_out, sems.at[6])
    save_n1.start()
    if gathers:
        gathers.vectors.step(2)
        stage(1)
        gathers.vectors.step(3)
    load_cot.wait()
    widen(half.at[1], nat)
    if gathers:
        gathers.vectors.step(4)
        join_vectors(tiles, vec, share)

    @pl.loop(0, steps, unroll=2)
    def _(step):
        gain, bias = vec[0:1, :], vec[1:2, :]
        rows = rows_at(step, SEG)
        now = norm[rows_at(step + 1, SEG), :] * gain + bias
        before = (norm[rows, :] * gain + bias) * wide_of(mask[rows, :], width)
        change = now - before
        for q in range(3):
            half[2 + q, rows, :] = (before + vec[2 + q : 3 + q, :] * change).astype(BF16)

    save_mix = local(half.at[2:5], mix_out, sems.at[7])
    save_mix.start()
    stage(2)

    @pl.loop(0, steps, unroll=2)
    def _(step):
        half[0, rows_at(step, SEG), :] = take_step(nat, step, steps).astype(BF16)

    save_up = local(half.at[0], up_out, sems.at[13])
    save_up.start()
    stage(3)
    stage(4)

    if not gathers:
        for copy in loads:
            copy.wait()
    for q in (1, 2, 0):
        if q == 0:
            stage(5)

        @pl.loop(0, 2)
        def _(part):
            rows = rows_at(part, length // 2)
            pre = dot_nn(half[2 + q, rows, :], w4[:, :, :, q].reshape(width, width))
            if q == 0:
                pre = jax.nn.sigmoid(pre)
            if q == 1:
                put_rows(keys, rows, jnp.exp(pre))
            else:
                state[q // 2, rows, :] = pre

    rate = -jnp.exp(vec[5:6, :])
    fade = jnp.exp(rate)

    def first(step, carry):
        top, bottom, through = carry
        rows = rows_at(step, SEG)
        keep = mask[rows, :]
        factor = fade * wide_of(keep, width)
        key = take_rows(keys, rows)
        return factor * top + key * state[1, rows, :], factor * bottom + key, through * keep

    zero = jnp.zeros((SEG, width), F32)
    top, bottom, through = lax.fori_loop(0, steps, first, (zero, zero, jnp.ones((SEG, LANES), F32)), unroll=2)
    through = wide_of(through, width) * jnp.exp(rate * steps)
    top, bottom = join_runs((top, bottom), through, False)

    stage(6)

    def second(step, carry):
        top, bottom = carry
        rows = rows_at(step, SEG)
        keep = wide_of(mask[rows, :], width)
        top, bottom = top * keep, bottom * keep
        key = take_rows(keys, rows)
        key_value = key * state[1, rows, :]
        bonus = jnp.exp(vec[6:7, :])
        blended = (top + bonus * key_value) / (bottom + bonus * key)
        half[5, rows, :] = (state[0, rows, :] * blended).astype(BF16)
        state[2, rows, :] = top
        state[3, rows, :] = bottom
        return fade * top + key_value, fade * bottom + key

    lax.fori_loop(0, steps, second, (top, bottom), unroll=2)
    save_state = local(state, state_out, sems.at[8])
    save_state.start()
    save_key = local(keys, key_out, sems.at[18])
    save_key.start()
    save_att = local(half.at[5], att_out, sems.at[9])
    save_att.start()

    stage(7)

    @pl.loop(0, 2)
    def _(part):
        rows = rows_at(part, length // 2)
        mid[rows, :] += dot_nn(half[5, rows, :], w4[:, :, :, 3].reshape(width, width))

    stage(8)

    save_n1.wait()

    @pl.loop(0, steps, unroll=2)
    def _(step):
        rows = rows_at(step, SEG)
        normed, scale = norm_rows(mid[rows, :])
        norm[rows_at(step + 1, SEG), :] = normed
        rsd[1, rows, :] = jnp.broadcast_to(scale, (SEG, LANES))

    norm[0:SEG, :] = pltpu.roll(norm[length : length + SEG, :], 1, 0)
    save_n2 = local(norm, n2_out, sems.at[10])
    save_n2.start()
    save_r = local(rsd, r_out, sems.at[11])
    save_r.start()
    save_mix.wait()

    @pl.loop(0, steps, unroll=2)
    def _(step):
        gain, bias = vec[7:8, :], vec[8:9, :]
        rows = rows_at(step, SEG)
        now = norm[rows_at(step + 1, SEG), :] * gain + bias
        before = (norm[rows, :] * gain + bias) * wide_of(mask[rows, :], width)
        change = now - before
        for q in range(2):
            half[2 + q, rows, :] = (before + vec[9 + q : 10 + q, :] * change).astype(BF16)

    save_cig = local(half.at[2:4], cig_out, sems.at[12])
    save_cig.start()

    stage(9)

    for q in range(4):

        @pl.loop(0, 2)
        def _(part):
            rows = rows_at(part, length // 2)
            pre = jnp.maximum(dot_nn(half[2, rows, :], wk[:, :, :, q].reshape(width, width)), 0.0)
            sq[rows, q * width : (q + 1) * width] = (pre * pre).astype(BF16)

    save_sq = local(sq, sq_out, sems.at[14])
    save_sq.start()

    save_state.wait()

    @pl.loop(0, 2)
    def _(part):
        rows = rows_at(part, length // 2)
        state[0, rows, :] = jax.nn.sigmoid(dot_nn(half[3, rows, :], wg[...].reshape(width, width)))

    stage(10)
    stage(11)
    if gathers:
        saves = [
            local(source, target, sems.at[i])
            for source, target, i in (
                (w4, w4_out, 2), (wk, wk_out, 3), (wv, wv_out, 4), (wg, wg_out, 5), (vec, vec_out, 17)
            )
        ]
        for copy in saves:
            copy.start()

    @pl.loop(0, 2)
    def _(part):
        rows = rows_at(part, length // 2)
        state[1, rows, :] = dot_nn(sq[rows, :], wv[...].reshape(4 * width, width))

    save_att.wait()

    @pl.loop(0, steps, unroll=2)
    def _(step):
        rows = rows_at(step, SEG)
        gate, shrunk = state[0, rows, :], state[1, rows, :]
        upstream = half[0, rows, :].astype(F32)
        gated = gate * shrunk
        put_step(nat, step, steps, mid[rows, :] + gated)
        half[4, rows, :] = (upstream * gate).astype(BF16)
        half[5, rows, :] = (upstream * gated * (1.0 - gate)).astype(BF16)

    save_gsg = local(half.at[4:6], gsg_out, sems.at[15])
    save_gsg.start()
    narrow(nat, half.at[1])
    save_res = local(half.at[1], result, sems.at[16])
    save_res.start()
    for copy in (save_key, save_n2, save_r, save_cig, save_up, save_sq, save_gsg, save_res):
        copy.wait()
    if gathers:
        for copy in saves:
            copy.wait()
        gathers.finish()


def backward_kernel(direct, *refs):
    lengths, vec, w4_in, wk_in, wv_in, wg_in, n1_in, n2_in, r_in, mix_in, state_in, key_in = refs[:12]
    att_in, cig_in, sq_in, gsg_in, up_in, input_grad, vec_grad, g4_out, gk_out, gv_out, gg_out = refs[12:23]
    weights, big, keys, sq, half, mask, rsd, grad, grad_gate, sums, sems = refs[23:34]
    length, width = input_grad.shape
    steps = length // SEG
    n_buf, gm_buf, nb_buf, s_buf = 0, 1, 2, 3
    gate_buf, value_buf, top_buf, bottom_buf = 3, 4, 5, 6
    scatters = None
    if direct:
        total, first_y, first_x, second_in, third, s4, sk, sv, sg, a4, ak, av, ag, send, recv, free = refs[34:]
        scatters = Scatters(
            grad, grad_gate, {"4": g4_out, "k": gk_out, "v": gv_out, "g": gg_out},
            (total, first_y, first_x, second_in, third),
            {"4": s4, "k": sk, "v": sv, "g": sg}, {"4": a4, "k": ak, "v": av, "g": ag}, sums, send, recv, free,
        )

    def take(name, *steps_of):
        if scatters:
            for qs, number in steps_of:
                scatters.step(name, qs, number)

    def keep(source, target, sem):
        if not scatters:
            copy = local(source, target, sems.at[sem])
            copy.start()
            copy.wait()

    front, back = (0, 1), (2, 3)
    load_gsg = local(gsg_in, half.at[0:2], sems.at[0])
    load_sq = local(sq_in, sq, sems.at[1])
    load_wv = local(wv_in, weights, sems.at[2])
    load_cig = local(cig_in, half.at[2:4], sems.at[3])
    load_wg = local(wg_in, grad_gate, sems.at[5])
    load_n2 = local(n2_in, big.at[n_buf], sems.at[6])
    load_r2 = local(r_in.at[1], rsd, sems.at[7])
    for copy in (load_gsg, load_sq, load_wv, load_cig, load_wg, load_n2, load_r2):
        copy.start()
    if scatters:
        greet(scatters.place)
    fill_mask(lengths, mask, length)

    load_gsg.wait()
    load_sq.wait()

    @pl.loop(0, 4)
    def _(part):
        out = dot_tn(sq[:, rows_at(part, width)], half[0]).astype(BF16)
        grad[part] = out.reshape(2, 2, 4, 48, width)

    take("v", (front, 0), (back, 0))
    keep(grad, gv_out, 8)

    load_wv.wait()

    def expand_back(part):
        cols = rows_at(part, width)

        @pl.loop(0, 2)
        def _(number):
            rows = rows_at(number, length // 2)
            back_part = dot_nt(half[0, rows, :], weights[part].reshape(width, width))
            expanded = jnp.sqrt(sq[rows, cols].astype(F32))
            sq[rows, cols] = (2.0 * expanded * back_part).astype(BF16)

    pl.loop(0, 2)(expand_back)
    take("v", (front, 1))
    pl.loop(2, 4)(expand_back)
    load_wk = local(wk_in, weights, sems.at[4])
    load_wk.start()
    take("v", (back, 1))

    load_cig.wait()
    if scatters:
        for q in range(4):
            scatters.pieces["v", q].sent(0)

    def key_grad(q):
        grad[:, :, :, q] = dot_tn(half[2], sq[:, q * width : (q + 1) * width]).astype(BF16).reshape(4, 2, 2, 48, width)

    key_grad(0)
    key_grad(1)
    take("k", (front, 0))
    key_grad(2)
    key_grad(3)
    take("k", (back, 0))
    take("v", (front, 2))
    keep(grad, gk_out, 13)

    load_wg.wait()

    @pl.loop(0, 2)
    def _(part):
        rows = rows_at(part, length // 2)
        big[s_buf, rows, :] = dot_nt(half[1, rows, :], grad_gate[...].reshape(width, width))

    grad_gate[...] = dot_tn(half[3], half[1]).astype(BF16).reshape(4, 2, 2, 1, 48, width)
    take("g", ((0,), 0))
    take("k", (front, 1))
    keep(grad_gate, gg_out, 10)

    load_wk.wait()

    @pl.loop(0, 2)
    def _(part):
        rows = rows_at(part, length // 2)
        for q in range(4):
            out = dot_nt(sq[rows, q * width : (q + 1) * width], weights[:, :, :, q].reshape(width, width))
            big[gm_buf, rows, :] = out if q == 0 else big[gm_buf, rows, :] + out

    load_up = local(up_in, half.at[1], sems.at[11])
    load_up.start()
    load_w4 = local(w4_in, weights, sems.at[12])
    load_w4.start()
    load_att = local(att_in, sq.at[:, 0:width], sems.at[14])
    load_att.start()
    load_mix_key = local(mix_in.at[1:3], half.at[2:4], sems.at[9])
    load_mix_key.start()
    take("v", (back, 2))
    take("k", (back, 1))
    take("v", (front, 3))

    load_n2.wait()
    load_r2.wait()

    zero8 = jnp.zeros((8, width), F32)
    zero = jnp.zeros((SEG, width), F32)

    def fold(rows):
        return rows[0:8] + rows[8:16]

    def put_sum(row, value):
        sums[0, row : row + 1, :] = jnp.sum(value, axis=0, keepdims=True)

    def mix_two(step, carry):
        sum_channel, sum_gate = carry
        rows = rows_at(step, SEG)
        gain, bias = vec[7:8, :], vec[8:9, :]
        keep = wide_of(mask[rows, :], width)
        now = big[n_buf, rows_at(step + 1, SEG), :] * gain + bias
        before = (big[n_buf, rows, :] * gain + bias) * keep
        change = now - before
        in_channel, in_gate = big[gm_buf, rows, :], big[s_buf, rows, :]
        mix_channel, mix_gate = vec[9:10, :], vec[10:11, :]
        scaled = mix_channel * in_channel + mix_gate * in_gate
        big[gm_buf, rows, :] = scaled
        big[nb_buf, rows, :] = (in_channel + in_gate - scaled) * keep
        return sum_channel + fold(in_channel * change), sum_gate + fold(in_gate * change)

    sum_channel, sum_gate = lax.fori_loop(0, steps, mix_two, (zero8, zero8), unroll=2)
    put_sum(9, sum_channel)
    put_sum(10, sum_gate)
    big[nb_buf, length : length + SEG, :] = pltpu.roll(big[nb_buf, 0:SEG, :], SEG - 1, 0)
    load_up.wait()
    take("g", ((0,), 1))
    take("k", (front, 2))
    take("v", (back, 3))

    def norm_two(step, carry):
        sum_gain, sum_bias = carry
        rows = rows_at(step, SEG)
        normed = big[n_buf, rows_at(step + 1, SEG), :]
        incoming = big[gm_buf, rows, :] + big[nb_buf, rows_at(step + 1, SEG), :]
        scaled = incoming * vec[7:8, :]
        mean = jnp.mean(scaled, axis=-1, keepdims=True)
        along = jnp.mean(scaled * normed, axis=-1, keepdims=True)
        scale = wide_of(rsd[rows, :], width)
        out = half[1, rows, :].astype(F32) + scale * (scaled - mean - normed * along)
        big[gm_buf, rows, :] = out
        half[0, rows, :] = out.astype(BF16)
        return sum_gain + fold(incoming * normed), sum_bias + fold(incoming)

    sum_gain, sum_bias = lax.fori_loop(0, steps, norm_two, (zero8, zero8), unroll=2)
    put_sum(7, sum_gain)
    put_sum(8, sum_bias)
    load_n1 = local(n1_in, big.at[n_buf], sems.at[15])
    load_n1.start()
    load_state = local(state_in, big.at[3:7, 0:length], sems.at[16])
    load_state.start()
    load_key = local(key_in, keys, sems.at[17])
    load_key.start()
    load_r1 = local(r_in.at[0], rsd, sems.at[18])
    load_r1.start()
    load_mix = local(mix_in.at[0], half.at[1], sems.at[19])
    load_mix.start()
    if scatters:
        scatters.close("v", front)
    take("k", (back, 2))

    load_att.wait()
    load_w4.wait()
    if scatters:
        for q in range(4):
            scatters.pieces["k", q].sent(0)
    grad[:, :, :, 3] = dot_tn(sq[:, 0:width], half[0]).astype(BF16).reshape(4, 2, 2, 48, width)

    @pl.loop(0, 2)
    def _(part):
        rows = rows_at(part, length // 2)
        big[nb_buf, rows, :] = dot_nt(half[0, rows, :], weights[:, :, :, 3].reshape(width, width))

    take("g", ((0,), 2))
    take("k", (front, 3))
    if scatters:
        scatters.close("v", back)
        scatters.send_rows("v")

    rate = -jnp.exp(vec[5:6, :])
    fade = jnp.exp(rate)
    load_state.wait()
    load_key.wait()

    def first(index, carry):
        right, below, through = carry
        step = steps - 1 - index
        rows = rows_at(step, SEG)
        keep_column = mask[rows, :]
        keep = wide_of(keep_column, width)
        bonus = jnp.exp(vec[6:7, :])
        gate, key, value = big[gate_buf, rows, :], take_rows(keys, rows), big[value_buf, rows, :]
        own = bonus * key
        inverse = 1.0 / (big[bottom_buf, rows, :] + own)
        blended = (big[top_buf, rows, :] + own * value) * inverse
        incoming = big[nb_buf, rows, :] * gate
        sq[rows, width : 2 * width] = (incoming * blended * (1.0 - gate)).astype(BF16)
        weight = incoming * inverse
        big[nb_buf, rows, :] = weight
        big[gate_buf, rows, :] = blended
        right = keep * (weight + fade * right)
        below = keep * (weight * blended + fade * below)
        return right, below, through * keep_column

    right, below, through = lax.fori_loop(0, steps, first, (zero, zero, jnp.ones((SEG, LANES), F32)), unroll=2)
    through = wide_of(through, width) * jnp.exp(rate * steps)
    right, below = join_runs((right, below), through, True)
    take("k", (back, 3))
    take("g", ((0,), 3))
    if scatters:
        scatters.release()

    def second(index, carry):
        right, below, sum_decay, sum_bonus = carry
        step = steps - 1 - index
        rows = rows_at(step, SEG)
        keep = wide_of(mask[rows, :], width)
        bonus = jnp.exp(vec[6:7, :])
        weight, blended = big[nb_buf, rows, :], big[gate_buf, rows, :]
        key, value = take_rows(keys, rows), big[value_buf, rows, :]
        own = bonus * key * weight
        own_key = own * (value - blended)
        sq[rows, 2 * width : 3 * width] = (own_key + key * (right * value - below)).astype(BF16)
        sq[rows, 3 * width : 4 * width] = (own + key * right).astype(BF16)
        sum_bonus = sum_bonus + fold(own_key)
        sum_decay = sum_decay + fold(right * big[top_buf, rows, :] - below * big[bottom_buf, rows, :])
        right = keep * (weight + fade * right)
        below = keep * (weight * blended + fade * below)
        return right, below, sum_decay, sum_bonus

    _, _, sum_decay, sum_bonus = lax.fori_loop(0, steps, second, (right, below, zero8, zero8), unroll=2)
    sums[0, 5:6, :] = jnp.sum(sum_decay, axis=0, keepdims=True) * (rate * fade)
    put_sum(6, sum_bonus)

    load_mix.wait()
    load_mix_key.wait()
    if scatters:
        scatters.claim()
    for q in range(3):
        grad[:, :, :, q] = (
            dot_tn(half[1 + q], sq[:, (q + 1) * width : (q + 2) * width]).astype(BF16).reshape(4, 2, 2, 48, width)
        )
        if q == 1:
            take("4", (front, 0))
    take("4", (back, 0))
    keep(grad, g4_out, 13)
    if scatters:
        scatters.close("k", front)
    for q, place in enumerate((gate_buf, top_buf, bottom_buf)):

        @pl.loop(0, 2)
        def _(part):
            rows = rows_at(part, length // 2)
            big[place, rows, :] = dot_nt(
                sq[rows, (q + 1) * width : (q + 2) * width], weights[:, :, :, q].reshape(width, width)
            )

        if q == 0:
            take("4", (front, 1))
        if q == 1:
            take("4", (back, 1))
        if q == 2 and scatters:
            scatters.close("k", back)
            scatters.send_rows("k")

    load_n1.wait()
    load_r1.wait()

    def mix_one(step, carry):
        rows = rows_at(step, SEG)
        gain, bias = vec[0:1, :], vec[1:2, :]
        keep = wide_of(mask[rows, :], width)
        now = big[n_buf, rows_at(step + 1, SEG), :] * gain + bias
        before = (big[n_buf, rows, :] * gain + bias) * keep
        change = now - before
        out = []
        scaled, total = None, None
        for q, place in enumerate((gate_buf, top_buf, bottom_buf)):
            incoming = big[place, rows, :]
            part = vec[2 + q : 3 + q, :] * incoming
            scaled = part if scaled is None else scaled + part
            total = incoming if total is None else total + incoming
            out.append(carry[q] + fold(incoming * change))
        big[gate_buf, rows, :] = scaled
        big[nb_buf, rows, :] = (total - scaled) * keep
        return tuple(out)

    sum_mix = lax.fori_loop(0, steps, mix_one, (zero8, zero8, zero8), unroll=2)
    for q in range(3):
        put_sum(2 + q, sum_mix[q])
    big[nb_buf, length : length + SEG, :] = pltpu.roll(big[nb_buf, 0:SEG, :], SEG - 1, 0)
    if scatters:
        scatters.close("g", (0,))
        scatters.send_rows("g")
    take("4", (front, 2))

    def norm_one(step, carry):
        sum_gain, sum_bias = carry
        rows = rows_at(step, SEG)
        normed = big[n_buf, rows_at(step + 1, SEG), :]
        incoming = big[gate_buf, rows, :] + big[nb_buf, rows_at(step + 1, SEG), :]
        scaled = incoming * vec[0:1, :]
        mean = jnp.mean(scaled, axis=-1, keepdims=True)
        along = jnp.mean(scaled * normed, axis=-1, keepdims=True)
        scale = wide_of(rsd[rows, :], width)
        out = big[gm_buf, rows, :] + scale * (scaled - mean - normed * along)
        put_step(keys, step, steps, out)
        return sum_gain + fold(incoming * normed), sum_bias + fold(incoming)

    sum_gain, sum_bias = lax.fori_loop(0, steps, norm_one, (zero8, zero8), unroll=2)
    put_sum(0, sum_gain)
    put_sum(1, sum_bias)
    sums[0, 11:16, :] = jnp.zeros((5, width), F32)
    if scatters:
        scatters.hop(0)
    take("4", (back, 2))
    take("4", (front, 3))
    narrow(keys, half.at[0])
    save_in = local(half.at[0], input_grad, sems.at[20])
    save_in.start()
    if scatters:
        scatters.hop(1)
        scatters.take_rows("v")
        scatters.hop(2)
        scatters.take_rows("k")
        scatters.hop(3)
        scatters.take_rows("g")
        take("4", (back, 3))
        scatters.hop(4)
        vec_grad[...] = sums[3] + sums[7] + sums[8] + sums[9]
        scatters.close("4", front)
        scatters.close("4", back)
        scatters.send_rows("4")
        scatters.take_rows("4")
        scatters.finish()
    else:
        vec_grad[...] = sums[0]
    save_in.wait()


ANY = pl.BlockSpec(memory_space=pl.ANY)
SMEM = pl.BlockSpec(memory_space=pltpu.SMEM)
VMEM = pl.BlockSpec(memory_space=pltpu.VMEM)


def run_forward(lengths, tokens, cotangent, vec, w4, wk, wv, wg, share=None):
    length, width = tokens.shape
    shape = jax.ShapeDtypeStruct
    outs = (
        shape((length, width), BF16),
        shape((length + SEG, width), F32),
        shape((length + SEG, width), F32),
        shape((2, length, LANES), F32),
        shape((3, length, width), BF16),
        shape((4, length, width), F32),
        shape((width // LANES, length, LANES), F32),
        shape((length, width), BF16),
        shape((2, length, width), BF16),
        shape((length, 4 * width), BF16),
        shape((2, length, width), BF16),
        shape((length, width), BF16),
    )
    slabs, gate = (4, 2, 2, 4, 48, width), (4, 2, 2, 1, 48, width)
    scratch = [
        pltpu.VMEM(slabs, BF16),
        pltpu.VMEM(slabs, BF16),
        pltpu.VMEM(slabs, BF16),
        pltpu.VMEM(gate, BF16),
        pltpu.VMEM((width // LANES, length, LANES), F32),
        pltpu.VMEM((length + SEG, width), F32),
        pltpu.VMEM((length, width), F32),
        pltpu.VMEM((4, length, width), F32),
        pltpu.VMEM((width // LANES, length, LANES), F32),
        pltpu.VMEM((6, length, width), BF16),
        pltpu.VMEM((length, 4 * width), BF16),
        pltpu.VMEM((length, LANES), F32),
        pltpu.VMEM((2, length, LANES), F32),
        pltpu.SemaphoreType.DMA((19,)),
    ]
    in_specs = [SMEM, ANY, ANY, VMEM, ANY, ANY, ANY, ANY]
    params = {}
    if share:
        outs += (shape(slabs, BF16),) * 3 + (shape(gate, BF16), shape((16, width), F32))
        scratch += [pltpu.VMEM(part.shape[1:], BF16) for part in (w4, wk, wv, wg)]
        scratch += [
            pltpu.VMEM((4, 2, 2, 2, 16, LANES), F32),
            pltpu.VMEM((16, width), F32),
            pltpu.SemaphoreType.DMA((15, 6)),
            pltpu.SemaphoreType.DMA((15, 6)),
        ]
        in_specs = [SMEM, ANY, ANY, VMEM, VMEM, VMEM, VMEM, VMEM]
        params = dict(collective_id=0, has_side_effects=True)
    return pl.pallas_call(
        partial(forward_kernel, share),
        out_shape=outs,
        in_specs=in_specs,
        out_specs=[ANY] * len(outs),
        scratch_shapes=scratch,
        compiler_params=pltpu.CompilerParams(vmem_limit_bytes=VMEM_LIMIT, **params),
        name="forward",
    )(lengths, tokens, cotangent, vec, w4, wk, wv, wg)


def run_backward(lengths, vec, w4, wk, wv, wg, saved, direct):
    n1, n2, r, mix, state, keys, att, cig, sq, gsg, up = saved
    length, width = up.shape
    half = width // 2
    shape = jax.ShapeDtypeStruct
    slabs, gate = (4, 2, 2, 4, 48, width), (4, 2, 2, 1, 48, width)
    outs = (shape((length, width), BF16), shape((16, width), F32))
    out_specs = [ANY, VMEM]
    scratch = [
        pltpu.VMEM(slabs, BF16),
        pltpu.VMEM((7, length + SEG, width), F32),
        pltpu.VMEM((width // LANES, length, LANES), F32),
        pltpu.VMEM((length, 4 * width), BF16),
        pltpu.VMEM((4, length, width), BF16),
        pltpu.VMEM((length, LANES), F32),
        pltpu.VMEM((length, LANES), F32),
        pltpu.VMEM(slabs, BF16),
        pltpu.VMEM(gate, BF16),
        pltpu.VMEM((10, 16, width), F32),
        pltpu.SemaphoreType.DMA((21,)),
    ]
    params = {}
    if direct:
        rows = ((4, 24), (4, 24), (2, 48), (1, 24))
        outs += tuple(shape(part + (width,), F32) for part in rows)
        out_specs += [VMEM] * 4
        scratch += [
            pltpu.VMEM((9, 4, 2, 48, width), BF16),
            pltpu.VMEM((5, 4, 2, 48, half), BF16),
            pltpu.VMEM((4, 4, 48, width), BF16),
            pltpu.VMEM((9, 4, 48, half), BF16),
            pltpu.VMEM((9, 3, 48, half), BF16),
        ]
        scratch += [pltpu.VMEM(part + (half,), BF16) for part in rows] * 2
        scratch += [
            pltpu.SemaphoreType.DMA((15, 6)), pltpu.SemaphoreType.DMA((15, 6)), pltpu.SemaphoreType.REGULAR
        ]
        params = dict(collective_id=1, has_side_effects=True)
    else:
        outs += (shape(slabs, BF16),) * 3 + (shape(gate, BF16),)
        out_specs += [ANY] * 4
    return pl.pallas_call(
        partial(backward_kernel, direct),
        out_shape=outs,
        in_specs=[SMEM, VMEM] + [ANY] * 15,
        out_specs=out_specs,
        scratch_shapes=scratch,
        compiler_params=pltpu.CompilerParams(vmem_limit_bytes=VMEM_LIMIT, **params),
        name="backward",
    )(lengths, vec, w4, wk, wv, wg, n1, n2, r, mix, state, keys, att, cig, sq, gsg, up)


AXES = ("wide", "narrow")


def per_device(
    direct, tokens, lengths, cotangent, vectors,
    time_recept, time_key, time_value, time_output, channel_key, channel_value, channel_recept,
):
    _, length, width = tokens.shape
    slabs, gate = (4, 2, 2, 4, 48, width), (4, 2, 2, 1, 48, width)

    if direct:
        share = vectors.shape[1]

        def halves(parts, blocks, rows):
            return jnp.moveaxis(parts.reshape(blocks, rows, 2, width // 2), 2, 0)

        tile = jnp.pad(vectors.astype(F32), ((0, 5), (0, LANES - share)))
        times = jnp.stack([time_recept, time_key, time_value, time_output])
        key = jnp.swapaxes(channel_key.reshape(24, 4, width), 0, 1)
        out = run_forward(
            lengths, tokens[0], cotangent[0], tile,
            halves(times, 4, 24), halves(key, 4, 24), halves(channel_value, 2, 48), halves(channel_recept, 1, 24),
            share=share,
        )
        w4, wk, wv, wg, vec = out[12:]
    else:

        def whole(part, axis=0):
            return lax.all_gather(part, AXES, axis=axis, tiled=True)

        vec = jnp.pad(whole(vectors, 1).astype(F32), ((0, 5), (0, 0)))
        square = [whole(m).reshape(16, 48, width) for m in (time_recept, time_key, time_value, time_output)]
        w4 = jnp.stack(square, axis=1).reshape(slabs)
        wk = jnp.swapaxes(whole(channel_key).reshape(16, 48, 4, width), 1, 2).reshape(slabs)
        wv = whole(channel_value).reshape(slabs)
        wg = whole(channel_recept).reshape(gate)
        out = run_forward(lengths, tokens[0], cotangent[0], vec, w4, wk, wv, wg)
    input_grad, vec_grad, g4, gk, gv, gg = run_backward(lengths, vec, w4, wk, wv, wg, out[1:12], direct)
    if direct:
        place = lax.axis_index("wide") * 2 + lax.axis_index("narrow")
        return (
            out[0][None],
            input_grad[None],
            lax.dynamic_slice(vec_grad, (0, place * share), (vectors.shape[0], share)),
            *[g4[q].reshape(-1) for q in range(4)],
            jnp.swapaxes(gk, 0, 1).reshape(-1),
            gv.reshape(-1),
            gg.reshape(-1),
        )

    def owned(full, axis=0):
        return lax.psum_scatter(full.astype(F32), AXES, scatter_dimension=axis, tiled=True)

    return (
        out[0][None],
        input_grad[None],
        owned(vec_grad[:11], 1),
        *[owned(g4[:, :, :, q].reshape(-1)) for q in range(4)],
        owned(jnp.swapaxes(gk.reshape(16, 4, 48, width), 1, 2).reshape(-1)),
        owned(gv.reshape(-1)),
        owned(gg.reshape(-1)),
    )


def solution(mesh):
    both = P(AXES)
    rows = P(AXES, None, None)
    direct = dict(mesh.shape) == {"wide": 16, "narrow": 2}
    return jax.shard_map(
        partial(per_device, direct),
        mesh=mesh,
        in_specs=(rows, P(AXES, None), rows, P(None, AXES)) + (both,) * 7,
        out_specs=(rows, rows, P(None, AXES)) + (both,) * 7,
        check_vma=False,
    )
```

```python
from functools import partial

import jax
import jax.numpy as jnp
from jax import lax
from jax.experimental import pallas as pl
from jax.experimental.pallas import tpu as pltpu
from jax.sharding import PartitionSpec as P


SEG = 16
TAKE = 16
MIX = 4
UNROLL = 4
LANES = 128
EPS = 1e-05
F32 = jnp.float32
BF16 = jnp.bfloat16
VMEM_LIMIT = 63 * 1024 * 1024


def wide_of(column, width):
    return jnp.concatenate([column] * (width // LANES), axis=1)


def dot_nn(left, right):
    return jnp.dot(left, right, preferred_element_type=F32)


def dot_nt(left, right):
    return lax.dot_general(left, right, (((1,), (1,)), ((), ())), preferred_element_type=F32)


def dot_tn(left, right):
    return lax.dot_general(left, right, (((0,), (0,)), ((), ())), preferred_element_type=F32)


def local(source, target, sem):
    return pltpu.make_async_copy(source, target, sem)


def rows_at(index, size):
    return pl.ds(pl.multiple_of(index * size, size), size)


def rows_after(index, size):
    return pl.ds(pl.multiple_of(index * size + SEG, SEG), size)


def fold(rows):
    total = rows[0:8]
    for first in range(8, rows.shape[0], 8):
        total = total + rows[first : first + 8]
    return total


def fill_mask(lengths, mask, length):
    steps = length // SEG

    @pl.loop(0, length // 128)
    def _(block):
        row = block * 128 + lax.broadcasted_iota(jnp.int32, (128, LANES), 0)
        place = (row % SEG) * steps + row // SEG
        start = jnp.int32(0)
        fresh = place == 0
        for doc in range(lengths.shape[1] - 1):
            start = start + lengths[0, doc]
            fresh = jnp.logical_or(fresh, place == start)
        mask[rows_at(block, 128), :] = jnp.where(fresh, 0.0, 1.0)


def widen(source, target):
    @pl.loop(0, source.shape[0] // 32)
    def _(block):
        rows = rows_at(block, 32)
        for c in range(target.shape[0]):
            target[c, rows, :] = source[rows, c * LANES : (c + 1) * LANES].astype(F32)


def narrow(source, target):
    @pl.loop(0, target.shape[0] // 32)
    def _(block):
        rows = rows_at(block, 32)
        for c in range(source.shape[0]):
            target[rows, c * LANES : (c + 1) * LANES] = source[c, rows, :].astype(BF16)


def take_step(source, step, steps):
    strip = pl.ds(step, SEG, stride=steps)
    return jnp.concatenate([source[c, strip, :] for c in range(source.shape[0])], axis=1)


def put_step(target, step, steps, rows):
    strip = pl.ds(step, SEG, stride=steps)
    for c in range(target.shape[0]):
        target[c, strip, :] = rows[:, c * LANES : (c + 1) * LANES]


def take_rows(source, rows):
    return jnp.concatenate([source[c, rows, :] for c in range(source.shape[0])], axis=1)


def put_rows(target, rows, value):
    for c in range(target.shape[0]):
        target[c, rows, :] = value[:, c * LANES : (c + 1) * LANES]


def norm_rows(rows):
    centred = rows - jnp.mean(rows, axis=-1, keepdims=True)
    scale = lax.rsqrt(jnp.mean(centred * centred, axis=-1, keepdims=True) + EPS)
    return centred * scale, scale


def join_runs(local_end, through, backward):
    index = lax.broadcasted_iota(jnp.int32, local_end[0].shape, 0)
    if backward:
        index = SEG - 1 - index
    states = list(local_end)
    hop = 1
    while hop < SEG:
        turn = SEG - hop if backward else hop
        inside = index >= hop
        moved = pltpu.roll(through, turn, 0)
        states = [jnp.where(inside, s + through * pltpu.roll(s, turn, 0), s) for s in states]
        through = jnp.where(inside, through * moved, through)
        hop *= 2
    turn = SEG - 1 if backward else 1
    return [jnp.where(index >= 1, pltpu.roll(s, turn, 0), 0.0) for s in states]


FORWARD = (
    0, 100, 500, 1, 2, 101, 501, 200, 300, 400, 800, 900, 600, 700, 3, 4, 502, 201, 301, 1400, 1000, 1100, 1300,
    1200, 801, 401, 1500, 1800, 1600, 1700, 1401, 503, 1101, 1801, 901, 504, 1701, 5, 802, 601, 1702, 902, 701, 602,
    1001, 803, 1301, 804, 903, 702, 8, 1201, 904, 1302, 1501, 603, 1601, 604, 703, 1002, 6, 704, 7, 1402, 1502,
    1202, 9, 1602, 10, 1303, 11, 1102, 12, 1003, 1304, 13, 1403, 19, 1004, 1802, 16, 1404, 1203, 14, 1503, 1204, 18,
    1504, 1103, 20, 1104, 1603, 17, 1703, 1604, 1803, 21, 1704, 22, 1804, 23, 15,
)
BACKWARD = (
    0, 13, 200, 12, 100, 15, 201, 400, 14, 101, 300, 17, 401, 18, 301, 22, 202, 1100, 21, 102, 1000, 16, 1101, 20,
    900, 1001, 19, 203, 103, 402, 23, 901, 1200, 1, 2, 104, 403, 302, 1201, 1300, 24, 25, 1301, 26, 902, 404, 1102,
    27, 303, 3, 4, 204, 304, 1202, 1002, 1400, 1800, 5, 903, 800, 6, 1801, 7, 801, 1302, 1203, 8, 1103, 30, 700, 29,
    600, 802, 1003, 28, 701, 904, 1204, 601, 500, 32, 803, 33, 1004, 501, 31, 1303, 9, 602, 702, 1104, 1700, 10,
    804, 502, 1500, 1304, 703, 1900, 11, 1501, 1701, 1901, 603, 503, 1502, 604, 704, 1503, 504, 1600, 1601, 1504,
)


class Place:
    def __init__(self):
        index = lax.axis_index("wide")
        self.z, self.x, self.c = index // 4, index // 2 % 2, index % 2
        self.y = lax.axis_index("narrow")

    def at(self, z=None, x=None, c=None, y=None):
        z, x = self.z if z is None else z, self.x if x is None else x
        c, y = self.c if c is None else c, self.y if y is None else y
        return (z * 4 + x * 2 + c, y)

    def along_z(self, hop):
        return (self.z + hop) % 4

    def partners(self):
        return [self.at(z=self.along_z(hop)) for hop in (1, 2, 3)] + [
            self.at(x=1 - self.x), self.at(y=1 - self.y), self.at(c=1 - self.c)
        ]


def greet(place):
    barrier = pltpu.get_barrier_semaphore()
    for partner in place.partners():
        pl.semaphore_signal(barrier, inc=1, device_id=partner, device_id_type=pl.DeviceIdType.MESH)


def greeted(place):
    pl.semaphore_wait(pltpu.get_barrier_semaphore(), len(place.partners()))


def remote(source, target, send, recv, device):
    return pltpu.make_async_remote_copy(
        src_ref=source, dst_ref=target, send_sem=send, recv_sem=recv,
        device_id=device, device_id_type=pl.DeviceIdType.MESH,
    )


class Gather:
    def __init__(self, place, piece, half_cols, order, send, recv):
        every = slice(None)
        p, held, number = place, {"z": place.z, "x": place.x, "y": half_cols}, 0
        self.phases = []
        for axis in order + "c":
            ref = piece(held["z"], held["x"], p.c, held["y"])
            if axis == "z":
                targets = [p.at(z=p.along_z(hop)) for hop in (1, 2, 3)]
            else:
                targets = [{"x": p.at(x=1 - p.x), "y": p.at(y=1 - p.y), "c": p.at(c=1 - p.c)}[axis]]
            copies = []
            for target in targets:
                copies.append(remote(ref, ref, send.at[number], recv.at[number], target))
                number += 1
            self.phases.append(copies)
            held[axis] = every

    def step(self, phase):
        if phase:
            for copy in self.phases[phase - 1]:
                copy.wait_recv()
        if phase < len(self.phases):
            for copy in self.phases[phase]:
                copy.start()

    def finish(self):
        for copies in self.phases:
            for copy in copies:
                copy.wait_send()


def join_vectors(tiles, vec, share):
    width = vec.shape[1]
    lane = lax.broadcasted_iota(jnp.int32, (16, LANES), 1)
    blocks = [jnp.zeros((16, LANES), F32) for _ in range(width // LANES)]
    for index in range(width // share):
        z, x, c, y = index // 8, index // 4 % 2, index // 2 % 2, index % 2
        block, shift = index * share // LANES, index * share % LANES
        tile = tiles[z, x, c, y]
        tile = pltpu.roll(tile, shift, 1) if shift else tile
        if shift + share > LANES:
            blocks[block] += jnp.where(lane >= shift, tile, 0.0)
            blocks[block + 1] += jnp.where(lane < shift, tile, 0.0)
        else:
            blocks[block] += tile
    for block, tile in enumerate(blocks):
        vec[:, block * LANES : (block + 1) * LANES] = tile


class Gathers:
    WAYS = ("zxy", "zyx", "zxy", "zyx", "zyx", "yzx", "zyx", "zxy", "xzy", "zxy", "zxy", "yxz", "yzx")
    BLOCKS = {"4": (0, 4), "k": (4, 4), "g": (8, 1), "v": (9, 4)}

    def __init__(self, raw, weights, scratch, share, send, recv):
        self.place = place = Place()
        self.raw, self.weights, self.share = raw, weights, share
        self.flat, self.blocks, self.stages, self.tiles, self.vec = scratch
        tiles = self.tiles
        half = weights["4"].shape[-1] // 2
        self.cols = pl.ds(pl.multiple_of(place.y * half, half), half)
        self.halves = {}
        for i, (name, (first, count)) in enumerate(self.BLOCKS.items()):
            span = pl.ds(first, count)
            self.halves[name] = remote(
                self.blocks.at[1 - place.y, span], self.stages.at[span], send.at[0, i], recv.at[0, i],
                place.at(y=1 - place.y),
            )
        self.vectors = Gather(
            place, lambda z, x, c, y: tiles.at[z, x, c, y], place.y, "zxy", send.at[1], recv.at[1]
        )
        self.pieces, number = [self.vectors], 2
        for name, (_, count) in self.BLOCKS.items():
            for q in range(count):

                def piece(z, x, c, cols, ref=weights[name], q=q):
                    return ref.at[z, x, c, q, :, cols]

                order = self.WAYS[number - 2]
                self.pieces.append(Gather(place, piece, self.cols, order, send.at[number], recv.at[number]))
                number += 1

    def begin(self):
        place = self.place
        vectors = self.raw["vectors"]
        tile = self.tiles.at[place.z, place.x, place.c, place.y]
        tile[...] = jnp.zeros(tile.shape, F32)
        tile[0 : vectors.shape[0], 0 : self.share] = vectors[...].astype(F32)
        self.split("recept", 0)
        self.split("key", 1)
        self.split("value", 2)
        self.split("output", 3)
        greeted(place)
        half = self.blocks.shape[-1]
        for q in range(4):
            for h in range(2):
                self.blocks[h, 4 + q] = self.raw["expand"][q, :, h * half : (h + 1) * half]
        self.split("gate", 8)
        self.split("shrink", 9)

    def split(self, name, block):
        raw, flat = self.raw[name], self.flat
        rows = self.blocks.shape[2]
        across = flat.shape[0] // rows
        for part in range(raw.shape[0] // flat.shape[0]):
            flat[...] = raw[part * flat.shape[0] : (part + 1) * flat.shape[0], :].astype(F32)
            strips = [flat[pl.ds(j, rows, stride=across), :] for j in range(across)]
            for h in range(2):
                own = strips[h * across // 2 : (h + 1) * across // 2]
                self.blocks[h, block + part] = jnp.concatenate(own, axis=1).astype(BF16)

    def do(self, number, step):
        if number < 4:
            name = "4kgv"[number]
            if step:
                self.merge(name)
            else:
                self.halves[name].start()
            return
        self.pieces[number - 4].step(step)
        if number == 4 and step == 4:
            join_vectors(self.tiles, self.vec, self.share)

    def merge(self, name):
        place, y = self.place, self.place.y
        self.halves[name].wait_recv()
        slab = self.weights[name].at[place.z, place.x, place.c]
        first, count = self.BLOCKS[name]
        mine = [self.blocks[y, first + q].astype(F32) for q in range(count)]
        theirs = [self.stages[first + q].astype(F32) for q in range(count)]
        for q in range(count):
            if name == "v":
                pair = (mine if q < 2 else theirs)[q % 2 * 2 : q % 2 * 2 + 2]
                slab[(2 * y + q) % 4, :, self.cols] = jnp.concatenate(pair, axis=0).astype(BF16)
            else:
                upper, lower = jnp.where(y == 0, mine[q], theirs[q]), jnp.where(y == 0, theirs[q], mine[q])
                slab[q, :, self.cols] = jnp.concatenate([upper, lower], axis=0).astype(BF16)

    def finish(self):
        for copy in self.halves.values():
            copy.wait_send()
        for piece in self.pieces:
            piece.finish()


class Scatter:
    def __init__(self, place, cols, grad, total, arrivals, order, send, recv):
        p, (mine, other), every = place, cols, slice(None)
        self.place, self.mine, self.grad, self.total = place, mine, grad, total
        self.order, self.arrivals = order, arrivals
        self.copies = [[remote(grad.at[:, :, 1 - p.c], total, send.at[0], recv.at[0], p.at(c=1 - p.c))]]
        held, number = {"z": every, "x": every, "y": every}, 1
        for axis, ref in zip(order, arrivals):
            ways = {
                "z": [(p.along_z(hop), ref.at[hop - 1], p.at(z=p.along_z(hop))) for hop in (1, 2, 3)],
                "x": [(1 - p.x, ref, p.at(x=1 - p.x))],
                "y": [(other, ref, p.at(y=1 - p.y))],
            }[axis]
            copies = []
            for place_of, target, device in ways:
                at = {**held, axis: place_of}
                copies.append(
                    remote(total.at[at["z"], at["x"], :, at["y"]], target, send.at[number], recv.at[number], device)
                )
                number += 1
            self.copies.append(copies)
            held[axis] = {"z": p.z, "x": p.x, "y": mine}[axis]

    def sent(self, *phases):
        for phase in phases:
            for copy in self.copies[phase]:
                copy.wait_send()

    def step(self, number):
        if number:
            for copy in self.copies[number - 1]:
                copy.wait_recv()
        if number == 1:

            @pl.loop(0, 4)
            def _(z):
                for x in range(2):
                    self.total[z, x] += self.grad[z, x, self.place.c]

        if number in (2, 3):
            self.add(number - 2)
        if number < 4:
            for copy in self.copies[number]:
                copy.start()

    def add(self, index):
        p, total, ref, past = self.place, self.total, self.arrivals[index], self.order[: index + 1]
        cols = self.mine if "y" in past else slice(None)

        def rows(z):
            for x in (p.x,) if "x" in past else (0, 1):
                lead = (() if "z" in past else (z,)) + (() if "x" in past else (x,))
                if past[-1] == "z":
                    value = total[z, x, :, cols].astype(F32)
                    for hop in range(3):
                        value += ref[(hop,) + lead].astype(F32)
                    total[z, x, :, cols] = value.astype(BF16)
                else:
                    total[z, x, :, cols] += ref[lead if lead else ...]

        if "z" in past:
            rows(p.z)
        else:
            pl.loop(0, 4)(rows)

    def result(self):
        p, ref = self.place, self.arrivals[2]
        value = self.total[p.z, p.x, :, self.mine].astype(F32)
        if self.order[2] == "z":
            for hop in range(3):
                value += ref[hop].astype(F32)
        else:
            value += ref[...].astype(F32)
        return value


def arrival_shapes(order, width):
    shape, out = {"z": 4, "x": 2, "y": width}, []
    for axis in order:
        shape[axis] = width // 2 if axis == "y" else 1
        lead = tuple(n for n in (shape["z"], shape["x"]) if n > 1)
        out.append(((3,) if axis == "z" else ()) + lead + (48, shape["y"]))
    return out


class Scatters:
    SLOTS = {"v": (0, 1, 2, 3), "4": (0, 1, 2, 3), "k": (4, 5, 6, 7), "g": (8,)}
    WAYS = ("yxz", "xzy", "yxz", "yxz", "xyz", "yzx", "yxz", "xzy", "xzy")

    def __init__(self, grad, grad_gate, outs, total, arrivals, finals, arrived, sums, send, recv, free):
        self.place = place = Place()
        self.outs, self.finals, self.arrived, self.sums, self.free = outs, finals, arrived, sums, free
        half = grad.shape[-1] // 2
        mine = pl.ds(pl.multiple_of(place.y * half, half), half)
        other = pl.ds(pl.multiple_of((1 - place.y) * half, half), half)
        self.mine, self.other = mine, other
        self.pieces, number, self.claimed, self.greeted = {}, 0, False, False
        for name, slots in self.SLOTS.items():
            source = grad_gate if name == "g" else grad
            for q, slot in enumerate(slots):
                self.pieces[name, q] = Scatter(
                    place, (mine, other), source.at[:, :, :, q], total.at[slot], arrivals[3 * slot : 3 * slot + 3],
                    self.WAYS[slot], send.at[number], recv.at[number],
                )
                number += 1
        self.last = {
            name: remote(finals[name], arrived[name], send.at[number, i], recv.at[number, i], place.at(y=1 - place.y))
            for i, name in enumerate("4kvg")
        }
        number += 1
        to = [place.at(c=1 - place.c), place.at(y=1 - place.y), place.at(x=1 - place.x)]
        self.hops = [
            [remote(sums.at[i], sums.at[4 + i], send.at[number, i], recv.at[number, i], device)]
            for i, device in enumerate(to)
        ]
        self.hops.append([
            remote(sums.at[3], sums.at[6 + hop], send.at[number, 2 + hop], recv.at[number, 2 + hop],
                   place.at(z=place.along_z(hop)))
            for hop in (1, 2, 3)
        ])

    def do(self, number, step):
        if not self.greeted:
            self.greeted = True
            greeted(self.place)
        names = list(self.pieces)
        if number >= len(names):
            number -= len(names)
            if number == 0:
                self.release()
            elif number == 1:
                self.hop(step)
            else:
                name = "4kvg"[number - 2]
                self.take_rows(name) if step else self.send_rows(name)
            return
        name, q = names[number]
        if name == "4" and not self.claimed:
            self.claimed = True
            pl.semaphore_wait(self.free, 6)
        self.pieces[name, q].step(step)
        if step == 4:
            self.close(name, q)

    def put(self, name, q, half, value):
        out = self.outs[name]
        if name == "k":
            half_cols = value.shape[1]
            out[q, :, pl.ds(pl.multiple_of(half * half_cols, half_cols), half_cols)] = value
            return
        if name == "v":
            flat, first = out, q * value.shape[0]
        else:
            flat, first = out[q], 0
        strips = value.shape[1] // LANES
        across = 2 * strips
        for j in range(strips):
            rows = pl.ds(first * across + half * strips + j, value.shape[0], stride=across)
            flat[rows, :] = value[:, j * LANES : (j + 1) * LANES]

    def close(self, name, q):
        y, total = self.place.y, self.pieces[name, q].result()
        if name == "v":

            @pl.when(y == q // 2)
            def _():
                self.put(name, q % 2, y, total)

            @pl.when(y != q // 2)
            def _():
                self.finals[name][q % 2] = total.astype(BF16)
        else:
            half = total.shape[0] // 2
            upper, lower = total[:half], total[half:]
            self.put(name, q, y, jnp.where(y == 0, upper, lower))
            self.finals[name][q] = jnp.where(y == 0, lower, upper).astype(BF16)

    def send_rows(self, name):
        self.last[name].start()

    def take_rows(self, name):
        self.last[name].wait_recv()
        for q in range(self.arrived[name].shape[0]):
            self.put(name, q, 1 - self.place.y, self.arrived[name][q].astype(F32))

    def release(self):
        for q in range(4):
            self.pieces["v", q].sent(1, 2, 3)
        for partner in self.place.partners():
            pl.semaphore_signal(self.free, inc=1, device_id=partner, device_id_type=pl.DeviceIdType.MESH)

    def hop(self, number):
        if number:
            for copy in self.hops[number - 1]:
                copy.wait_recv()
        if 1 <= number <= 3:
            self.sums[number] = self.sums[number - 1] + self.sums[3 + number]
        if number < 4:
            for copy in self.hops[number]:
                copy.start()

    def finish(self):
        for (name, _), piece in self.pieces.items():
            if name == "v":
                continue
            piece.sent(1, 2, 3)
            if name != "k":
                piece.sent(0)
        for copy in self.last.values():
            copy.wait_send()
        for copies in self.hops:
            for copy in copies:
                copy.wait_send()


def forward_kernel(share, *refs):
    lengths, tokens, cotangent = refs[:3]
    length, width = tokens.shape
    steps = length // SEG
    names = ("vectors", "recept", "key", "value", "output", "expand", "shrink", "gate")
    inputs = 11 if share else 8
    result, n1_out, n2_out, r_out, mix_out, state_out, key_out, att_out, cig_out, sq_out, gsg_out, up_out = refs[
        inputs : inputs + 12
    ]
    rest = refs[inputs + 12 :]
    gathers = None
    if share:
        w4_out, wk_out, wv_out, wg_out, vec_out = rest[:5]
        rest = rest[5:]
    w4, wk, wv, wg, nat, norm, mid, state, keys, half, sq, mask, rsd, sems = rest[:14]
    if share:
        gathers = Gathers(
            dict(zip(names, refs[3:11])), {"4": w4, "k": wk, "v": wv, "g": wg}, rest[14:19], share, *rest[19:]
        )
        vec = gathers.vec
    else:
        vec = refs[3]

    load_tok = local(tokens, half.at[0], sems.at[0])
    load_cot = local(cotangent, half.at[1], sems.at[1])
    load_tok.start()
    load_cot.start()
    save_n1 = local(norm, n1_out, sems.at[6])
    save_mix = local(half.at[2:5], mix_out, sems.at[7])
    save_state = local(state, state_out, sems.at[8])
    save_att = local(half.at[5], att_out, sems.at[9])
    save_n2 = local(norm, n2_out, sems.at[10])
    save_r = local(rsd, r_out, sems.at[11])
    save_cig = local(half.at[2:4], cig_out, sems.at[12])
    save_up = local(half.at[0], up_out, sems.at[13])
    save_sq = local(sq, sq_out, sems.at[14])
    save_gsg = local(half.at[4:6], gsg_out, sems.at[15])
    save_res = local(half.at[1], result, sems.at[16])
    save_key = local(keys, key_out, sems.at[18])
    late = [save_key, save_n2, save_r, save_cig, save_up, save_sq, save_gsg, save_res]
    if gathers:
        save_w4, save_wk = local(w4, w4_out, sems.at[2]), local(wk, wk_out, sems.at[3])
        save_wv, save_wg = local(wv, wv_out, sems.at[4]), local(wg, wg_out, sems.at[5])
        save_vec = local(vec, vec_out, sems.at[17])
        late += [save_w4, save_wk, save_wv, save_wg, save_vec]
    two = length // 2
    carried = {}

    def keep(*copies):
        if gathers:
            for copy in copies:
                copy.start()

    def start():
        if gathers:
            greet(gathers.place)
        fill_mask(lengths, mask, length)
        if gathers:
            gathers.begin()
        else:
            loads = [local(one, other, sems.at[2 + i]) for i, (one, other) in enumerate(zip(refs[4:8], (w4, wk, wv, wg)))]
            for copy in loads:
                copy.start()
            for copy in loads:
                copy.wait()

    def tok():
        load_tok.wait()
        widen(half.at[0], nat)

    def first_norm():
        @pl.loop(0, steps // TAKE)
        def _(block):
            values = jnp.concatenate([take_step(nat, block * TAKE + i, steps) for i in range(TAKE)], axis=0)
            rows = rows_at(block, TAKE * SEG)
            normed, scale = norm_rows(values)
            mid[rows, :] = values
            norm[rows_after(block, TAKE * SEG), :] = normed
            rsd[0, rows, :] = jnp.broadcast_to(scale, (TAKE * SEG, LANES))

        norm[0:SEG, :] = pltpu.roll(norm[length : length + SEG, :], 1, 0)
        save_n1.start()

    def mix(gain_row, mix_row, count):
        @pl.loop(0, steps // MIX)
        def _(block):
            gain, bias = vec[gain_row : gain_row + 1, :], vec[gain_row + 1 : gain_row + 2, :]
            rows = rows_at(block, MIX * SEG)
            now = norm[rows_after(block, MIX * SEG), :] * gain + bias
            before = (norm[rows, :] * gain + bias) * wide_of(mask[rows, :], width)
            change = now - before
            for q in range(count):
                half[2 + q, rows, :] = (before + vec[mix_row + q : mix_row + q + 1, :] * change).astype(BF16)

    def first_mix():
        mix(0, 2, 3)
        save_mix.start()

    def cot():
        load_cot.wait()
        widen(half.at[1], nat)

    def upstream():
        @pl.loop(0, steps // TAKE)
        def _(block):
            values = jnp.concatenate([take_step(nat, block * TAKE + i, steps) for i in range(TAKE)], axis=0)
            half[0, rows_at(block, TAKE * SEG), :] = values.astype(BF16)

        save_up.start()

    def product(q):
        @pl.loop(0, 2)
        def _(part):
            rows = rows_at(part, two)
            pre = dot_nn(half[2 + q, rows, :], w4[:, :, :, q].reshape(width, width))
            if q == 0:
                state[0, rows, :] = jax.nn.sigmoid(pre)
            if q == 1:
                put_rows(keys, rows, jnp.exp(pre))
            if q == 2:
                state[1, rows, :] = pre

    def first_scan():
        rate = -jnp.exp(vec[5:6, :])
        fade = jnp.exp(rate)

        def first(step, carry):
            top, bottom, through = carry
            rows = rows_at(step, SEG)
            keep = mask[rows, :]
            factor = fade * wide_of(keep, width)
            key = take_rows(keys, rows)
            return factor * top + key * state[1, rows, :], factor * bottom + key, through * keep

        zero = jnp.zeros((SEG, width), F32)
        ones = jnp.ones((SEG, LANES), F32)
        top, bottom, through = lax.fori_loop(0, steps, first, (zero, zero, ones), unroll=UNROLL)
        through = wide_of(through, width) * jnp.exp(rate * steps)
        carried["sums"] = join_runs((top, bottom), through, False)
        carried["fade"] = fade

    def second_scan():
        fade = carried["fade"]

        def second(step, carry):
            top, bottom = carry
            rows = rows_at(step, SEG)
            keep = wide_of(mask[rows, :], width)
            top, bottom = top * keep, bottom * keep
            key = take_rows(keys, rows)
            key_value = key * state[1, rows, :]
            bonus = jnp.exp(vec[6:7, :])
            blended = (top + bonus * key_value) / (bottom + bonus * key)
            half[5, rows, :] = (state[0, rows, :] * blended).astype(BF16)
            state[2, rows, :] = top
            state[3, rows, :] = bottom
            return fade * top + key_value, fade * bottom + key

        lax.fori_loop(0, steps, second, tuple(carried["sums"]), unroll=UNROLL)
        save_state.start()
        save_key.start()
        save_att.start()

    def middle():
        @pl.loop(0, 2)
        def _(part):
            rows = rows_at(part, two)
            mid[rows, :] += dot_nn(half[5, rows, :], w4[:, :, :, 3].reshape(width, width))

        keep(*([save_w4, save_vec] if gathers else []))

    def second_norm():
        save_n1.wait()

        @pl.loop(0, steps // TAKE)
        def _(block):
            rows = rows_at(block, TAKE * SEG)
            normed, scale = norm_rows(mid[rows, :])
            norm[rows_after(block, TAKE * SEG), :] = normed
            rsd[1, rows, :] = jnp.broadcast_to(scale, (TAKE * SEG, LANES))

        norm[0:SEG, :] = pltpu.roll(norm[length : length + SEG, :], 1, 0)
        save_n2.start()
        save_r.start()

    def second_mix():
        save_mix.wait()
        mix(7, 9, 2)
        save_cig.start()

    def expanded(q):
        @pl.loop(0, 2)
        def _(part):
            rows = rows_at(part, two)
            pre = jnp.maximum(dot_nn(half[2, rows, :], wk[:, :, :, q].reshape(width, width)), 0.0)
            sq[rows, q * width : (q + 1) * width] = (pre * pre).astype(BF16)

        carried["blocks"] = carried.get("blocks", 0) + 1
        if carried["blocks"] == 4:
            save_sq.start()
            keep(*([save_wk] if gathers else []))

    def gate():
        save_state.wait()

        @pl.loop(0, 2)
        def _(part):
            rows = rows_at(part, two)
            state[0, rows, :] = jax.nn.sigmoid(dot_nn(half[3, rows, :], wg[...].reshape(width, width)))

        keep(*([save_wg] if gathers else []))

    def shrunk(q):
        @pl.loop(0, 2)
        def _(part):
            rows = rows_at(part, two)
            out = dot_nn(sq[rows, q * width : (q + 1) * width], wv[:, :, :, q].reshape(width, width))
            state[1, rows, :] = state[1, rows, :] + out if q else out

    def final():
        keep(*([save_wv] if gathers else []))
        save_att.wait()

        @pl.loop(0, steps // TAKE)
        def _(block):
            rows = rows_at(block, TAKE * SEG)
            gate_value, shrunk_value = state[0, rows, :], state[1, rows, :]
            incoming = half[0, rows, :].astype(F32)
            gated = gate_value * shrunk_value
            out = mid[rows, :] + gated
            for i in range(TAKE):
                put_step(nat, block * TAKE + i, steps, out[i * SEG : (i + 1) * SEG])
            half[4, rows, :] = (incoming * gate_value).astype(BF16)
            half[5, rows, :] = (incoming * gated * (1.0 - gate_value)).astype(BF16)

        save_gsg.start()
        narrow(nat, half.at[1])
        save_res.start()

    work = [
        start, tok, first_norm, cot, upstream, first_mix, partial(product, 0), partial(product, 1), partial(product, 2),
        first_scan, second_scan, middle, second_norm, second_mix, gate, final,
    ]
    work += [partial(expanded, q) for q in range(4)] + [partial(shrunk, q) for q in range(4)]
    for item in FORWARD:
        if item < 100:
            work[item]()
        elif gathers:
            gathers.do(item // 100 - 1, item % 100)
    for copy in late:
        copy.wait()
    if gathers:
        gathers.finish()


def backward_kernel(direct, *refs):
    lengths, vec, w4_in, wk_in, wv_in, wg_in, n1_in, n2_in, r_in, mix_in, state_in, key_in = refs[:12]
    att_in, cig_in, sq_in, gsg_in, up_in, input_grad, vec_grad = refs[12:19]
    g4_out, gk_out, gv_out, gg_out = (refs[19:23], *refs[23:26]) if direct else refs[19:23]
    rest = refs[26:] if direct else refs[23:]
    weights, big, keys, sq, half, mask, rsd, grad, grad_gate, sums, sems = rest[:11]
    rest = rest[11:]
    length, width = input_grad.shape
    steps = length // SEG
    n_buf, gm_buf, nb_buf, s_buf = 0, 1, 2, 3
    gate_buf, value_buf, top_buf, bottom_buf = 3, 4, 5, 6
    scatters = None
    if direct:
        total, arrivals, rest = rest[0], rest[1:28], rest[28:]
        scatters = Scatters(
            grad, grad_gate, {"4": g4_out, "k": gk_out, "v": gv_out, "g": [gg_out]}, total, arrivals,
            dict(zip("4kvg", rest[:4])), dict(zip("4kvg", rest[4:8])), sums, *rest[8:],
        )

    def keep(source, target, *q):
        if not scatters:
            place = (slice(None),) * 3 + q
            copy = local(source.at[place], target.at[place], sems.at[8])
            copy.start()
            copy.wait()

    load_gsg = local(gsg_in, half.at[0:2], sems.at[0])
    load_sq = [
        local(sq_in.at[:, q * width : (q + 1) * width], sq.at[:, q * width : (q + 1) * width], sems.at[19 + q])
        for q in range(4)
    ]
    load_wv = local(wv_in, weights, sems.at[2])
    load_cig = local(cig_in, half.at[2:4], sems.at[3])
    load_wk = local(wk_in, weights, sems.at[4])
    load_wg = local(wg_in, grad_gate, sems.at[5])
    load_n2 = local(n2_in, big.at[n_buf], sems.at[6])
    load_r2 = local(r_in.at[1], rsd, sems.at[7])
    load_up = local(up_in, half.at[0], sems.at[9])
    load_w4 = local(w4_in, weights, sems.at[10])
    load_att = local(att_in, sq.at[:, 0:width], sems.at[11])
    load_n1 = local(n1_in, big.at[n_buf], sems.at[12])
    load_gate = local(state_in.at[0], big.at[gate_buf, 0:length], sems.at[13])
    load_state = local(state_in.at[1:4], big.at[value_buf : bottom_buf + 1, 0:length], sems.at[14])
    load_key = local(key_in, keys, sems.at[15])
    load_r1 = local(r_in.at[0], rsd, sems.at[16])
    load_mix = local(mix_in, half.at[1:4], sems.at[17])
    save_in = local(half.at[0], input_grad, sems.at[18])
    for copy in (load_gsg, *[load_sq[q] for q in (1, 0, 3, 2)], load_wv, load_cig, load_wg, load_n2, load_r2, load_state, load_key):
        copy.start()
    two = length // 2
    zero8 = jnp.zeros((8, width), F32)
    zero = jnp.zeros((SEG, width), F32)
    carried = {}

    def put_sum(row, value):
        sums[0, row : row + 1, :] = jnp.sum(value, axis=0, keepdims=True)

    def columns(block):
        return slice(block * width, (block + 1) * width)

    def slabs(product):
        return product.astype(BF16).reshape(4, 2, 2, 48, width)

    def start():
        if scatters:
            greet(scatters.place)
        fill_mask(lengths, mask, length)
        load_gsg.wait()

    def value_grad(q):
        load_sq[q].wait()
        grad[:, :, :, q] = slabs(dot_tn(sq[:, columns(q)], half[0]))
        keep(grad, gv_out, q)

    def expand_back(q):
        if "wv" not in carried:
            carried["wv"] = 0
            load_wv.wait()
        carried["wv"] += 1

        @pl.loop(0, 2)
        def _(part):
            rows = rows_at(part, two)
            back = dot_nt(half[0, rows, :], weights[:, :, :, q].reshape(width, width))
            expanded = jnp.sqrt(sq[rows, columns(q)].astype(F32))
            sq[rows, columns(q)] = (2.0 * expanded * back).astype(BF16)

        if carried["wv"] == 4:
            load_wk.start()
            load_up.start()

    def wait_channel():
        if "cig" not in carried:
            carried["cig"] = True
            load_cig.wait()

    def key_grad(q):
        wait_channel()
        if scatters:
            scatters.pieces["v", q].sent(0)
        grad[:, :, :, q] = slabs(dot_tn(half[2], sq[:, columns(q)]))
        keep(grad, gk_out, q)

    def gate_in():
        load_wg.wait()

        @pl.loop(0, 2)
        def _(part):
            rows = rows_at(part, two)
            big[s_buf, rows, :] = dot_nt(half[1, rows, :], grad_gate[...].reshape(width, width))

    def gate_grad():
        wait_channel()
        grad_gate[...] = slabs(dot_tn(half[3], half[1])).reshape(grad_gate.shape)
        keep(grad_gate, gg_out)

    def channel_in(q):
        if q == 0:
            load_wk.wait()

        @pl.loop(0, 2)
        def _(part):
            rows = rows_at(part, two)
            out = dot_nt(sq[rows, columns(q)], weights[:, :, :, q].reshape(width, width))
            big[gm_buf, rows, :] = out if q == 0 else big[gm_buf, rows, :] + out

        if q == 3:
            load_w4.start()

    def second_mix():
        load_n2.wait()
        load_r2.wait()

        def mix_two(block, carry):
            sum_channel, sum_gate = carry
            rows, after = rows_at(block, MIX * SEG), rows_after(block, MIX * SEG)
            gain, bias = vec[7:8, :], vec[8:9, :]
            keep = wide_of(mask[rows, :], width)
            now = big[n_buf, after, :] * gain + bias
            before = (big[n_buf, rows, :] * gain + bias) * keep
            change = now - before
            in_channel, in_gate = big[gm_buf, rows, :], big[s_buf, rows, :]
            mix_channel, mix_gate = vec[9:10, :], vec[10:11, :]
            scaled = mix_channel * in_channel + mix_gate * in_gate
            big[gm_buf, rows, :] = scaled
            big[nb_buf, rows, :] = (in_channel + in_gate - scaled) * keep
            return sum_channel + fold(in_channel * change), sum_gate + fold(in_gate * change)

        sum_channel, sum_gate = lax.fori_loop(0, steps // MIX, mix_two, (zero8, zero8))
        load_gate.start()
        load_att.start()
        put_sum(9, sum_channel)
        put_sum(10, sum_gate)
        big[nb_buf, length : length + SEG, :] = pltpu.roll(big[nb_buf, 0:SEG, :], SEG - 1, 0)

    def second_norm():
        load_up.wait()

        def norm_two(block, carry):
            sum_gain, sum_bias = carry
            rows, after = rows_at(block, TAKE * SEG), rows_after(block, TAKE * SEG)
            normed = big[n_buf, after, :]
            incoming = big[gm_buf, rows, :] + big[nb_buf, after, :]
            scaled = incoming * vec[7:8, :]
            mean = jnp.mean(scaled, axis=-1, keepdims=True)
            along = jnp.mean(scaled * normed, axis=-1, keepdims=True)
            scale = wide_of(rsd[rows, :], width)
            out = half[0, rows, :].astype(F32) + scale * (scaled - mean - normed * along)
            big[gm_buf, rows, :] = out
            half[0, rows, :] = out.astype(BF16)
            return sum_gain + fold(incoming * normed), sum_bias + fold(incoming)

        sum_gain, sum_bias = lax.fori_loop(0, steps // TAKE, norm_two, (zero8, zero8))
        put_sum(7, sum_gain)
        put_sum(8, sum_bias)
        load_n1.start()
        load_r1.start()

    def output_grad():
        if scatters:
            scatters.pieces["k", 3].sent(0)
        load_att.wait()
        grad[:, :, :, 3] = slabs(dot_tn(sq[:, columns(0)], half[0]))
        keep(grad, g4_out, 3)

    def attended_back():
        load_w4.wait()

        @pl.loop(0, 2)
        def _(part):
            rows = rows_at(part, two)
            big[nb_buf, rows, :] = dot_nt(half[0, rows, :], weights[:, :, :, 3].reshape(width, width))

    def first_scan():
        load_mix.start()
        rate = -jnp.exp(vec[5:6, :])
        fade = jnp.exp(rate)
        load_gate.wait()
        load_state.wait()
        load_key.wait()

        def first(index, carry):
            right, below, through = carry
            step = steps - 1 - index
            rows = rows_at(step, SEG)
            keep_column = mask[rows, :]
            keep = wide_of(keep_column, width)
            bonus = jnp.exp(vec[6:7, :])
            gate, key, value = big[gate_buf, rows, :], take_rows(keys, rows), big[value_buf, rows, :]
            own = bonus * key
            inverse = 1.0 / (big[bottom_buf, rows, :] + own)
            blended = (big[top_buf, rows, :] + own * value) * inverse
            incoming = big[nb_buf, rows, :] * gate
            sq[rows, width : 2 * width] = (incoming * blended * (1.0 - gate)).astype(BF16)
            weight = incoming * inverse
            big[nb_buf, rows, :] = weight
            big[gate_buf, rows, :] = blended
            right = keep * (weight + fade * right)
            below = keep * (weight * blended + fade * below)
            return right, below, through * keep_column

        ones = jnp.ones((SEG, LANES), F32)
        right, below, through = lax.fori_loop(0, steps, first, (zero, zero, ones), unroll=UNROLL)
        through = wide_of(through, width) * jnp.exp(rate * steps)
        carried["sums"] = join_runs((right, below), through, True)
        carried["rate"], carried["fade"] = rate, fade

    def second_scan():
        rate, fade = carried["rate"], carried["fade"]

        def second(index, carry):
            right, below, sum_decay, sum_bonus = carry
            step = steps - 1 - index
            rows = rows_at(step, SEG)
            keep = wide_of(mask[rows, :], width)
            bonus = jnp.exp(vec[6:7, :])
            weight, blended = big[nb_buf, rows, :], big[gate_buf, rows, :]
            key, value = take_rows(keys, rows), big[value_buf, rows, :]
            own = bonus * key * weight
            own_key = own * (value - blended)
            sq[rows, 2 * width : 3 * width] = (own_key + key * (right * value - below)).astype(BF16)
            sq[rows, 3 * width : 4 * width] = (own + key * right).astype(BF16)
            sum_bonus = sum_bonus + fold(own_key)
            sum_decay = sum_decay + fold(right * big[top_buf, rows, :] - below * big[bottom_buf, rows, :])
            right = keep * (weight + fade * right)
            below = keep * (weight * blended + fade * below)
            return right, below, sum_decay, sum_bonus

        carry = (*carried["sums"], zero8, zero8)
        _, _, sum_decay, sum_bonus = lax.fori_loop(0, steps, second, carry, unroll=UNROLL)
        sums[0, 5:6, :] = jnp.sum(sum_decay, axis=0, keepdims=True) * (rate * fade)
        put_sum(6, sum_bonus)

    def time_grad(q):
        if "mix" not in carried:
            carried["mix"] = True
            load_mix.wait()
        if scatters:
            scatters.pieces["k", q].sent(0)
        grad[:, :, :, q] = slabs(dot_tn(half[1 + q], sq[:, columns(1 + q)]))
        keep(grad, g4_out, q)

    mixed_bufs = (gate_buf, top_buf, bottom_buf)

    def time_back(q):
        @pl.loop(0, 2)
        def _(part):
            rows = rows_at(part, two)
            big[mixed_bufs[q], rows, :] = dot_nt(sq[rows, columns(1 + q)], weights[:, :, :, q].reshape(width, width))

    def first_mix():
        load_n1.wait()
        load_r1.wait()

        def mix_one(block, carry):
            rows, after = rows_at(block, MIX * SEG), rows_after(block, MIX * SEG)
            gain, bias = vec[0:1, :], vec[1:2, :]
            keep = wide_of(mask[rows, :], width)
            now = big[n_buf, after, :] * gain + bias
            before = (big[n_buf, rows, :] * gain + bias) * keep
            change = now - before
            out = []
            scaled, total = None, None
            for q, place in enumerate(mixed_bufs):
                incoming = big[place, rows, :]
                part = vec[2 + q : 3 + q, :] * incoming
                scaled = part if scaled is None else scaled + part
                total = incoming if total is None else total + incoming
                out.append(carry[q] + fold(incoming * change))
            big[gate_buf, rows, :] = scaled
            big[nb_buf, rows, :] = (total - scaled) * keep
            return tuple(out)

        sum_mix = lax.fori_loop(0, steps // MIX, mix_one, (zero8, zero8, zero8))
        for q in range(3):
            put_sum(2 + q, sum_mix[q])
        big[nb_buf, length : length + SEG, :] = pltpu.roll(big[nb_buf, 0:SEG, :], SEG - 1, 0)

    def first_norm():
        def norm_one(block, carry):
            sum_gain, sum_bias = carry
            rows, after = rows_at(block, TAKE * SEG), rows_after(block, TAKE * SEG)
            normed = big[n_buf, after, :]
            incoming = big[gate_buf, rows, :] + big[nb_buf, after, :]
            scaled = incoming * vec[0:1, :]
            mean = jnp.mean(scaled, axis=-1, keepdims=True)
            along = jnp.mean(scaled * normed, axis=-1, keepdims=True)
            scale = wide_of(rsd[rows, :], width)
            out = big[gm_buf, rows, :] + scale * (scaled - mean - normed * along)
            for i in range(TAKE):
                put_step(keys, block * TAKE + i, steps, out[i * SEG : (i + 1) * SEG])
            return sum_gain + fold(incoming * normed), sum_bias + fold(incoming)

        sum_gain, sum_bias = lax.fori_loop(0, steps // TAKE, norm_one, (zero8, zero8))
        put_sum(0, sum_gain)
        put_sum(1, sum_bias)
        sums[0, 11:16, :] = jnp.zeros((5, width), F32)

    def final():
        narrow(keys, half.at[0])
        save_in.start()

    work = [
        start, gate_in, gate_grad, second_mix, second_norm, output_grad, attended_back, first_scan, second_scan, first_mix,
        first_norm, final,
    ]
    for function, count in (
        (value_grad, 4), (expand_back, 4), (key_grad, 4), (channel_in, 4), (time_grad, 3), (time_back, 3)
    ):
        work += [partial(function, q) for q in range(count)]
    for item in BACKWARD:
        if item < 100:
            work[item]()
        elif scatters:
            scatters.do(item // 100 - 1, item % 100)
    if scatters:
        vec_grad[...] = sums[3] + sums[7] + sums[8] + sums[9]
        scatters.finish()
    else:
        vec_grad[...] = sums[0]
    save_in.wait()


ANY = pl.BlockSpec(memory_space=pl.ANY)
SMEM = pl.BlockSpec(memory_space=pltpu.SMEM)
VMEM = pl.BlockSpec(memory_space=pltpu.VMEM)


def run_forward(lengths, tokens, cotangent, parameters, share=None):
    length, width = tokens.shape
    shape = jax.ShapeDtypeStruct
    outs = (
        shape((length, width), BF16),
        shape((length + SEG, width), F32),
        shape((length + SEG, width), F32),
        shape((2, length, LANES), F32),
        shape((3, length, width), BF16),
        shape((4, length, width), F32),
        shape((width // LANES, length, LANES), F32),
        shape((length, width), BF16),
        shape((2, length, width), BF16),
        shape((length, 4 * width), BF16),
        shape((2, length, width), BF16),
        shape((length, width), BF16),
    )
    slabs, gate = (4, 2, 2, 4, 48, width), (4, 2, 2, 1, 48, width)
    scratch = [
        pltpu.VMEM(slabs, BF16),
        pltpu.VMEM(slabs, BF16),
        pltpu.VMEM(slabs, BF16),
        pltpu.VMEM(gate, BF16),
        pltpu.VMEM((width // LANES, length, LANES), F32),
        pltpu.VMEM((length + SEG, width), F32),
        pltpu.VMEM((length, width), F32),
        pltpu.VMEM((4, length, width), F32),
        pltpu.VMEM((width // LANES, length, LANES), F32),
        pltpu.VMEM((6, length, width), BF16),
        pltpu.VMEM((length, 4 * width), BF16),
        pltpu.VMEM((length, LANES), F32),
        pltpu.VMEM((2, length, LANES), F32),
        pltpu.SemaphoreType.DMA((19,)),
    ]
    in_specs = [SMEM, ANY, ANY, VMEM, ANY, ANY, ANY, ANY]
    params = {}
    if share:
        outs += (shape(slabs, BF16),) * 3 + (shape(gate, BF16), shape((16, width), F32))
        scratch += [
            pltpu.VMEM((24 * width // LANES, LANES), F32),
            pltpu.VMEM((2, 13, 24, width // 2), BF16),
            pltpu.VMEM((13, 24, width // 2), BF16),
            pltpu.VMEM((4, 2, 2, 2, 16, LANES), F32),
            pltpu.VMEM((16, width), F32),
            pltpu.SemaphoreType.DMA((15, 6)),
            pltpu.SemaphoreType.DMA((15, 6)),
        ]
        in_specs = [SMEM, ANY, ANY] + [VMEM] * 8
        params = dict(collective_id=0, has_side_effects=True)
    return pl.pallas_call(
        partial(forward_kernel, share),
        out_shape=outs,
        in_specs=in_specs,
        out_specs=[ANY] * len(outs),
        scratch_shapes=scratch,
        compiler_params=pltpu.CompilerParams(vmem_limit_bytes=VMEM_LIMIT, **params),
        name="forward",
    )(lengths, tokens, cotangent, *parameters)


def run_backward(lengths, vec, w4, wk, wv, wg, saved, direct):
    n1, n2, r, mix, state, keys, att, cig, sq, gsg, up = saved
    length, width = up.shape
    half = width // 2
    shape = jax.ShapeDtypeStruct
    slabs, gate = (4, 2, 2, 4, 48, width), (4, 2, 2, 1, 48, width)
    outs = (shape((length, width), BF16), shape((16, width), F32))
    out_specs = [ANY, VMEM]
    scratch = [
        pltpu.VMEM(slabs, BF16),
        pltpu.VMEM((7, length + SEG, width), F32),
        pltpu.VMEM((width // LANES, length, LANES), F32),
        pltpu.VMEM((length, 4 * width), BF16),
        pltpu.VMEM((4, length, width), BF16),
        pltpu.VMEM((length, LANES), F32),
        pltpu.VMEM((length, LANES), F32),
        pltpu.VMEM(slabs, BF16),
        pltpu.VMEM(gate, BF16),
        pltpu.VMEM((10, 16, width), F32),
        pltpu.SemaphoreType.DMA((23,)),
    ]
    params = {}
    if direct:
        rows = ((4, 24), (4, 24), (2, 48), (1, 24))
        lines = 24 * width // LANES
        outs += (shape((lines, LANES), F32),) * 4 + (
            shape((4, 24, width), F32), shape((4 * lines, LANES), F32), shape((lines, LANES), F32)
        )
        out_specs += [VMEM] * 7
        scratch += [pltpu.VMEM((9, 4, 2, 48, width), BF16)]
        scratch += [pltpu.VMEM(part, BF16) for way in Scatters.WAYS for part in arrival_shapes(way, width)]
        scratch += [pltpu.VMEM(part + (half,), BF16) for part in rows] * 2
        scratch += [
            pltpu.SemaphoreType.DMA((15, 6)), pltpu.SemaphoreType.DMA((15, 6)), pltpu.SemaphoreType.REGULAR
        ]
        params = dict(collective_id=1, has_side_effects=True)
    else:
        outs += (shape(slabs, BF16),) * 3 + (shape(gate, BF16),)
        out_specs += [ANY] * 4
    return pl.pallas_call(
        partial(backward_kernel, direct),
        out_shape=outs,
        in_specs=[SMEM, VMEM] + [ANY] * 15,
        out_specs=out_specs,
        scratch_shapes=scratch,
        compiler_params=pltpu.CompilerParams(vmem_limit_bytes=VMEM_LIMIT, **params),
        name="backward",
    )(lengths, vec, w4, wk, wv, wg, n1, n2, r, mix, state, keys, att, cig, sq, gsg, up)


AXES = ("wide", "narrow")


def per_device(
    direct, tokens, lengths, cotangent, vectors,
    time_recept, time_key, time_value, time_output, channel_key, channel_value, channel_recept,
):
    _, length, width = tokens.shape
    slabs, gate = (4, 2, 2, 4, 48, width), (4, 2, 2, 1, 48, width)

    if direct:
        share = vectors.shape[1]
        key = channel_key.reshape(24, 16, 4, 48).transpose(2, 0, 1, 3).reshape(4, 24, width)
        flat = [m.reshape(-1, LANES) for m in (time_recept, time_key, time_value, time_output, channel_value, channel_recept)]
        out = run_forward(
            lengths, tokens[0], cotangent[0], (vectors, *flat[:4], key, flat[4], flat[5]), share=share
        )
        w4, wk, wv, wg, vec = out[12:]
    else:

        def whole(part, axis=0):
            return lax.all_gather(part, AXES, axis=axis, tiled=True)

        vec = jnp.pad(whole(vectors, 1).astype(F32), ((0, 5), (0, 0)))
        square = [whole(m).reshape(16, 48, width) for m in (time_recept, time_key, time_value, time_output)]
        w4 = jnp.stack(square, axis=1).reshape(slabs)
        wk = whole(channel_key).reshape(16, 48, 16, 4, 48).transpose(0, 3, 1, 2, 4).reshape(slabs)
        wv = whole(channel_value).reshape(slabs)
        wg = whole(channel_recept).reshape(gate)
        out = run_forward(lengths, tokens[0], cotangent[0], (vec, w4, wk, wv, wg))
    input_grad, vec_grad, *grads = run_backward(lengths, vec, w4, wk, wv, wg, out[1:12], direct)
    if direct:
        place = lax.axis_index("wide") * 2 + lax.axis_index("narrow")
        gk, gv, gg = grads[4:]
        return (
            out[0][None],
            input_grad[None],
            lax.dynamic_slice(vec_grad, (0, place * share), (vectors.shape[0], share)),
            *[g.reshape(-1) for g in grads[:4]],
            gk.reshape(4, 24, 16, 48).transpose(1, 2, 0, 3).reshape(-1),
            gv.reshape(-1),
            gg.reshape(-1),
        )
    g4, gk, gv, gg = grads

    def owned(full, axis=0):
        return lax.psum_scatter(full.astype(F32), AXES, scatter_dimension=axis, tiled=True)

    return (
        out[0][None],
        input_grad[None],
        owned(vec_grad[:11], 1),
        *[owned(g4[:, :, :, q].reshape(-1)) for q in range(4)],
        owned(gk.reshape(16, 4, 48, 16, 48).transpose(0, 2, 3, 1, 4).reshape(-1)),
        owned(gv.reshape(-1)),
        owned(gg.reshape(-1)),
    )


def solution(mesh):
    both = P(AXES)
    rows = P(AXES, None, None)
    direct = dict(mesh.shape) == {"wide": 16, "narrow": 2}
    return jax.shard_map(
        partial(per_device, direct),
        mesh=mesh,
        in_specs=(rows, P(AXES, None), rows, P(None, AXES)) + (both,) * 7,
        out_specs=(rows, rows, P(None, AXES)) + (both,) * 7,
        check_vma=False,
    )
```

```python
from functools import partial

import jax
import jax.numpy as jnp
from jax import lax
from jax.experimental import pallas as pl
from jax.experimental.pallas import tpu as pltpu
from jax.sharding import PartitionSpec as P


SEG = 16
TAKE = 16
MIX = 4
UNROLL = 4
LANES = 128
EPS = 1e-05
F32 = jnp.float32
BF16 = jnp.bfloat16
VMEM_LIMIT = 63 * 1024 * 1024


def wide_of(column, width):
    return jnp.concatenate([column] * (width // LANES), axis=1)


def dot_nn(left, right):
    return jnp.dot(left, right, preferred_element_type=F32)


def dot_nt(left, right):
    return lax.dot_general(left, right, (((1,), (1,)), ((), ())), preferred_element_type=F32)


def dot_tn(left, right):
    return lax.dot_general(left, right, (((0,), (0,)), ((), ())), preferred_element_type=F32)


def local(source, target, sem):
    return pltpu.make_async_copy(source, target, sem)


def rows_at(index, size):
    return pl.ds(pl.multiple_of(index * size, size), size)


def rows_after(index, size):
    return pl.ds(pl.multiple_of(index * size + SEG, SEG), size)


def fold(rows):
    total = rows[0:8]
    for first in range(8, rows.shape[0], 8):
        total = total + rows[first : first + 8]
    return total


def fill_mask(lengths, mask, length):
    steps = length // SEG

    @pl.loop(0, length // 128)
    def _(block):
        row = block * 128 + lax.broadcasted_iota(jnp.int32, (128, LANES), 0)
        place = (row % SEG) * steps + row // SEG
        start = jnp.int32(0)
        fresh = place == 0
        for doc in range(lengths.shape[1] - 1):
            start = start + lengths[0, doc]
            fresh = jnp.logical_or(fresh, place == start)
        mask[rows_at(block, 128), :] = jnp.where(fresh, 0.0, 1.0)


def widen(source, target):
    @pl.loop(0, source.shape[0] // 32)
    def _(block):
        rows = rows_at(block, 32)
        for c in range(target.shape[0]):
            target[c, rows, :] = source[rows, c * LANES : (c + 1) * LANES].astype(F32)


def narrow(source, target):
    @pl.loop(0, target.shape[0] // 32)
    def _(block):
        rows = rows_at(block, 32)
        for c in range(source.shape[0]):
            target[rows, c * LANES : (c + 1) * LANES] = source[c, rows, :].astype(BF16)


def take_step(source, step, steps):
    strip = pl.ds(step, SEG, stride=steps)
    return jnp.concatenate([source[c, strip, :] for c in range(source.shape[0])], axis=1)


def put_step(target, step, steps, rows):
    strip = pl.ds(step, SEG, stride=steps)
    for c in range(target.shape[0]):
        target[c, strip, :] = rows[:, c * LANES : (c + 1) * LANES]


def take_rows(source, rows):
    return jnp.concatenate([source[c, rows, :] for c in range(source.shape[0])], axis=1)


def put_rows(target, rows, value):
    for c in range(target.shape[0]):
        target[c, rows, :] = value[:, c * LANES : (c + 1) * LANES]


def norm_rows(rows):
    centred = rows - jnp.mean(rows, axis=-1, keepdims=True)
    scale = lax.rsqrt(jnp.mean(centred * centred, axis=-1, keepdims=True) + EPS)
    return centred * scale, scale


def join_runs(local_end, through, backward):
    index = lax.broadcasted_iota(jnp.int32, local_end[0].shape, 0)
    if backward:
        index = SEG - 1 - index
    states = list(local_end)
    hop = 1
    while hop < SEG:
        turn = SEG - hop if backward else hop
        inside = index >= hop
        moved = pltpu.roll(through, turn, 0)
        states = [jnp.where(inside, s + through * pltpu.roll(s, turn, 0), s) for s in states]
        through = jnp.where(inside, through * moved, through)
        hop *= 2
    turn = SEG - 1 if backward else 1
    return [jnp.where(index >= 1, pltpu.roll(s, turn, 0), 0.0) for s in states]


FORWARD = (
    0, 100, 500, 1, 2, 101, 501, 200, 300, 400, 900, 600, 800, 700, 3, 4, 502, 201, 301, 1300, 1000, 1100, 1400,
    1200, 901, 401, 1500, 1700, 1600, 1800, 1301, 503, 1201, 601, 1601, 504, 1801, 5, 902, 801, 1302, 602, 701, 802,
    1001, 903, 1101, 904, 603, 702, 1401, 604, 6, 1501, 1102, 803, 1701, 804, 8, 1002, 703, 1502, 1402, 1202, 704,
    7, 1702, 9, 10, 1103, 1602, 11, 1003, 12, 1104, 1403, 13, 1004, 1802, 16, 1503, 1404, 17, 14, 1504, 1203, 20,
    1603, 1204, 18, 1703, 1604, 21, 1303, 1704, 1803, 22, 1304, 19, 1804, 23, 15,
)
BACKWARD = (
    0, 13, 200, 12, 100, 15, 400, 201, 19, 101, 14, 401, 300, 17, 1, 301, 2, 202, 1300, 18, 102, 16, 1301, 20, 402,
    900, 23, 1200, 302, 21, 1000, 203, 103, 901, 22, 1201, 1100, 24, 1001, 303, 1302, 25, 403, 204, 1101, 26, 104,
    27, 1202, 3, 404, 902, 304, 1400, 1800, 4, 1203, 5, 1002, 800, 1801, 6, 1303, 7, 1003, 801, 8, 903, 1102, 1304,
    1900, 30, 700, 1204, 29, 600, 802, 1004, 28, 701, 904, 500, 1103, 1901, 601, 33, 32, 501, 31, 803, 9, 702, 1104,
    602, 1700, 10, 1500, 11, 703, 1501, 502, 804, 1701, 603, 1502, 503, 604, 704, 1503, 504, 1600, 1601, 1504,
)


class Place:
    def __init__(self):
        index = lax.axis_index("wide")
        self.z, self.x, self.c = index // 4, index // 2 % 2, index % 2
        self.y = lax.axis_index("narrow")

    def at(self, z=None, x=None, c=None, y=None):
        z, x = self.z if z is None else z, self.x if x is None else x
        c, y = self.c if c is None else c, self.y if y is None else y
        return (z * 4 + x * 2 + c, y)

    def along_z(self, hop):
        return (self.z + hop) % 4

    def partners(self):
        return [self.at(z=self.along_z(hop)) for hop in (1, 2, 3)] + [
            self.at(x=1 - self.x), self.at(y=1 - self.y), self.at(c=1 - self.c)
        ]


def greet(place):
    barrier = pltpu.get_barrier_semaphore()
    for partner in place.partners():
        pl.semaphore_signal(barrier, inc=1, device_id=partner, device_id_type=pl.DeviceIdType.MESH)


def greeted(place):
    pl.semaphore_wait(pltpu.get_barrier_semaphore(), len(place.partners()))


def remote(source, target, send, recv, device):
    return pltpu.make_async_remote_copy(
        src_ref=source, dst_ref=target, send_sem=send, recv_sem=recv,
        device_id=device, device_id_type=pl.DeviceIdType.MESH,
    )


class Gather:
    def __init__(self, place, piece, half_cols, order, send, recv):
        every = slice(None)
        p, held, number = place, {"z": place.z, "x": place.x, "y": half_cols}, 0
        self.phases = []
        for axis in order + "c":
            ref = piece(held["z"], held["x"], p.c, held["y"])
            if axis == "z":
                targets = [p.at(z=p.along_z(hop)) for hop in (1, 2, 3)]
            else:
                targets = [{"x": p.at(x=1 - p.x), "y": p.at(y=1 - p.y), "c": p.at(c=1 - p.c)}[axis]]
            copies = []
            for target in targets:
                copies.append(remote(ref, ref, send.at[number], recv.at[number], target))
                number += 1
            self.phases.append(copies)
            held[axis] = every

    def step(self, phase):
        if phase:
            for copy in self.phases[phase - 1]:
                copy.wait_recv()
        if phase < len(self.phases):
            for copy in self.phases[phase]:
                copy.start()

    def finish(self):
        for copies in self.phases:
            for copy in copies:
                copy.wait_send()


def join_vectors(tiles, vec, share):
    width = vec.shape[1]
    lane = lax.broadcasted_iota(jnp.int32, (16, LANES), 1)
    blocks = [jnp.zeros((16, LANES), F32) for _ in range(width // LANES)]
    for index in range(width // share):
        z, x, c, y = index // 8, index // 4 % 2, index // 2 % 2, index % 2
        block, shift = index * share // LANES, index * share % LANES
        tile = tiles[z, x, c, y]
        tile = pltpu.roll(tile, shift, 1) if shift else tile
        if shift + share > LANES:
            blocks[block] += jnp.where(lane >= shift, tile, 0.0)
            blocks[block + 1] += jnp.where(lane < shift, tile, 0.0)
        else:
            blocks[block] += tile
    for block, tile in enumerate(blocks):
        vec[:, block * LANES : (block + 1) * LANES] = tile


class Gathers:
    WAYS = ("zxy", "zxy", "zyx", "zyx", "zxy", "zyx", "yzx", "xyz", "zyx", "zxy", "xzy", "zyx", "xzy")
    BLOCKS = {"4": (0, 4), "k": (4, 4), "g": (8, 1), "v": (9, 4)}

    def __init__(self, raw, weights, scratch, share, send, recv):
        self.place = place = Place()
        self.raw, self.weights, self.share = raw, weights, share
        self.flat, self.blocks, self.stages, self.tiles, self.vec = scratch
        tiles = self.tiles
        half = weights["4"].shape[-1] // 2
        self.cols = pl.ds(pl.multiple_of(place.y * half, half), half)
        self.halves = {}
        for i, (name, (first, count)) in enumerate(self.BLOCKS.items()):
            span = pl.ds(first, count)
            self.halves[name] = remote(
                self.blocks.at[1 - place.y, span], self.stages.at[span], send.at[0, i], recv.at[0, i],
                place.at(y=1 - place.y),
            )
        self.vectors = Gather(
            place, lambda z, x, c, y: tiles.at[z, x, c, y], place.y, "zxy", send.at[1], recv.at[1]
        )
        self.pieces, number = [self.vectors], 2
        for name, (_, count) in self.BLOCKS.items():
            for q in range(count):

                def piece(z, x, c, cols, ref=weights[name], q=q):
                    return ref.at[z, x, c, q, :, cols]

                order = self.WAYS[number - 2]
                self.pieces.append(Gather(place, piece, self.cols, order, send.at[number], recv.at[number]))
                number += 1

    def begin(self):
        place = self.place
        vectors = self.raw["vectors"]
        tile = self.tiles.at[place.z, place.x, place.c, place.y]
        tile[...] = jnp.zeros(tile.shape, F32)
        tile[0 : vectors.shape[0], 0 : self.share] = vectors[...].astype(F32)
        self.split("recept", 0)
        self.split("key", 1)
        self.split("value", 2)
        self.split("output", 3)
        greeted(place)
        half = self.blocks.shape[-1]
        for q in range(4):
            for h in range(2):
                self.blocks[h, 4 + q] = self.raw["expand"][q, :, h * half : (h + 1) * half]
        self.split("gate", 8)
        self.split("shrink", 9)

    def split(self, name, block):
        raw, flat = self.raw[name], self.flat
        rows = self.blocks.shape[2]
        across = flat.shape[0] // rows
        for part in range(raw.shape[0] // flat.shape[0]):
            flat[...] = raw[part * flat.shape[0] : (part + 1) * flat.shape[0], :].astype(F32)
            strips = [flat[pl.ds(j, rows, stride=across), :] for j in range(across)]
            for h in range(2):
                own = strips[h * across // 2 : (h + 1) * across // 2]
                self.blocks[h, block + part] = jnp.concatenate(own, axis=1).astype(BF16)

    def do(self, number, step):
        if number < 4:
            name = "4kgv"[number]
            if step:
                self.merge(name)
            else:
                self.halves[name].start()
            return
        self.pieces[number - 4].step(step)
        if number == 4 and step == 4:
            join_vectors(self.tiles, self.vec, self.share)

    def merge(self, name):
        place, y = self.place, self.place.y
        self.halves[name].wait_recv()
        slab = self.weights[name].at[place.z, place.x, place.c]
        first, count = self.BLOCKS[name]
        mine = [self.blocks[y, first + q].astype(F32) for q in range(count)]
        theirs = [self.stages[first + q].astype(F32) for q in range(count)]
        for q in range(count):
            if name == "v":
                pair = (mine if q < 2 else theirs)[q % 2 * 2 : q % 2 * 2 + 2]
                slab[(2 * y + q) % 4, :, self.cols] = jnp.concatenate(pair, axis=0).astype(BF16)
            else:
                upper, lower = jnp.where(y == 0, mine[q], theirs[q]), jnp.where(y == 0, theirs[q], mine[q])
                slab[q, :, self.cols] = jnp.concatenate([upper, lower], axis=0).astype(BF16)

    def finish(self):
        for copy in self.halves.values():
            copy.wait_send()
        for piece in self.pieces:
            piece.finish()


class Scatter:
    def __init__(self, place, cols, grad, total, arrivals, order, send, recv):
        p, (mine, other), every = place, cols, slice(None)
        self.place, self.mine, self.grad, self.total = place, mine, grad, total
        self.order, self.arrivals = order, arrivals
        self.copies = [[remote(grad.at[:, :, 1 - p.c], total, send.at[0], recv.at[0], p.at(c=1 - p.c))]]
        held, number = {"z": every, "x": every, "y": every}, 1
        for axis, ref in zip(order, arrivals):
            ways = {
                "z": [(p.along_z(hop), ref.at[hop - 1], p.at(z=p.along_z(hop))) for hop in (1, 2, 3)],
                "x": [(1 - p.x, ref, p.at(x=1 - p.x))],
                "y": [(other, ref, p.at(y=1 - p.y))],
            }[axis]
            copies = []
            for place_of, target, device in ways:
                at = {**held, axis: place_of}
                copies.append(
                    remote(total.at[at["z"], at["x"], :, at["y"]], target, send.at[number], recv.at[number], device)
                )
                number += 1
            self.copies.append(copies)
            held[axis] = {"z": p.z, "x": p.x, "y": mine}[axis]

    def sent(self, *phases):
        for phase in phases:
            for copy in self.copies[phase]:
                copy.wait_send()

    def step(self, number):
        if number:
            for copy in self.copies[number - 1]:
                copy.wait_recv()
        if number == 1:

            @pl.loop(0, 4)
            def _(z):
                for x in range(2):
                    self.total[z, x] += self.grad[z, x, self.place.c]

        if number in (2, 3):
            self.add(number - 2)
        if number < 4:
            for copy in self.copies[number]:
                copy.start()

    def add(self, index):
        p, total, ref, past = self.place, self.total, self.arrivals[index], self.order[: index + 1]
        cols = self.mine if "y" in past else slice(None)

        def rows(z):
            for x in (p.x,) if "x" in past else (0, 1):
                lead = (() if "z" in past else (z,)) + (() if "x" in past else (x,))
                if past[-1] == "z":
                    value = total[z, x, :, cols].astype(F32)
                    for hop in range(3):
                        value += ref[(hop,) + lead].astype(F32)
                    total[z, x, :, cols] = value.astype(BF16)
                else:
                    total[z, x, :, cols] += ref[lead if lead else ...]

        if "z" in past:
            rows(p.z)
        else:
            pl.loop(0, 4)(rows)

    def result(self):
        p, ref = self.place, self.arrivals[2]
        value = self.total[p.z, p.x, :, self.mine].astype(F32)
        if self.order[2] == "z":
            for hop in range(3):
                value += ref[hop].astype(F32)
        else:
            value += ref[...].astype(F32)
        return value


def arrival_shapes(order, width):
    shape, out = {"z": 4, "x": 2, "y": width}, []
    for axis in order:
        shape[axis] = width // 2 if axis == "y" else 1
        lead = tuple(n for n in (shape["z"], shape["x"]) if n > 1)
        out.append(((3,) if axis == "z" else ()) + lead + (48, shape["y"]))
    return out


class Scatters:
    SLOTS = {"v": (0, 1, 2, 3), "4": (0, 1, 2, 3), "k": (4, 5, 6, 7), "g": (8,)}
    WAYS = ("yxz", "xzy", "yxz", "xzy", "yzx", "xyz", "xyz", "xyz", "yzx")

    def __init__(self, grad, grad_gate, outs, total, arrivals, finals, arrived, sums, send, recv, free):
        self.place = place = Place()
        self.outs, self.finals, self.arrived, self.sums, self.free = outs, finals, arrived, sums, free
        half = grad.shape[-1] // 2
        mine = pl.ds(pl.multiple_of(place.y * half, half), half)
        other = pl.ds(pl.multiple_of((1 - place.y) * half, half), half)
        self.mine, self.other = mine, other
        self.pieces, number, self.claimed, self.greeted = {}, 0, False, False
        for name, slots in self.SLOTS.items():
            source = grad_gate if name == "g" else grad
            for q, slot in enumerate(slots):
                self.pieces[name, q] = Scatter(
                    place, (mine, other), source.at[:, :, :, q], total.at[slot], arrivals[3 * slot : 3 * slot + 3],
                    self.WAYS[slot], send.at[number], recv.at[number],
                )
                number += 1
        self.last = {
            name: remote(finals[name], arrived[name], send.at[number, i], recv.at[number, i], place.at(y=1 - place.y))
            for i, name in enumerate("4kvg")
        }
        number += 1
        to = [place.at(c=1 - place.c), place.at(y=1 - place.y), place.at(x=1 - place.x)]
        self.hops = [
            [remote(sums.at[i], sums.at[4 + i], send.at[number, i], recv.at[number, i], device)]
            for i, device in enumerate(to)
        ]
        self.hops.append([
            remote(sums.at[3], sums.at[6 + hop], send.at[number, 2 + hop], recv.at[number, 2 + hop],
                   place.at(z=place.along_z(hop)))
            for hop in (1, 2, 3)
        ])

    def do(self, number, step):
        if not self.greeted:
            self.greeted = True
            greeted(self.place)
        names = list(self.pieces)
        if number >= len(names):
            number -= len(names)
            if number == 0:
                self.release()
            elif number == 1:
                self.hop(step)
            else:
                name = "4kvg"[number - 2]
                self.take_rows(name) if step else self.send_rows(name)
            return
        name, q = names[number]
        if name == "4" and not self.claimed:
            self.claimed = True
            pl.semaphore_wait(self.free, 6)
        self.pieces[name, q].step(step)
        if step == 4:
            self.close(name, q)

    def put(self, name, q, half, value):
        out = self.outs[name]
        if name == "k":
            half_cols = value.shape[1]
            out[q, :, pl.ds(pl.multiple_of(half * half_cols, half_cols), half_cols)] = value
            return
        if name == "v":
            flat, first = out, q * value.shape[0]
        else:
            flat, first = out[q], 0
        strips = value.shape[1] // LANES
        across = 2 * strips
        for j in range(strips):
            rows = pl.ds(first * across + half * strips + j, value.shape[0], stride=across)
            flat[rows, :] = value[:, j * LANES : (j + 1) * LANES]

    def close(self, name, q):
        y, total = self.place.y, self.pieces[name, q].result()
        if name == "v":

            @pl.when(y == q // 2)
            def _():
                self.put(name, q % 2, y, total)

            @pl.when(y != q // 2)
            def _():
                self.finals[name][q % 2] = total.astype(BF16)
        else:
            half = total.shape[0] // 2
            upper, lower = total[:half], total[half:]
            self.put(name, q, y, jnp.where(y == 0, upper, lower))
            self.finals[name][q] = jnp.where(y == 0, lower, upper).astype(BF16)

    def send_rows(self, name):
        self.last[name].start()

    def take_rows(self, name):
        self.last[name].wait_recv()
        for q in range(self.arrived[name].shape[0]):
            self.put(name, q, 1 - self.place.y, self.arrived[name][q].astype(F32))

    def release(self):
        for q in range(4):
            self.pieces["v", q].sent(1, 2, 3)
        for partner in self.place.partners():
            pl.semaphore_signal(self.free, inc=1, device_id=partner, device_id_type=pl.DeviceIdType.MESH)

    def hop(self, number):
        if number:
            for copy in self.hops[number - 1]:
                copy.wait_recv()
        if 1 <= number <= 3:
            self.sums[number] = self.sums[number - 1] + self.sums[3 + number]
        if number < 4:
            for copy in self.hops[number]:
                copy.start()

    def finish(self):
        for (name, _), piece in self.pieces.items():
            if name == "v":
                continue
            piece.sent(1, 2, 3)
            if name != "k":
                piece.sent(0)
        for copy in self.last.values():
            copy.wait_send()
        for copies in self.hops:
            for copy in copies:
                copy.wait_send()


def forward_kernel(share, *refs):
    lengths, tokens, cotangent = refs[:3]
    length, width = tokens.shape
    steps = length // SEG
    names = ("vectors", "recept", "key", "value", "output", "expand", "shrink", "gate")
    inputs = 11 if share else 8
    result, n1_out, n2_out, r_out, mix_out, state_out, key_out, att_out, cig_out, sq_out, gsg_out, up_out = refs[
        inputs : inputs + 12
    ]
    rest = refs[inputs + 12 :]
    gathers = None
    if share:
        w4_out, wk_out, wv_out, wg_out, vec_out = rest[:5]
        rest = rest[5:]
    w4, wk, wv, wg, nat, norm, mid, state, keys, half, sq, mask, rsd, sems = rest[:14]
    if share:
        gathers = Gathers(
            dict(zip(names, refs[3:11])), {"4": w4, "k": wk, "v": wv, "g": wg}, rest[14:19], share, *rest[19:]
        )
        vec = gathers.vec
    else:
        vec = refs[3]

    load_tok = local(tokens, half.at[0], sems.at[0])
    load_cot = local(cotangent, half.at[1], sems.at[1])
    load_tok.start()
    load_cot.start()
    save_n1 = local(norm, n1_out, sems.at[6])
    save_mix = local(half.at[2:5], mix_out, sems.at[7])
    save_state = local(state, state_out, sems.at[8])
    save_att = local(half.at[5], att_out, sems.at[9])
    save_n2 = local(norm, n2_out, sems.at[10])
    save_r = local(rsd, r_out, sems.at[11])
    save_cig = local(half.at[2:4], cig_out, sems.at[12])
    save_up = local(half.at[0], up_out, sems.at[13])
    save_sq = local(sq, sq_out, sems.at[14])
    save_gsg = local(half.at[4:6], gsg_out, sems.at[15])
    save_res = local(half.at[1], result, sems.at[16])
    save_key = local(keys, key_out, sems.at[18])
    late = [save_key, save_n2, save_r, save_cig, save_up, save_sq, save_gsg, save_res]
    if gathers:
        save_w4, save_wk = local(w4, w4_out, sems.at[2]), local(wk, wk_out, sems.at[3])
        save_wv, save_wg = local(wv, wv_out, sems.at[4]), local(wg, wg_out, sems.at[5])
        save_vec = local(vec, vec_out, sems.at[17])
        late += [save_w4, save_wk, save_wv, save_wg, save_vec]
    two = length // 2
    carried = {}

    def keep(*copies):
        if gathers:
            for copy in copies:
                copy.start()

    def start():
        if gathers:
            greet(gathers.place)
        fill_mask(lengths, mask, length)
        if gathers:
            gathers.begin()
        else:
            loads = [local(one, other, sems.at[2 + i]) for i, (one, other) in enumerate(zip(refs[4:8], (w4, wk, wv, wg)))]
            for copy in loads:
                copy.start()
            for copy in loads:
                copy.wait()

    def tok():
        load_tok.wait()
        widen(half.at[0], nat)

    def first_norm():
        @pl.loop(0, steps // TAKE)
        def _(block):
            values = jnp.concatenate([take_step(nat, block * TAKE + i, steps) for i in range(TAKE)], axis=0)
            rows = rows_at(block, TAKE * SEG)
            normed, scale = norm_rows(values)
            mid[rows, :] = values
            norm[rows_after(block, TAKE * SEG), :] = normed
            rsd[0, rows, :] = jnp.broadcast_to(scale, (TAKE * SEG, LANES))

        norm[0:SEG, :] = pltpu.roll(norm[length : length + SEG, :], 1, 0)
        save_n1.start()

    def mix(gain_row, mix_row, count):
        @pl.loop(0, steps // MIX)
        def _(block):
            gain, bias = vec[gain_row : gain_row + 1, :], vec[gain_row + 1 : gain_row + 2, :]
            rows = rows_at(block, MIX * SEG)
            now = norm[rows_after(block, MIX * SEG), :] * gain + bias
            before = (norm[rows, :] * gain + bias) * wide_of(mask[rows, :], width)
            change = now - before
            for q in range(count):
                half[2 + q, rows, :] = (before + vec[mix_row + q : mix_row + q + 1, :] * change).astype(BF16)

    def first_mix():
        mix(0, 2, 3)
        save_mix.start()

    def cot():
        load_cot.wait()
        widen(half.at[1], nat)

    def upstream():
        @pl.loop(0, steps // TAKE)
        def _(block):
            values = jnp.concatenate([take_step(nat, block * TAKE + i, steps) for i in range(TAKE)], axis=0)
            half[0, rows_at(block, TAKE * SEG), :] = values.astype(BF16)

        save_up.start()

    def product(q):
        @pl.loop(0, 2)
        def _(part):
            rows = rows_at(part, two)
            pre = dot_nn(half[2 + q, rows, :], w4[:, :, :, q].reshape(width, width))
            if q == 0:
                state[0, rows, :] = jax.nn.sigmoid(pre)
            if q == 1:
                put_rows(keys, rows, jnp.exp(pre))
            if q == 2:
                state[1, rows, :] = pre

    def first_scan():
        rate = -jnp.exp(vec[5:6, :])
        fade = jnp.exp(rate)

        def first(step, carry):
            top, bottom, through = carry
            rows = rows_at(step, SEG)
            keep = mask[rows, :]
            factor = fade * wide_of(keep, width)
            key = take_rows(keys, rows)
            return factor * top + key * state[1, rows, :], factor * bottom + key, through * keep

        zero = jnp.zeros((SEG, width), F32)
        ones = jnp.ones((SEG, LANES), F32)
        top, bottom, through = lax.fori_loop(0, steps, first, (zero, zero, ones), unroll=UNROLL)
        through = wide_of(through, width) * jnp.exp(rate * steps)
        carried["sums"] = join_runs((top, bottom), through, False)
        carried["fade"] = fade

    def second_scan():
        fade = carried["fade"]

        def second(step, carry):
            top, bottom = carry
            rows = rows_at(step, SEG)
            keep = wide_of(mask[rows, :], width)
            top, bottom = top * keep, bottom * keep
            key = take_rows(keys, rows)
            key_value = key * state[1, rows, :]
            bonus = jnp.exp(vec[6:7, :])
            blended = (top + bonus * key_value) / (bottom + bonus * key)
            half[5, rows, :] = (state[0, rows, :] * blended).astype(BF16)
            state[2, rows, :] = top
            state[3, rows, :] = bottom
            return fade * top + key_value, fade * bottom + key

        lax.fori_loop(0, steps, second, tuple(carried["sums"]), unroll=UNROLL)
        save_state.start()
        save_key.start()
        save_att.start()

    def middle():
        @pl.loop(0, 2)
        def _(part):
            rows = rows_at(part, two)
            mid[rows, :] += dot_nn(half[5, rows, :], w4[:, :, :, 3].reshape(width, width))

        keep(*([save_w4, save_vec] if gathers else []))

    def second_norm():
        save_n1.wait()

        @pl.loop(0, steps // TAKE)
        def _(block):
            rows = rows_at(block, TAKE * SEG)
            normed, scale = norm_rows(mid[rows, :])
            norm[rows_after(block, TAKE * SEG), :] = normed
            rsd[1, rows, :] = jnp.broadcast_to(scale, (TAKE * SEG, LANES))

        norm[0:SEG, :] = pltpu.roll(norm[length : length + SEG, :], 1, 0)
        save_n2.start()
        save_r.start()

    def second_mix():
        save_mix.wait()
        mix(7, 9, 2)
        save_cig.start()

    def expanded(q):
        @pl.loop(0, 2)
        def _(part):
            rows = rows_at(part, two)
            pre = jnp.maximum(dot_nn(half[2, rows, :], wk[:, :, :, q].reshape(width, width)), 0.0)
            sq[rows, q * width : (q + 1) * width] = (pre * pre).astype(BF16)

        carried["blocks"] = carried.get("blocks", 0) + 1
        if carried["blocks"] == 4:
            save_sq.start()
            keep(*([save_wk] if gathers else []))

    def gate():
        save_state.wait()

        @pl.loop(0, 2)
        def _(part):
            rows = rows_at(part, two)
            state[0, rows, :] = jax.nn.sigmoid(dot_nn(half[3, rows, :], wg[...].reshape(width, width)))

        keep(*([save_wg] if gathers else []))

    def shrunk(q):
        @pl.loop(0, 2)
        def _(part):
            rows = rows_at(part, two)
            out = dot_nn(sq[rows, q * width : (q + 1) * width], wv[:, :, :, q].reshape(width, width))
            state[1, rows, :] = state[1, rows, :] + out if q else out

    def final():
        keep(*([save_wv] if gathers else []))
        save_att.wait()

        @pl.loop(0, steps // TAKE)
        def _(block):
            rows = rows_at(block, TAKE * SEG)
            gate_value, shrunk_value = state[0, rows, :], state[1, rows, :]
            incoming = half[0, rows, :].astype(F32)
            gated = gate_value * shrunk_value
            out = mid[rows, :] + gated
            for i in range(TAKE):
                put_step(nat, block * TAKE + i, steps, out[i * SEG : (i + 1) * SEG])
            half[4, rows, :] = (incoming * gate_value).astype(BF16)
            half[5, rows, :] = (incoming * gated * (1.0 - gate_value)).astype(BF16)

        save_gsg.start()
        narrow(nat, half.at[1])
        save_res.start()

    work = [
        start, tok, first_norm, cot, upstream, first_mix, partial(product, 0), partial(product, 1), partial(product, 2),
        first_scan, second_scan, middle, second_norm, second_mix, gate, final,
    ]
    work += [partial(expanded, q) for q in range(4)] + [partial(shrunk, q) for q in range(4)]
    for item in FORWARD:
        if item < 100:
            work[item]()
        elif gathers:
            gathers.do(item // 100 - 1, item % 100)
    for copy in late:
        copy.wait()
    if gathers:
        gathers.finish()


def backward_kernel(direct, *refs):
    lengths, vec, w4_in, wk_in, wv_in, wg_in, n1_in, n2_in, r_in, mix_in, state_in, key_in = refs[:12]
    att_in, cig_in, sq_in, gsg_in, up_in, input_grad, vec_grad = refs[12:19]
    g4_out, gk_out, gv_out, gg_out = (refs[19:23], *refs[23:26]) if direct else refs[19:23]
    rest = refs[26:] if direct else refs[23:]
    weights, big, keys, sq, half, mask, rsd, grad, grad_gate, sums, sems = rest[:11]
    rest = rest[11:]
    length, width = input_grad.shape
    steps = length // SEG
    n_buf, gm_buf, nb_buf, s_buf = 0, 1, 2, 3
    gate_buf, value_buf, top_buf, bottom_buf = 3, 4, 5, 6
    scatters = None
    if direct:
        total, arrivals, rest = rest[0], rest[1:28], rest[28:]
        scatters = Scatters(
            grad, grad_gate, {"4": g4_out, "k": gk_out, "v": gv_out, "g": [gg_out]}, total, arrivals,
            dict(zip("4kvg", rest[:4])), dict(zip("4kvg", rest[4:8])), sums, *rest[8:],
        )

    def keep(source, target, *q):
        if not scatters:
            place = (slice(None),) * 3 + q
            copy = local(source.at[place], target.at[place], sems.at[8])
            copy.start()
            copy.wait()

    load_gsg = local(gsg_in, half.at[0:2], sems.at[0])
    load_sq = [
        local(sq_in.at[:, q * width : (q + 1) * width], sq.at[:, q * width : (q + 1) * width], sems.at[19 + q])
        for q in range(4)
    ]
    load_wv = local(wv_in, weights, sems.at[2])
    load_cig = local(cig_in, half.at[2:4], sems.at[3])
    load_wk = local(wk_in, weights, sems.at[4])
    load_wg = local(wg_in, grad_gate, sems.at[5])
    load_n2 = local(n2_in, big.at[n_buf], sems.at[6])
    load_r2 = local(r_in.at[1], rsd, sems.at[7])
    load_up = local(up_in, half.at[0], sems.at[9])
    load_w4 = local(w4_in, weights, sems.at[10])
    load_att = local(att_in, sq.at[:, 0:width], sems.at[11])
    load_n1 = local(n1_in, big.at[n_buf], sems.at[12])
    load_gate = local(state_in.at[0], big.at[gate_buf, 0:length], sems.at[13])
    load_state = local(state_in.at[1:4], big.at[value_buf : bottom_buf + 1, 0:length], sems.at[14])
    load_key = local(key_in, keys, sems.at[15])
    load_r1 = local(r_in.at[0], rsd, sems.at[16])
    load_mix = local(mix_in, half.at[1:4], sems.at[17])
    save_in = local(half.at[0], input_grad, sems.at[18])
    for copy in (load_gsg, *[load_sq[q] for q in (1, 0, 3, 2)], load_wv, load_cig, load_wg, load_n2, load_r2, load_state, load_key):
        copy.start()
    two = length
    zero8 = jnp.zeros((8, width), F32)
    zero = jnp.zeros((SEG, width), F32)
    carried = {}

    def put_sum(row, value):
        sums[0, row : row + 1, :] = jnp.sum(value, axis=0, keepdims=True)

    def columns(block):
        return slice(block * width, (block + 1) * width)

    def slabs(product):
        return product.astype(BF16).reshape(4, 2, 2, 48, width)

    def start():
        if scatters:
            greet(scatters.place)
        fill_mask(lengths, mask, length)
        load_gsg.wait()

    def value_grad(q):
        load_sq[q].wait()
        grad[:, :, :, q] = slabs(dot_tn(sq[:, columns(q)], half[0]))
        keep(grad, gv_out, q)

    def expand_back(q):
        if "wv" not in carried:
            carried["wv"] = 0
            load_wv.wait()
        carried["wv"] += 1

        @pl.loop(0, 1)
        def _(part):
            rows = rows_at(part, two)
            back = dot_nt(half[0, rows, :], weights[:, :, :, q].reshape(width, width))
            expanded = jnp.sqrt(sq[rows, columns(q)].astype(F32))
            sq[rows, columns(q)] = (2.0 * expanded * back).astype(BF16)

        if carried["wv"] == 4:
            load_wk.start()
            load_up.start()

    def wait_channel():
        if "cig" not in carried:
            carried["cig"] = True
            load_cig.wait()

    def key_grad(q):
        wait_channel()
        if scatters:
            scatters.pieces["v", q].sent(0)
        grad[:, :, :, q] = slabs(dot_tn(half[2], sq[:, columns(q)]))
        keep(grad, gk_out, q)

    def gate_in():
        load_wg.wait()

        @pl.loop(0, 1)
        def _(part):
            rows = rows_at(part, two)
            big[s_buf, rows, :] = dot_nt(half[1, rows, :], grad_gate[...].reshape(width, width))

    def gate_grad():
        wait_channel()
        grad_gate[...] = slabs(dot_tn(half[3], half[1])).reshape(grad_gate.shape)
        keep(grad_gate, gg_out)

    def channel_in(q):
        if q == 0:
            load_wk.wait()

        @pl.loop(0, 1)
        def _(part):
            rows = rows_at(part, two)
            out = dot_nt(sq[rows, columns(q)], weights[:, :, :, q].reshape(width, width))
            big[gm_buf, rows, :] = out if q == 0 else big[gm_buf, rows, :] + out

        if q == 3:
            load_w4.start()

    def second_mix():
        load_n2.wait()
        load_r2.wait()

        def mix_two(block, carry):
            sum_channel, sum_gate = carry
            rows, after = rows_at(block, MIX * SEG), rows_after(block, MIX * SEG)
            gain, bias = vec[7:8, :], vec[8:9, :]
            keep = wide_of(mask[rows, :], width)
            now = big[n_buf, after, :] * gain + bias
            before = (big[n_buf, rows, :] * gain + bias) * keep
            change = now - before
            in_channel, in_gate = big[gm_buf, rows, :], big[s_buf, rows, :]
            mix_channel, mix_gate = vec[9:10, :], vec[10:11, :]
            scaled = mix_channel * in_channel + mix_gate * in_gate
            big[gm_buf, rows, :] = scaled
            big[nb_buf, rows, :] = (in_channel + in_gate - scaled) * keep
            return sum_channel + fold(in_channel * change), sum_gate + fold(in_gate * change)

        sum_channel, sum_gate = lax.fori_loop(0, steps // MIX, mix_two, (zero8, zero8))
        load_gate.start()
        load_att.start()
        put_sum(9, sum_channel)
        put_sum(10, sum_gate)
        big[nb_buf, length : length + SEG, :] = pltpu.roll(big[nb_buf, 0:SEG, :], SEG - 1, 0)

    def second_norm():
        load_up.wait()

        def norm_two(block, carry):
            sum_gain, sum_bias = carry
            rows, after = rows_at(block, TAKE * SEG), rows_after(block, TAKE * SEG)
            normed = big[n_buf, after, :]
            incoming = big[gm_buf, rows, :] + big[nb_buf, after, :]
            scaled = incoming * vec[7:8, :]
            mean = jnp.mean(scaled, axis=-1, keepdims=True)
            along = jnp.mean(scaled * normed, axis=-1, keepdims=True)
            scale = wide_of(rsd[rows, :], width)
            out = half[0, rows, :].astype(F32) + scale * (scaled - mean - normed * along)
            big[gm_buf, rows, :] = out
            half[0, rows, :] = out.astype(BF16)
            return sum_gain + fold(incoming * normed), sum_bias + fold(incoming)

        sum_gain, sum_bias = lax.fori_loop(0, steps // TAKE, norm_two, (zero8, zero8))
        put_sum(7, sum_gain)
        put_sum(8, sum_bias)
        load_n1.start()
        load_r1.start()

    def output_grad():
        if scatters:
            scatters.pieces["k", 3].sent(0)
        load_att.wait()
        grad[:, :, :, 3] = slabs(dot_tn(sq[:, columns(0)], half[0]))
        keep(grad, g4_out, 3)

    def attended_back():
        load_w4.wait()

        @pl.loop(0, 1)
        def _(part):
            rows = rows_at(part, two)
            big[nb_buf, rows, :] = dot_nt(half[0, rows, :], weights[:, :, :, 3].reshape(width, width))

    def first_scan():
        load_mix.start()
        rate = -jnp.exp(vec[5:6, :])
        fade = jnp.exp(rate)
        load_gate.wait()
        load_state.wait()
        load_key.wait()

        def first(index, carry):
            right, below, through = carry
            step = steps - 1 - index
            rows = rows_at(step, SEG)
            keep_column = mask[rows, :]
            keep = wide_of(keep_column, width)
            bonus = jnp.exp(vec[6:7, :])
            gate, key, value = big[gate_buf, rows, :], take_rows(keys, rows), big[value_buf, rows, :]
            own = bonus * key
            inverse = 1.0 / (big[bottom_buf, rows, :] + own)
            blended = (big[top_buf, rows, :] + own * value) * inverse
            incoming = big[nb_buf, rows, :] * gate
            sq[rows, width : 2 * width] = (incoming * blended * (1.0 - gate)).astype(BF16)
            weight = incoming * inverse
            big[nb_buf, rows, :] = weight
            big[gate_buf, rows, :] = blended
            right = keep * (weight + fade * right)
            below = keep * (weight * blended + fade * below)
            return right, below, through * keep_column

        ones = jnp.ones((SEG, LANES), F32)
        right, below, through = lax.fori_loop(0, steps, first, (zero, zero, ones), unroll=UNROLL)
        through = wide_of(through, width) * jnp.exp(rate * steps)
        carried["sums"] = join_runs((right, below), through, True)
        carried["rate"], carried["fade"] = rate, fade

    def second_scan():
        rate, fade = carried["rate"], carried["fade"]

        def second(index, carry):
            right, below, sum_decay, sum_bonus = carry
            step = steps - 1 - index
            rows = rows_at(step, SEG)
            keep = wide_of(mask[rows, :], width)
            bonus = jnp.exp(vec[6:7, :])
            weight, blended = big[nb_buf, rows, :], big[gate_buf, rows, :]
            key, value = take_rows(keys, rows), big[value_buf, rows, :]
            own = bonus * key * weight
            own_key = own * (value - blended)
            sq[rows, 2 * width : 3 * width] = (own_key + key * (right * value - below)).astype(BF16)
            sq[rows, 3 * width : 4 * width] = (own + key * right).astype(BF16)
            sum_bonus = sum_bonus + fold(own_key)
            sum_decay = sum_decay + fold(right * big[top_buf, rows, :] - below * big[bottom_buf, rows, :])
            right = keep * (weight + fade * right)
            below = keep * (weight * blended + fade * below)
            return right, below, sum_decay, sum_bonus

        carry = (*carried["sums"], zero8, zero8)
        _, _, sum_decay, sum_bonus = lax.fori_loop(0, steps, second, carry, unroll=UNROLL)
        sums[0, 5:6, :] = jnp.sum(sum_decay, axis=0, keepdims=True) * (rate * fade)
        put_sum(6, sum_bonus)

    def time_grad(q):
        if "mix" not in carried:
            carried["mix"] = True
            load_mix.wait()
        if scatters:
            scatters.pieces["k", q].sent(0)
        grad[:, :, :, q] = slabs(dot_tn(half[1 + q], sq[:, columns(1 + q)]))
        keep(grad, g4_out, q)

    mixed_bufs = (gate_buf, top_buf, bottom_buf)

    def time_back(q):
        @pl.loop(0, 1)
        def _(part):
            rows = rows_at(part, two)
            big[mixed_bufs[q], rows, :] = dot_nt(sq[rows, columns(1 + q)], weights[:, :, :, q].reshape(width, width))

    def first_mix():
        load_n1.wait()
        load_r1.wait()

        def mix_one(block, carry):
            rows, after = rows_at(block, MIX * SEG), rows_after(block, MIX * SEG)
            gain, bias = vec[0:1, :], vec[1:2, :]
            keep = wide_of(mask[rows, :], width)
            now = big[n_buf, after, :] * gain + bias
            before = (big[n_buf, rows, :] * gain + bias) * keep
            change = now - before
            out = []
            scaled, total = None, None
            for q, place in enumerate(mixed_bufs):
                incoming = big[place, rows, :]
                part = vec[2 + q : 3 + q, :] * incoming
                scaled = part if scaled is None else scaled + part
                total = incoming if total is None else total + incoming
                out.append(carry[q] + fold(incoming * change))
            big[gate_buf, rows, :] = scaled
            big[nb_buf, rows, :] = (total - scaled) * keep
            return tuple(out)

        sum_mix = lax.fori_loop(0, steps // MIX, mix_one, (zero8, zero8, zero8))
        for q in range(3):
            put_sum(2 + q, sum_mix[q])
        big[nb_buf, length : length + SEG, :] = pltpu.roll(big[nb_buf, 0:SEG, :], SEG - 1, 0)

    def first_norm():
        def norm_one(block, carry):
            sum_gain, sum_bias = carry
            rows, after = rows_at(block, TAKE * SEG), rows_after(block, TAKE * SEG)
            normed = big[n_buf, after, :]
            incoming = big[gate_buf, rows, :] + big[nb_buf, after, :]
            scaled = incoming * vec[0:1, :]
            mean = jnp.mean(scaled, axis=-1, keepdims=True)
            along = jnp.mean(scaled * normed, axis=-1, keepdims=True)
            scale = wide_of(rsd[rows, :], width)
            out = big[gm_buf, rows, :] + scale * (scaled - mean - normed * along)
            for i in range(TAKE):
                put_step(keys, block * TAKE + i, steps, out[i * SEG : (i + 1) * SEG])
            return sum_gain + fold(incoming * normed), sum_bias + fold(incoming)

        sum_gain, sum_bias = lax.fori_loop(0, steps // TAKE, norm_one, (zero8, zero8))
        put_sum(0, sum_gain)
        put_sum(1, sum_bias)
        sums[0, 11:16, :] = jnp.zeros((5, width), F32)

    def final():
        narrow(keys, half.at[0])
        save_in.start()

    work = [
        start, gate_in, gate_grad, second_mix, second_norm, output_grad, attended_back, first_scan, second_scan, first_mix,
        first_norm, final,
    ]
    for function, count in (
        (value_grad, 4), (expand_back, 4), (key_grad, 4), (channel_in, 4), (time_grad, 3), (time_back, 3)
    ):
        work += [partial(function, q) for q in range(count)]
    for item in BACKWARD:
        if item < 100:
            work[item]()
        elif scatters:
            scatters.do(item // 100 - 1, item % 100)
    if scatters:
        vec_grad[...] = sums[3] + sums[7] + sums[8] + sums[9]
        scatters.finish()
    else:
        vec_grad[...] = sums[0]
    save_in.wait()


ANY = pl.BlockSpec(memory_space=pl.ANY)
SMEM = pl.BlockSpec(memory_space=pltpu.SMEM)
VMEM = pl.BlockSpec(memory_space=pltpu.VMEM)


def run_forward(lengths, tokens, cotangent, parameters, share=None):
    length, width = tokens.shape
    shape = jax.ShapeDtypeStruct
    outs = (
        shape((length, width), BF16),
        shape((length + SEG, width), F32),
        shape((length + SEG, width), F32),
        shape((2, length, LANES), F32),
        shape((3, length, width), BF16),
        shape((4, length, width), F32),
        shape((width // LANES, length, LANES), F32),
        shape((length, width), BF16),
        shape((2, length, width), BF16),
        shape((length, 4 * width), BF16),
        shape((2, length, width), BF16),
        shape((length, width), BF16),
    )
    slabs, gate = (4, 2, 2, 4, 48, width), (4, 2, 2, 1, 48, width)
    scratch = [
        pltpu.VMEM(slabs, BF16),
        pltpu.VMEM(slabs, BF16),
        pltpu.VMEM(slabs, BF16),
        pltpu.VMEM(gate, BF16),
        pltpu.VMEM((width // LANES, length, LANES), F32),
        pltpu.VMEM((length + SEG, width), F32),
        pltpu.VMEM((length, width), F32),
        pltpu.VMEM((4, length, width), F32),
        pltpu.VMEM((width // LANES, length, LANES), F32),
        pltpu.VMEM((6, length, width), BF16),
        pltpu.VMEM((length, 4 * width), BF16),
        pltpu.VMEM((length, LANES), F32),
        pltpu.VMEM((2, length, LANES), F32),
        pltpu.SemaphoreType.DMA((19,)),
    ]
    in_specs = [SMEM, ANY, ANY, VMEM, ANY, ANY, ANY, ANY]
    params = {}
    if share:
        outs += (shape(slabs, BF16),) * 3 + (shape(gate, BF16), shape((16, width), F32))
        scratch += [
            pltpu.VMEM((24 * width // LANES, LANES), F32),
            pltpu.VMEM((2, 13, 24, width // 2), BF16),
            pltpu.VMEM((13, 24, width // 2), BF16),
            pltpu.VMEM((4, 2, 2, 2, 16, LANES), F32),
            pltpu.VMEM((16, width), F32),
            pltpu.SemaphoreType.DMA((15, 6)),
            pltpu.SemaphoreType.DMA((15, 6)),
        ]
        in_specs = [SMEM, ANY, ANY] + [VMEM] * 8
        params = dict(collective_id=0, has_side_effects=True)
    return pl.pallas_call(
        partial(forward_kernel, share),
        out_shape=outs,
        in_specs=in_specs,
        out_specs=[ANY] * len(outs),
        scratch_shapes=scratch,
        compiler_params=pltpu.CompilerParams(vmem_limit_bytes=VMEM_LIMIT, **params),
        name="forward",
    )(lengths, tokens, cotangent, *parameters)


def run_backward(lengths, vec, w4, wk, wv, wg, saved, direct):
    n1, n2, r, mix, state, keys, att, cig, sq, gsg, up = saved
    length, width = up.shape
    half = width // 2
    shape = jax.ShapeDtypeStruct
    slabs, gate = (4, 2, 2, 4, 48, width), (4, 2, 2, 1, 48, width)
    outs = (shape((length, width), BF16), shape((16, width), F32))
    out_specs = [ANY, VMEM]
    scratch = [
        pltpu.VMEM(slabs, BF16),
        pltpu.VMEM((7, length + SEG, width), F32),
        pltpu.VMEM((width // LANES, length, LANES), F32),
        pltpu.VMEM((length, 4 * width), BF16),
        pltpu.VMEM((4, length, width), BF16),
        pltpu.VMEM((length, LANES), F32),
        pltpu.VMEM((length, LANES), F32),
        pltpu.VMEM(slabs, BF16),
        pltpu.VMEM(gate, BF16),
        pltpu.VMEM((10, 16, width), F32),
        pltpu.SemaphoreType.DMA((23,)),
    ]
    params = {}
    if direct:
        rows = ((4, 24), (4, 24), (2, 48), (1, 24))
        lines = 24 * width // LANES
        outs += (shape((lines, LANES), F32),) * 4 + (
            shape((4, 24, width), F32), shape((4 * lines, LANES), F32), shape((lines, LANES), F32)
        )
        out_specs += [VMEM] * 7
        scratch += [pltpu.VMEM((9, 4, 2, 48, width), BF16)]
        scratch += [pltpu.VMEM(part, BF16) for way in Scatters.WAYS for part in arrival_shapes(way, width)]
        scratch += [pltpu.VMEM(part + (half,), BF16) for part in rows] * 2
        scratch += [
            pltpu.SemaphoreType.DMA((15, 6)), pltpu.SemaphoreType.DMA((15, 6)), pltpu.SemaphoreType.REGULAR
        ]
        params = dict(collective_id=1, has_side_effects=True)
    else:
        outs += (shape(slabs, BF16),) * 3 + (shape(gate, BF16),)
        out_specs += [ANY] * 4
    return pl.pallas_call(
        partial(backward_kernel, direct),
        out_shape=outs,
        in_specs=[SMEM, VMEM] + [ANY] * 15,
        out_specs=out_specs,
        scratch_shapes=scratch,
        compiler_params=pltpu.CompilerParams(vmem_limit_bytes=VMEM_LIMIT, **params),
        name="backward",
    )(lengths, vec, w4, wk, wv, wg, n1, n2, r, mix, state, keys, att, cig, sq, gsg, up)


AXES = ("wide", "narrow")


def per_device(
    direct, tokens, lengths, cotangent, vectors,
    time_recept, time_key, time_value, time_output, channel_key, channel_value, channel_recept,
):
    _, length, width = tokens.shape
    slabs, gate = (4, 2, 2, 4, 48, width), (4, 2, 2, 1, 48, width)

    if direct:
        share = vectors.shape[1]
        key = channel_key.reshape(24, 16, 4, 48).transpose(2, 0, 1, 3).reshape(4, 24, width)
        flat = [m.reshape(-1, LANES) for m in (time_recept, time_key, time_value, time_output, channel_value, channel_recept)]
        out = run_forward(
            lengths, tokens[0], cotangent[0], (vectors, *flat[:4], key, flat[4], flat[5]), share=share
        )
        w4, wk, wv, wg, vec = out[12:]
    else:

        def whole(part, axis=0):
            return lax.all_gather(part, AXES, axis=axis, tiled=True)

        vec = jnp.pad(whole(vectors, 1).astype(F32), ((0, 5), (0, 0)))
        square = [whole(m).reshape(16, 48, width) for m in (time_recept, time_key, time_value, time_output)]
        w4 = jnp.stack(square, axis=1).reshape(slabs)
        wk = whole(channel_key).reshape(16, 48, 16, 4, 48).transpose(0, 3, 1, 2, 4).reshape(slabs)
        wv = whole(channel_value).reshape(slabs)
        wg = whole(channel_recept).reshape(gate)
        out = run_forward(lengths, tokens[0], cotangent[0], (vec, w4, wk, wv, wg))
    input_grad, vec_grad, *grads = run_backward(lengths, vec, w4, wk, wv, wg, out[1:12], direct)
    if direct:
        place = lax.axis_index("wide") * 2 + lax.axis_index("narrow")
        gk, gv, gg = grads[4:]
        return (
            out[0][None],
            input_grad[None],
            lax.dynamic_slice(vec_grad, (0, place * share), (vectors.shape[0], share)),
            *[g.reshape(-1) for g in grads[:4]],
            gk.reshape(4, 24, 16, 48).transpose(1, 2, 0, 3).reshape(-1),
            gv.reshape(-1),
            gg.reshape(-1),
        )
    g4, gk, gv, gg = grads

    def owned(full, axis=0):
        return lax.psum_scatter(full.astype(F32), AXES, scatter_dimension=axis, tiled=True)

    return (
        out[0][None],
        input_grad[None],
        owned(vec_grad[:11], 1),
        *[owned(g4[:, :, :, q].reshape(-1)) for q in range(4)],
        owned(gk.reshape(16, 4, 48, 16, 48).transpose(0, 2, 3, 1, 4).reshape(-1)),
        owned(gv.reshape(-1)),
        owned(gg.reshape(-1)),
    )


def solution(mesh):
    both = P(AXES)
    rows = P(AXES, None, None)
    direct = dict(mesh.shape) == {"wide": 16, "narrow": 2}
    return jax.shard_map(
        partial(per_device, direct),
        mesh=mesh,
        in_specs=(rows, P(AXES, None), rows, P(None, AXES)) + (both,) * 7,
        out_specs=(rows, rows, P(None, AXES)) + (both,) * 7,
        check_vma=False,
    )
```
